32 devices in a mesh: pos: 8 (over y, x, core), grp: 4 (over z).
Axes of the slice: x: 2, y: 2, z: 4, core: 2. Of those that a mesh axis runs over, the one named last changes fastest.
Arguments:
- inputs: bfloat16 [12544, 1024], P(('pos', 'grp')), may hold values from -9 to 9
- segment_ids: int32 [64], replicated, may hold values from 0 to 15, as said below
- pad_mask: int32 [12544], replicated, may hold values 0 or 1
- time_weight: bfloat16 [3, 1024, 256], replicated, may hold values from -0.109375 to 0.109375
- gain_first: float32 [256], replicated, may hold values from 0.5 to 1.5
- shift_first: float32 [256], replicated, may hold values from -4 to 4
- space_weight: bfloat16 [9, 256, 256], replicated, may hold values from -0.125 to 0.125
- gain_second: float32 [256], replicated, may hold values from 0.5 to 1.5
- shift_second: float32 [256], replicated, may hold values from -4 to 4
- expand_weight: bfloat16 [256, 1024], replicated, may hold values from -0.375 to 0.375
- gain_third: float32 [1024], replicated, may hold values from 0.5 to 1.5
- shift_third: float32 [1024], replicated, may hold values from -4 to 4
- query_weight: bfloat16 [1024, 512], replicated, may hold values from -0.1875 to 0.1875
- key_weight: bfloat16 [1024, 512], replicated, may hold values from -0.1875 to 0.1875
- value_weight: bfloat16 [1024, 512], replicated, may hold values from -0.1875 to 0.1875
- out_weight: bfloat16 [512, 1024], replicated, may hold values from -0.25 to 0.25
- gain_final: float32 [1024], replicated, may hold values from 0.5 to 1.5
- shift_final: float32 [1024], replicated, may hold values from -4 to 4
- cotangent: bfloat16 [12544, 1024], P(('pos', 'grp')), may hold values from -6 to 6
Outputs:
- output: bfloat16 [12544, 1024], P(('pos', 'grp'))
- input_grad: float32 [12544, 1024], P(('pos', 'grp'))
- time_grad: float32 [3, 1024, 256], P(None, 'pos')
- gain_first_grad: float32 [256], replicated
- shift_first_grad: float32 [256], replicated
- space_grad: float32 [9, 256, 256], P(None, 'pos')
- gain_second_grad: float32 [256], replicated
- shift_second_grad: float32 [256], replicated
- expand_grad: float32 [256, 1024], P(None, 'pos')
- gain_third_grad: float32 [1024], replicated
- shift_third_grad: float32 [1024], replicated
- query_grad: float32 [1024, 512], P('pos')
- key_grad: float32 [1024, 512], P('pos')
- value_grad: float32 [1024, 512], P('pos')
- out_weight_grad: float32 [512, 1024], P(None, 'pos')
- gain_final_grad: float32 [1024], replicated
- shift_final_grad: float32 [1024], replicated
The draws below stay inside these ranges and needn't reach their ends.
Inputs may be any that keep to these rules, and one draw needn't show every extreme that they name: `segment_ids`: ids never fall; the aligned block k of 8 frames holds the id 2k, then possibly 2k + 1, with 2k on half of the block or more.
All inputs are finite; a program needn't handle non-finite values.
Results may differ from the reference program's by a relative error of at most 0.035.
The reference program's roundings to bfloat16 on the way count: a program that leaves them out, or rounds other values in their place, can miss the bound.
Values may be sent and summed in bfloat16 or wider, within the bound.
No kernel may reach another device: no remote copies, remote signals or barrier semaphores. Data moves between devices by JAX's collectives and lax.ppermute only.
A program may use at most 128 MiB of HBM per device.

```python
import functools
import math
import jax
import jax.numpy as jnp
from jax import lax

C = 1024
CB = 256
INNER = 512
SIDE = 14
GROUP_FRAMES = 8
FRAMES = 64
POSITIONS = 12544
N_POS = 8


def draw_inputs(key, part):
    key = jax.random.fold_in(key, 11)
    ramp = jnp.arange(POSITIONS, dtype=jnp.float32) / max(POSITIONS - 1, 1)
    scales = 0.5 * jnp.exp(ramp * math.log(3.0))
    base = jnp.clip(jax.random.normal(key, (POSITIONS, C), jnp.float32), -6.0, 6.0)
    return (base * scales[:, None]).astype(jnp.bfloat16)


def draw_segment_ids(key, part):
    key = jax.random.fold_in(key, 23)
    group_count = FRAMES // GROUP_FRAMES
    cuts = jax.random.randint(key, (group_count, 1), (GROUP_FRAMES + 1) // 2, GROUP_FRAMES + 1)
    local = jnp.arange(GROUP_FRAMES, dtype=jnp.int32)[None, :]
    numbers = 2 * jnp.arange(group_count, dtype=jnp.int32)[:, None] + (local >= cuts).astype(jnp.int32)
    return numbers.reshape(FRAMES).astype(jnp.int32)


def with_ends(values, key, least, largest):
    dims = values.shape
    index_at = [jax.random.randint(jax.random.fold_in(key, axis), (), 0, dims[axis]) for axis in range(len(dims))]
    values = values.at[tuple(index_at)].set(least)
    longest = dims.index(max(dims))
    index_at[longest] = (index_at[longest] + 1) % dims[longest]
    return values.at[tuple(index_at)].set(largest)


def levels(stream_key, dims, cuts, smallest, top_value):
    gain = 1.0
    for axis_at, parts in cuts:
        steps = jax.random.uniform(jax.random.fold_in(jax.random.fold_in(stream_key, 6), axis_at), (parts,), jnp.float32, smallest / len(cuts), top_value / len(cuts))
        gain = gain * jnp.repeat(jnp.exp(steps), dims[axis_at] // parts).reshape((-1,) + (1,) * (len(dims) - 1 - axis_at))
    return gain


def centred(rng, extent, width, most, cuts=(), kind=jnp.bfloat16):
    array = width * jax.random.normal(rng, extent, jnp.float32)
    if cuts:
        array = array * levels(rng, extent, cuts, -0.22, 0.18)
    return jnp.clip(array, -most, most).astype(kind)


def setup_inputs(seed: int = 0) -> dict:
    key_list = jax.random.split(jax.random.key(seed), 20)
    return {
        "inputs": draw_inputs(jax.random.fold_in(key_list[19], 71), 0),
        "segment_ids": draw_segment_ids(jax.random.fold_in(key_list[19], 71), 0),
        "pad_mask": with_ends((jax.random.randint(key_list[2], (POSITIONS,), 0, 8) < 7).astype(jnp.int32), jax.random.fold_in(key_list[2], 1), 0, 1),
        "time_weight": centred(key_list[3], (3, C, CB), (3 * C) ** -0.5, 0.109375),
        "gain_first": jnp.clip(1.0 + 0.1 * jax.random.normal(key_list[4], (CB,), jnp.float32), 0.5, 1.5),
        "shift_first": centred(key_list[5], (CB,), 0.3, 4.0, (), jnp.float32),
        "space_weight": centred(key_list[6], (9, CB, CB), (9 * CB) ** -0.5, 0.125),
        "gain_second": jnp.clip(1.0 + 0.1 * jax.random.normal(key_list[7], (CB,), jnp.float32), 0.5, 1.5),
        "shift_second": centred(key_list[8], (CB,), 0.3, 4.0, (), jnp.float32),
        "expand_weight": centred(key_list[9], (CB, C), CB ** -0.5, 0.375),
        "gain_third": jnp.clip(1.0 + 0.1 * jax.random.normal(key_list[10], (C,), jnp.float32), 0.5, 1.5),
        "shift_third": centred(key_list[11], (C,), 0.3, 4.0, (), jnp.float32),
        "query_weight": centred(key_list[12], (C, INNER), C ** -0.5, 0.1875),
        "key_weight": centred(key_list[13], (C, INNER), C ** -0.5, 0.1875),
        "value_weight": centred(key_list[14], (C, INNER), C ** -0.5, 0.1875),
        "out_weight": centred(key_list[15], (INNER, C), INNER ** -0.5, 0.25),
        "gain_final": jnp.clip(1.0 + 0.1 * jax.random.normal(key_list[16], (C,), jnp.float32), 0.5, 1.5),
        "shift_final": centred(key_list[17], (C,), 0.3, 4.0, (), jnp.float32),
        "cotangent": centred(key_list[18], (POSITIONS, C), 1.0, 6.0, ((0, 32),)),
    }


EPSILON = 1e-05
TEMPER = 0.2
MASKED_SCORE = -1000000000.0
HIGHEST = lax.Precision.HIGHEST

@jax.custom_vjp
def low(v):
    return lax.optimization_barrier(v.astype(jnp.bfloat16)).astype(jnp.float32)

@jax.custom_vjp
def low_back(v):
    return v

def low_keep(v):
    return (low(v), None)

def low_pass(kept, grad):
    return (grad,)

def back_keep(v):
    return (v, None)

def back_low(kept, grad):
    return (low(grad),)
low.defvjp(low_keep, low_pass)
low_back.defvjp(back_keep, back_low)

def silu(value):
    return value * jax.nn.sigmoid(value)

def batch_norm(hidden, valid_rows, valid_total, gain_vec, shift_vec):
    average = lax.optimization_barrier(jnp.sum(hidden * valid_rows, axis=0)) / valid_total
    spread = lax.optimization_barrier(jnp.sum(hidden * hidden * valid_rows, axis=0)) / valid_total - average * average
    return (hidden - average) * lax.rsqrt(spread + EPSILON) * gain_vec + shift_vec

def time_conv(stacked, weight, prev_ok, next_ok):
    zeros_frame = jnp.zeros_like(stacked[:1])
    previous = jnp.concatenate([zeros_frame, stacked[:-1]], axis=0) * prev_ok[:, None, None]
    following = jnp.concatenate([stacked[1:], zeros_frame], axis=0) * next_ok[:, None, None]
    result = jnp.dot(previous, weight[0], precision=HIGHEST)
    result = result + jnp.dot(stacked, weight[1], precision=HIGHEST)
    return result + jnp.dot(following, weight[2], precision=HIGHEST)

def space_conv(frames_grid, weight):
    padded = jnp.pad(frames_grid, ((0, 0), (1, 1), (1, 1), (0, 0)))
    result = jnp.zeros(frames_grid.shape[:3] + (weight.shape[2],), jnp.float32)
    for tap_index in range(9):
        row_off = tap_index // 3
        col_off = tap_index % 3
        window = padded[:, row_off:row_off + SIDE, col_off:col_off + SIDE, :]
        result = result + jnp.dot(window, weight[tap_index], precision=HIGHEST)
    return result

def pool_blocks(values, valid_grid):
    half_side = SIDE // 2
    frame_count = values.shape[0]
    blocks = values.reshape(frame_count, half_side, 2, half_side, 2, values.shape[-1])
    weights = valid_grid.reshape(frame_count, half_side, 2, half_side, 2, 1)
    block_sums = lax.optimization_barrier(jnp.sum(blocks * weights, axis=(2, 4)))
    counts = lax.optimization_barrier(jnp.sum(weights, axis=(2, 4)))
    return (block_sums / jnp.maximum(counts, 1.0)).reshape(frame_count * half_side * half_side, values.shape[-1])

def attend(pieces):
    queries, keys, values, query_seg, key_seg, key_ok = pieces
    allowed = (query_seg[:, None] == key_seg[None, :]) & key_ok[None, :]
    logits = low_back(jnp.dot(queries, keys.T, precision=HIGHEST))
    scores = jnp.where(allowed, logits * TEMPER, MASKED_SCORE)
    row_max = lax.optimization_barrier(jnp.max(scores, axis=1, keepdims=True))
    exponent = jnp.exp(scores - row_max)
    probs = exponent / lax.optimization_barrier(jnp.sum(exponent, axis=1, keepdims=True))
    return low(low_back(jnp.dot(low(probs), values, precision=HIGHEST)))

def bottleneck_part(segment_ids, valid_rows, valid_total, inputs, time_weight, gain_first, shift_first, space_weight, gain_second, shift_second, expand_weight, gain_third, shift_third):
    area = SIDE * SIDE
    same_next = (segment_ids[1:] == segment_ids[:-1]).astype(jnp.float32)
    prev_ok = jnp.concatenate([jnp.zeros((1,), jnp.float32), same_next])
    next_ok = jnp.concatenate([same_next, jnp.zeros((1,), jnp.float32)])
    stacked = inputs.reshape(FRAMES, area, C)
    pre_first = low_back(time_conv(stacked, time_weight, prev_ok, next_ok).reshape(POSITIONS, CB))
    z_first = low(silu(batch_norm(pre_first, valid_rows, valid_total, gain_first, shift_first)))
    pre_second = low_back(space_conv(z_first.reshape(FRAMES, SIDE, SIDE, CB), space_weight).reshape(POSITIONS, CB))
    z_second = low(silu(batch_norm(pre_second, valid_rows, valid_total, gain_second, shift_second)))
    pre_third = low_back(jnp.dot(z_second, expand_weight, precision=HIGHEST))
    return inputs + batch_norm(pre_third, valid_rows, valid_total, gain_third, shift_third)

def nonlocal_part(segment_ids, valid_rows, valid_total, summed, query_weight, key_weight, value_weight, out_weight, gain_final, shift_final):
    area = SIDE * SIDE
    half_area = SIDE // 2 * (SIDE // 2)
    unit = low(silu(summed))
    theta = low(low_back(jnp.dot(unit, query_weight, precision=HIGHEST)))
    key_full = low_back(jnp.dot(unit, key_weight, precision=HIGHEST))
    value_full = low_back(jnp.dot(unit, value_weight, precision=HIGHEST))
    valid_grid = valid_rows.reshape(FRAMES, SIDE, SIDE)
    keys = low(pool_blocks(key_full.reshape(FRAMES, SIDE, SIDE, INNER), valid_grid))
    values = low(pool_blocks(value_full.reshape(FRAMES, SIDE, SIDE, INNER), valid_grid))
    half_side = SIDE // 2
    key_counts = lax.optimization_barrier(jnp.sum(valid_grid.reshape(FRAMES, half_side, 2, half_side, 2), axis=(2, 4)))
    key_ok = (key_counts > 0.5).reshape(N_POS, GROUP_FRAMES * half_area)
    query_seg = jnp.repeat(segment_ids, area).reshape(N_POS, GROUP_FRAMES * area)
    key_seg = jnp.repeat(segment_ids, half_area).reshape(N_POS, GROUP_FRAMES * half_area)
    attended = lax.map(jax.checkpoint(attend), (theta.reshape(N_POS, GROUP_FRAMES * area, INNER), keys.reshape(N_POS, GROUP_FRAMES * half_area, INNER), values.reshape(N_POS, GROUP_FRAMES * half_area, INNER), query_seg, key_seg, key_ok)).reshape(POSITIONS, INNER)
    pre_final = low_back(jnp.dot(attended, out_weight, precision=HIGHEST))
    return unit + batch_norm(pre_final, valid_rows, valid_total, gain_final, shift_final)

def forward(segment_ids, valid_rows, valid_total, inputs, time_weight, gain_first, shift_first, space_weight, gain_second, shift_second, expand_weight, gain_third, shift_third, query_weight, key_weight, value_weight, out_weight, gain_final, shift_final):
    first_section = jax.checkpoint(functools.partial(bottleneck_part, segment_ids, valid_rows, valid_total))
    second_section = jax.checkpoint(functools.partial(nonlocal_part, segment_ids, valid_rows, valid_total))
    summed = first_section(inputs, time_weight, gain_first, shift_first, space_weight, gain_second, shift_second, expand_weight, gain_third, shift_third)
    return second_section(summed, query_weight, key_weight, value_weight, out_weight, gain_final, shift_final)

def reference(inputs, segment_ids, pad_mask, time_weight, gain_first, shift_first, space_weight, gain_second, shift_second, expand_weight, gain_third, shift_third, query_weight, key_weight, value_weight, out_weight, gain_final, shift_final, cotangent):
    valid_rows = pad_mask.astype(jnp.float32)[:, None]
    valid_total = jnp.sum(valid_rows)
    params = (inputs, time_weight, gain_first, shift_first, space_weight, gain_second, shift_second, expand_weight, gain_third, shift_third, query_weight, key_weight, value_weight, out_weight, gain_final, shift_final)
    params = tuple((p.astype(jnp.float32) for p in params))
    bound = functools.partial(forward, segment_ids, valid_rows, valid_total)
    result, pullback = jax.vjp(bound, *params)
    grads = pullback(cotangent.astype(jnp.float32))
    return (result.astype(jnp.bfloat16), grads[0], grads[1], grads[2], grads[3], grads[4], grads[5], grads[6], grads[7], grads[8], grads[9], grads[10], grads[11], grads[12], grads[13], grads[14], grads[15])
```

```python
import functools

import jax
import jax.numpy as jnp
import numpy as np
from jax import lax
from jax.experimental import pallas as pl
from jax.experimental.pallas import tpu as pltpu
from jax.sharding import PartitionSpec as P

SIDE = 14
HALF = SIDE // 2
AREA = SIDE * SIDE
LANE = 128
EDGE = 16
EPSILON = 1e-05
TEMPER = 0.2
MASKED_SCORE = -1000000000.0
PAD_SCORE = -2000000000.0
F32 = jnp.float32
BF16 = jnp.bfloat16
VMEM_BYTES = 24 * 1024 * 1024


def flip(count, bit):
    return [(i, i ^ bit) for i in range(count)]


def dot(left, right):
    return jnp.dot(left, right, preferred_element_type=F32)


def dot_rows(left, right):
    return lax.dot_general(left, right, (((0,), (0,)), ((), ())), preferred_element_type=F32)


def dot_cols(left, right):
    return lax.dot_general(left, right, (((1,), (1,)), ((), ())), preferred_element_type=F32)


def first_count():
    pos_count, grp_count = lax.axis_size("pos"), lax.axis_size("grp")
    return pos_count * grp_count if pos_count * grp_count <= 64 else pos_count


def trade(copies):
    pos_count, grp_count = lax.axis_size("pos"), lax.axis_size("grp")
    if pos_count * grp_count <= 64:
        return lax.all_to_all(copies, ("pos", "grp"), 0, 0, tiled=True)
    part = lax.all_to_all(copies, "pos", 0, 0, tiled=True).sum(0)
    copies = jnp.broadcast_to(part[None], (grp_count,) + part.shape)
    return lax.all_to_all(copies, "grp", 0, 0, tiled=True)


def shrink(part):
    pos_count, grp_count = lax.axis_size("pos"), lax.axis_size("grp")
    place, layer = lax.axis_index("pos"), lax.axis_index("grp")
    bits = pos_count.bit_length() - 1
    held = part.reshape((2,) * bits + part.shape[1:])
    for bit in range(bits):
        axis = bits - 1 - bit
        mine = (place >> bit) & 1
        sent = lax.dynamic_index_in_dim(held, 1 - mine, axis, False).astype(BF16)
        kept = lax.dynamic_index_in_dim(held, mine, axis, False)
        held = kept + lax.ppermute(sent, "pos", flip(pos_count, 1 << bit)).astype(F32)
    levels = grp_count.bit_length() - 1
    for bit in range(levels - 1):
        mine = (layer >> bit) & 1
        pair = held.reshape((2, held.shape[0] // 2) + held.shape[1:])
        sent = lax.dynamic_index_in_dim(pair, 1 - mine, 0, False).astype(BF16)
        kept = lax.dynamic_index_in_dim(pair, mine, 0, False)
        held = kept + lax.ppermute(sent, "grp", flip(grp_count, 1 << bit)).astype(F32)
    low = held.astype(BF16)
    other = lax.ppermute(low, "grp", flip(grp_count, 1 << (levels - 1)))
    held = (low.astype(F32) + other.astype(F32)).astype(BF16)
    for bit in reversed(range(levels - 1)):
        mine = (layer >> bit) & 1
        other = lax.ppermute(held, "grp", flip(grp_count, 1 << bit))
        first = jnp.where(mine == 0, held, other)
        second = jnp.where(mine == 0, other, held)
        held = jnp.concatenate([first, second], axis=0)
    return held.astype(F32)


def call(kernel, outs, scalars, *arrays, scratch=(), flops=0):
    shapes = [jax.ShapeDtypeStruct(shape, kind) for shape, kind in outs]
    moved = sum(int(np.prod(s.shape)) * s.dtype.itemsize for s in shapes)
    moved += sum(a.size * a.dtype.itemsize for a in arrays)
    return pl.pallas_call(
        kernel,
        out_shape=shapes,
        in_specs=[pl.BlockSpec(memory_space=pltpu.SMEM)]
        + [pl.BlockSpec(memory_space=pltpu.VMEM)] * len(arrays),
        out_specs=[pl.BlockSpec(memory_space=pltpu.VMEM)] * len(shapes),
        scratch_shapes=list(scratch),
        compiler_params=pltpu.CompilerParams(vmem_limit_bytes=VMEM_BYTES),
        cost_estimate=pl.CostEstimate(flops=flops, bytes_accessed=moved, transcendentals=0),
    )(scalars, *arrays)


def chunks(width, step=LANE):
    return [slice(start, start + step) for start in range(0, width, step)]


def emit(copies_ref, row, where, value):
    count = copies_ref.shape[0]
    copies_ref[:, row : row + 1, where] = jnp.broadcast_to(
        value[None], (count,) + value.shape
    )


def column_sum(value):
    return jnp.sum(value, axis=0, keepdims=True)


def moments_of(sums, total):
    mean = sums[0:1] / total
    return mean, lax.rsqrt(sums[1:2] / total - mean * mean + EPSILON)


def silu_grad(pre_act, gradient):
    sig = jax.nn.sigmoid(pre_act)
    return gradient * sig * (1.0 + pre_act * (1.0 - sig))


def back_terms(gain, mean, inv, gain_grad, shift_grad, total):
    d_spread = -0.5 * gain * gain_grad * inv * inv
    d_mean = -gain * shift_grad * inv - 2.0 * mean * d_spread
    return gain * inv, d_mean / total, 2.0 * d_spread / total


def border_kernel(sc, x, w, tap_0, tap_2, up, down):
    rows = x.shape[0]
    tap_0[...] = dot(x[...], w[0])
    tap_2[...] = dot(x[...], w[2])
    up[...] = tap_0[rows - AREA : rows, :]
    down[...] = tap_2[0:AREA, :]


def first_kernel(frames, sc, tap_0, tap_1, tap_2, before, after, place, pre, copies, last, first):
    for t in range(frames):
        here = slice(t * AREA, (t + 1) * AREA)
        prev = before[...] if t == 0 else tap_0[(t - 1) * AREA : t * AREA, :]
        following = after[...] if t == frames - 1 else tap_2[(t + 1) * AREA : (t + 2) * AREA, :]
        pre[here, :] = tap_1[here, :] + sc[1 + t] * prev + sc[1 + frames + t] * following
    last[...] = pre[(frames - 1) * AREA : frames * AREA, :]
    first[...] = pre[0:AREA, :]
    valid = place[:, 0:1]
    for c in chunks(pre.shape[1]):
        hidden = pre[:, c]
        masked = hidden * valid
        emit(copies, 0, c, column_sum(masked))
        emit(copies, 1, c, column_sum(masked * hidden))


def inside(place, down, right):
    y = place[:, 2:3] + float(down)
    x = place[:, 1:2] + float(right)
    top = float(SIDE - 1)
    ok = (y >= 0.0) & (y <= top) & (x >= 0.0) & (x <= top)
    return ok.astype(F32)


def fill_padded(padded, value):
    rows, width = value.shape
    padded[0:EDGE, :] = jnp.zeros((EDGE, width), F32)
    padded[EDGE + rows : 2 * EDGE + rows, :] = jnp.zeros((EDGE, width), F32)
    padded[EDGE : EDGE + rows, :] = value


def second_kernel(sc, copies_in, pre_1, gain, shift, w, place, pre_2, windows, copies, stats, padded):
    rows, width = pre_1.shape
    total = sc[0]
    mean, inv = moments_of(jnp.sum(copies_in[...], axis=0), total)
    stats[0:1, :] = mean
    stats[1:2, :] = inv
    act = (pre_1[...] - mean) * inv * gain[...] + shift[...]
    fill_padded(padded, (act * jax.nn.sigmoid(act)).astype(BF16).astype(F32))
    for tap in range(9):
        down, right = tap // 3 - 1, tap % 3 - 1
        start = EDGE + down * SIDE + right
        window = padded[start : start + rows, :]
        if tap != 4:
            window = window * inside(place, down, right)
        windows[:, tap * width : (tap + 1) * width] = window.astype(BF16)
    pre_2[...] = dot(windows[...], w[...])
    valid = place[:, 0:1]
    for c in chunks(width):
        hidden = pre_2[:, c]
        masked = hidden * valid
        emit(copies, 0, c, column_sum(masked))
        emit(copies, 1, c, column_sum(masked * hidden))


def third_kernel(sc, copies_in, pre_2, gain, shift, w, place, cot, z_2, pre_3, copies, stats):
    total = sc[0]
    mean, inv = moments_of(jnp.sum(copies_in[...], axis=0), total)
    stats[0:1, :] = mean
    stats[1:2, :] = inv
    act = (pre_2[...] - mean) * inv * gain[...] + shift[...]
    z_2[...] = (act * jax.nn.sigmoid(act)).astype(BF16)
    valid = place[:, 0:1]
    for c in chunks(w.shape[1], 2 * LANE):
        pre_3[:, c] = dot(z_2[...], w[:, c])
    for c in chunks(w.shape[1]):
        hidden = pre_3[:, c]
        masked = hidden * valid
        emit(copies, 0, c, column_sum(masked))
        emit(copies, 1, c, column_sum(masked * hidden))
        emit(copies, 2, c, column_sum(cot[:, c].astype(F32)))


def unit_kernel(sc, copies_in, pre_3, x, gain, shift, pool, counts, w_key, w_value, unit, pooled, kv, stats):
    total = sc[0]
    sums = jnp.sum(copies_in[...], axis=0)
    mean, inv = moments_of(sums, total)
    stats[0:1, :] = mean
    stats[1:2, :] = inv
    stats[2:3, :] = sums[2:3]
    blocks, inner = pool.shape[0], w_key.shape[1]
    for c in chunks(x.shape[1]):
        scale = inv[:, c] * gain[:, c]
        summed = x[:, c].astype(F32) + (pre_3[:, c] - mean[:, c]) * scale + shift[:, c]
        unit[:, c] = (summed * jax.nn.sigmoid(summed)).astype(BF16)
    for c in chunks(x.shape[1], 2 * LANE):
        sums_here = dot(pool[...], unit[:, c])
        high = sums_here.astype(BF16)
        pooled[0:blocks, c] = high
        pooled[blocks : 2 * blocks, c] = (sums_here - high.astype(F32)).astype(BF16)
    many = jnp.maximum(counts[:, 0:1], 1.0)
    for k, w in enumerate((w_key, w_value)):
        for c in chunks(inner, 2 * LANE):
            both = dot(pooled[...], w[:, c])
            to = slice(k * inner + c.start, k * inner + c.stop)
            kv[:, to] = ((both[:blocks] + both[blocks:]) / many).astype(BF16)


def attend_kernel(slots, sc, theta, w, cot, place, key_row, *refs):
    blocks = refs[:slots]
    kv, probs, attended, pre_4, copies = refs[slots:]
    size, inner = blocks[0].shape[0], theta.shape[1]
    for k in range(slots):
        kv[k * size : (k + 1) * size, :] = blocks[k][...]
    logits = dot_cols(theta[...], kv[:, 0:inner])
    allowed = place[:, 3:4] == key_row[0:1, :]
    scores = jnp.where(allowed, logits * TEMPER, key_row[1:2, :])
    exponent = jnp.exp(scores - jnp.max(scores, axis=1, keepdims=True))
    weights = exponent / jnp.sum(exponent, axis=1, keepdims=True)
    probs[...] = weights
    attended[...] = dot(weights.astype(BF16), kv[:, inner:]).astype(BF16)
    valid = place[:, 0:1]
    for c in chunks(w.shape[1], 2 * LANE):
        pre_4[:, c] = dot(attended[...], w[:, c])
    for c in chunks(w.shape[1]):
        hidden = pre_4[:, c]
        masked = hidden * valid
        emit(copies, 0, c, column_sum(masked))
        emit(copies, 1, c, column_sum(masked * hidden))
        emit(copies, 2, c, column_sum(cot[:, c].astype(F32) * hidden))


def attend_back_kernel(slots, sc, copies_in, stats_3, pre_4, cot, gain, w, probs, kv, theta, place, key_row, *refs):
    d_final, d_logits, stats, own = refs[:4]
    sent = refs[4:]
    total = sc[0]
    size, inner = own.shape[0], theta.shape[1]
    sums = jnp.sum(copies_in[...], axis=0)
    mean, inv = moments_of(sums, total)
    shift_grad = stats_3[2:3, :]
    gain_grad = inv * (sums[2:3] - mean * shift_grad)
    stats[0:1, :] = mean
    stats[1:2, :] = inv
    stats[2:3, :] = gain_grad
    scale, base, slope = back_terms(gain[...], mean, inv, gain_grad, shift_grad, total)
    valid = place[:, 0:1]
    for c in chunks(cot.shape[1]):
        d_final[:, c] = (
            cot[:, c].astype(F32) * scale[:, c]
            + valid * (base[:, c] + pre_4[:, c] * slope[:, c])
        ).astype(BF16)
    d_attended = dot_cols(d_final[...], w[...]).astype(BF16)
    d_probs = dot_cols(d_attended, kv[:, inner:])
    weights = probs[...]
    row_terms = jnp.sum(weights * d_probs, axis=1, keepdims=True)
    allowed = place[:, 3:4] == key_row[0:1, :]
    d_scores = jnp.where(allowed, TEMPER * weights * (d_probs - row_terms), 0.0)
    d_logits[...] = d_scores.astype(BF16)
    d_keys = dot_rows(d_logits[...], theta[...])
    d_values = dot_rows(weights.astype(BF16), d_attended)
    own[:, 0:inner] = d_keys[0:size]
    own[:, inner:] = d_values[0:size]
    for k in range(1, slots):
        here = slice(k * size, (k + 1) * size)
        sent[k - 1][:, 0:inner] = d_keys[here].astype(BF16)
        sent[k - 1][:, inner:] = d_values[here].astype(BF16)


def summed_back_kernel(slots, sc, own, d_unit_part, pre_3, x, stats_3, gain, shift, spread, counts, w_key, w_value, *refs):
    received = refs[: slots - 1]
    d_pooled, d_summed, copies, stacked = refs[slots - 1 :]
    size, inner = own.shape[0], w_key.shape[1]
    many = jnp.maximum(counts[:, 0:1], 1.0)
    whole = own[...]
    for other in received:
        whole = whole + other[...].astype(F32)
    low = (whole / many).astype(BF16)
    d_pooled[0:size, :] = low
    d_pooled[size : 2 * size, :] = low
    for c in chunks(x.shape[1], 2 * LANE):
        part = dot_cols(low[:, 0:inner], w_key[c, :]) + dot_cols(low[:, inner:], w_value[c, :])
        high = part.astype(BF16)
        stacked[0:size, c] = high
        stacked[size : 2 * size, c] = (part - high.astype(F32)).astype(BF16)
    mean, inv = stats_3[0:1, :], stats_3[1:2, :]
    for c in chunks(x.shape[1], 2 * LANE):
        d_unit = d_unit_part[:, c] + dot(spread[...], stacked[:, c])
        normed = (pre_3[:, c] - mean[:, c]) * inv[:, c]
        summed = x[:, c].astype(F32) + normed * gain[:, c] + shift[:, c]
        d_here = silu_grad(summed, d_unit)
        d_summed[:, c] = d_here
        emit(copies, 0, c, column_sum(d_here * normed))
        emit(copies, 1, c, column_sum(d_here))


def third_back_kernel(sc, copies_in, stats_3, gain_3, d_summed, pre_3, w, pre_2, stats_2, gain_2, shift_2, place, d_third, d_act, copies, grads):
    total = sc[0]
    sums = jnp.sum(copies_in[...], axis=0)
    grads[...] = sums
    scale, base, slope = back_terms(
        gain_3[...], stats_3[0:1, :], stats_3[1:2, :], sums[0:1], sums[1:2], total
    )
    valid = place[:, 0:1]
    for c in chunks(d_summed.shape[1]):
        d_third[:, c] = (
            d_summed[:, c] * scale[:, c] + valid * (base[:, c] + pre_3[:, c] * slope[:, c])
        ).astype(BF16)
    d_z = dot_cols(d_third[...], w[...])
    normed = (pre_2[...] - stats_2[0:1, :]) * stats_2[1:2, :]
    d_here = silu_grad(normed * gain_2[...] + shift_2[...], d_z)
    d_act[...] = d_here
    for c in chunks(d_here.shape[1]):
        emit(copies, 0, c, column_sum((d_here * normed)[:, c]))
        emit(copies, 1, c, column_sum(d_here[:, c]))


def second_back_kernel(frames, sc, copies_in, stats_2, gain_2, d_act_2, pre_2, w, pre_1, stats_1, gain_1, shift_1, place, d_second, d_act, copies, grads, last, first, padded):
    total = sc[0]
    rows, width = pre_1.shape
    sums = jnp.sum(copies_in[...], axis=0)
    grads[...] = sums
    scale, base, slope = back_terms(
        gain_2[...], stats_2[0:1, :], stats_2[1:2, :], sums[0:1], sums[1:2], total
    )
    low = (d_act_2[...] * scale + place[:, 0:1] * (base + pre_2[...] * slope)).astype(BF16)
    d_second[...] = low
    fill_padded(padded, low.astype(F32))
    d_z = dot_cols(low, w[4])
    for tap in range(9):
        if tap == 4:
            continue
        down, right = 1 - tap // 3, 1 - tap % 3
        start = EDGE + down * SIDE + right
        window = padded[start : start + rows, :] * inside(place, down, right)
        d_z = d_z + dot_cols(window.astype(BF16), w[tap])
    normed = (pre_1[...] - stats_1[0:1, :]) * stats_1[1:2, :]
    d_here = silu_grad(normed * gain_1[...] + shift_1[...], d_z)
    d_act[...] = d_here
    last[...] = d_act[(frames - 1) * AREA : frames * AREA, :]
    first[...] = d_act[0:AREA, :]
    for c in chunks(width):
        emit(copies, 0, c, column_sum((d_here * normed)[:, c]))
        emit(copies, 1, c, column_sum(d_here[:, c]))


def first_back_kernel(frames, sc, copies_in, stats_1, gain_1, d_act, pre_1, d_before, d_after, pre_before, pre_after, w, d_summed, place, near, input_grad, d_taps, grads, whole, moved):
    total = sc[0]
    width = pre_1.shape[1]
    sums = jnp.sum(copies_in[...], axis=0)
    grads[...] = sums
    scale, base, slope = back_terms(
        gain_1[...], stats_1[0:1, :], stats_1[1:2, :], sums[0:1], sums[1:2], total
    )
    whole[...] = d_act[...] * scale + place[:, 0:1] * (base + pre_1[...] * slope)
    d_taps[:, width : 2 * width] = whole[...].astype(BF16)
    d_prev = d_before[...] * scale + near[:, 0:1] * (base + pre_before[...] * slope)
    d_next = d_after[...] * scale + near[:, 1:2] * (base + pre_after[...] * slope)
    for t in range(frames):
        here = slice(t * AREA, (t + 1) * AREA)
        ahead = d_next if t == frames - 1 else whole[(t + 1) * AREA : (t + 2) * AREA, :]
        moved[here, :] = ahead * sc[1 + frames + t]
    d_taps[:, 0:width] = moved[...].astype(BF16)
    for t in range(frames):
        here = slice(t * AREA, (t + 1) * AREA)
        behind = d_prev if t == 0 else whole[(t - 1) * AREA : t * AREA, :]
        moved[here, :] = behind * sc[1 + t]
    d_taps[:, 2 * width :] = moved[...].astype(BF16)
    for c in chunks(d_summed.shape[1], 2 * LANE):
        value = d_summed[:, c]
        for tap in range(3):
            value = value + dot_cols(d_taps[:, tap * width : (tap + 1) * width], w[tap, c, :])
        input_grad[:, c] = value


def local(
    inputs, segment_ids, pad_mask, time_weight, gain_first, shift_first, space_weight, gain_second,
    shift_second, expand_weight, gain_third, shift_third, query_weight, key_weight, value_weight,
    out_weight, gain_final, shift_final, cotangent,
):
    rows, channels = inputs.shape
    frames = rows // AREA
    narrow = time_weight.shape[2]
    inner = query_weight.shape[1]
    pos_count, grp_count = lax.axis_size("pos"), lax.axis_size("grp")
    group_frames = frames * grp_count
    layer, block = lax.axis_index("grp"), lax.axis_index("pos")
    up = [(i, i + 1) for i in range(grp_count - 1)]
    down = [(i + 1, i) for i in range(grp_count - 1)]
    copies = first_count()
    own_keys = frames * HALF * HALF
    size = -(-own_keys // 16) * 16
    row = lambda v: v.reshape(1, -1)
    gain_1, shift_1, gain_2, shift_2 = map(row, (gain_first, shift_first, gain_second, shift_second))
    gain_3, shift_3, gain_4 = map(row, (gain_third, shift_third, gain_final))

    seg_group = lax.dynamic_slice_in_dim(segment_ids, block * group_frames, group_frames)
    border = jnp.full((1,), -1, jnp.int32)
    seg_padded = jnp.concatenate([border, seg_group, border])
    seg_own = lax.dynamic_slice_in_dim(seg_padded, layer * frames + 1, frames)
    seg_before = lax.dynamic_slice_in_dim(seg_padded, layer * frames, frames)
    seg_after = lax.dynamic_slice_in_dim(seg_padded, layer * frames + 2, frames)
    total = jnp.sum(pad_mask.astype(F32))
    scalars = jnp.concatenate(
        [total[None], (seg_before == seg_own).astype(F32), (seg_after == seg_own).astype(F32)]
    )
    start = (block * grp_count + layer) * rows
    valid = lax.dynamic_slice_in_dim(pad_mask, start, rows).astype(F32)
    spot = np.arange(rows)
    place = jnp.stack(
        [
            valid,
            jnp.asarray(spot % SIDE, F32),
            jnp.asarray(spot % AREA // SIDE, F32),
            jnp.broadcast_to(seg_own[:, None], (frames, AREA)).reshape(rows).astype(F32),
        ],
        axis=1,
    )
    near_start = jnp.stack([jnp.maximum(start - AREA, 0), start + rows])
    near = jnp.stack(
        [lax.dynamic_slice_in_dim(pad_mask, near_start[k], AREA) for k in range(2)], axis=1
    ).astype(F32)
    owner = (spot // AREA) * HALF * HALF + (spot % AREA // SIDE // 2) * HALF + spot % SIDE // 2
    member = np.zeros((size, rows), np.float32)
    member[owner, spot] = 1.0
    pool = (jnp.asarray(member) * valid[None, :]).astype(BF16)
    half_spread = (jnp.asarray(member.T.copy()) * valid[:, None]).astype(BF16)
    spread = jnp.concatenate([half_spread, half_spread], axis=1)
    mask_group = lax.dynamic_slice_in_dim(
        pad_mask, block * group_frames * AREA, group_frames * AREA
    ).astype(F32)
    key_counts = jnp.sum(
        mask_group.reshape(grp_count, frames, HALF, 2, HALF, 2), axis=(3, 5)
    ).reshape(grp_count, own_keys)
    key_seg = jnp.broadcast_to(
        seg_group.reshape(grp_count, frames, 1), (grp_count, frames, HALF * HALF)
    ).reshape(grp_count, own_keys)
    key_seg = jnp.where(key_counts > 0.5, key_seg.astype(F32), -1.0)
    key_seg = jnp.pad(key_seg, ((0, 0), (0, size - own_keys)), constant_values=-1.0)
    order = layer ^ np.arange(grp_count)
    floor = np.full((grp_count, size), MASKED_SCORE, np.float32)
    floor[:, own_keys:] = PAD_SCORE
    key_row = jnp.stack([key_seg[order].reshape(-1), jnp.asarray(floor.reshape(-1))])
    counts = jnp.pad(
        lax.dynamic_index_in_dim(key_counts, layer, 0, False), (0, size - own_keys)
    )[:, None]

    narrow_f32 = ((rows, narrow), F32)
    wide_f32 = ((rows, channels), F32)
    wide_bf16 = ((rows, channels), BF16)
    frame_f32 = ((AREA, narrow), F32)

    tap_0, tap_2, to_next, to_prev = call(
        border_kernel, [narrow_f32, narrow_f32, frame_f32, frame_f32], scalars, inputs, time_weight,
        flops=4 * rows * channels * narrow,
    )
    before = lax.ppermute(to_next, "grp", up)
    after = lax.ppermute(to_prev, "grp", down)
    tap_1 = dot(inputs, time_weight[1])
    pre_1, sums, last, first = call(
        functools.partial(first_kernel, frames),
        [narrow_f32, ((copies, 2, narrow), F32), frame_f32, frame_f32],
        scalars, tap_0, tap_1, tap_2, before, after, place,
    )
    sums = trade(sums)
    pre_before = lax.ppermute(last, "grp", up)
    pre_after = lax.ppermute(first, "grp", down)
    pre_2, windows, sums, stats_1 = call(
        second_kernel,
        [narrow_f32, ((rows, 9 * narrow), BF16), ((copies, 2, narrow), F32), ((2, narrow), F32)],
        scalars, sums, pre_1, gain_1, shift_1, space_weight.reshape(9 * narrow, narrow), place,
        scratch=[pltpu.VMEM((rows + 2 * EDGE, narrow), F32)],
        flops=18 * rows * narrow * narrow,
    )
    sums = trade(sums)
    z_2, pre_3, sums, stats_2 = call(
        third_kernel,
        [((rows, narrow), BF16), wide_f32, ((copies, 3, channels), F32), ((2, narrow), F32)],
        scalars, sums, pre_2, gain_2, shift_2, expand_weight, place, cotangent,
        flops=2 * rows * narrow * channels,
    )
    sums = trade(sums)
    unit, pooled, kv_own, stats_3 = call(
        unit_kernel,
        [wide_bf16, ((2 * size, channels), BF16), ((size, 2 * inner), BF16), ((3, channels), F32)],
        scalars, sums, pre_3, inputs, gain_3, shift_3, pool, counts, key_weight, value_weight,
        flops=2 * size * channels * (rows + 4 * inner),
    )
    kv_blocks = [kv_own] + [
        lax.ppermute(kv_own, "grp", flip(grp_count, step)) for step in range(1, grp_count)
    ]
    theta = dot(unit, query_weight).astype(BF16)
    kv, probs, attended, pre_4, sums = call(
        functools.partial(attend_kernel, grp_count),
        [
            ((grp_count * size, 2 * inner), BF16), ((rows, grp_count * size), F32),
            ((rows, inner), BF16), wide_f32, ((copies, 3, channels), F32),
        ],
        scalars, theta, out_weight, cotangent, place, key_row, *kv_blocks,
        flops=2 * rows * inner * (2 * grp_count * size + channels),
    )
    sums = trade(sums)

    d_final, d_logits, stats_4, d_kv, *d_sent = call(
        functools.partial(attend_back_kernel, grp_count),
        [
            wide_bf16, ((rows, grp_count * size), BF16), ((3, channels), F32),
            ((size, 2 * inner), F32),
        ]
        + [((size, 2 * inner), BF16)] * (grp_count - 1),
        scalars, sums, stats_3, pre_4, cotangent, gain_4, out_weight, probs, kv, theta, place, key_row,
        flops=2 * rows * inner * (3 * grp_count * size + channels),
    )
    d_received = [
        lax.ppermute(d_sent[step - 1], "grp", flip(grp_count, step)) for step in range(1, grp_count)
    ]
    gain_final_grad, shift_final_grad = stats_4[2], stats_3[2]
    output = (
        unit.astype(F32)
        + (pre_4 - stats_4[0]) * stats_4[1] * gain_final
        + shift_final
    ).astype(BF16)
    d_theta = dot(d_logits, kv[:, :inner]).astype(BF16)
    d_unit_part = cotangent.astype(F32) + dot_cols(d_theta, query_weight)
    d_pooled, d_summed, sums = call(
        functools.partial(summed_back_kernel, grp_count),
        [((2 * size, 2 * inner), BF16), wide_f32, ((copies, 2, channels), F32)],
        scalars, d_kv, d_unit_part, pre_3, inputs, stats_3, gain_3, shift_3, spread, counts,
        key_weight, value_weight, *d_received,
        scratch=[pltpu.VMEM((2 * size, channels), BF16)],
        flops=4 * size * channels * (inner + rows),
    )
    sums = trade(sums)
    d_third, d_act_2, sums, grads_3 = call(
        third_back_kernel,
        [wide_bf16, narrow_f32, ((copies, 2, narrow), F32), ((2, channels), F32)],
        scalars, sums, stats_3, gain_3, d_summed, pre_3, expand_weight, pre_2, stats_2, gain_2,
        shift_2, place,
        flops=2 * rows * narrow * channels,
    )
    sums = trade(sums)
    d_second, d_act_1, sums, grads_2, last, first = call(
        functools.partial(second_back_kernel, frames),
        [
            ((rows, narrow), BF16), narrow_f32, ((copies, 2, narrow), F32), ((2, narrow), F32),
            frame_f32, frame_f32,
        ],
        scalars, sums, stats_2, gain_2, d_act_2, pre_2, space_weight, pre_1, stats_1, gain_1,
        shift_1, place,
        scratch=[pltpu.VMEM((rows + 2 * EDGE, narrow), F32)],
        flops=18 * rows * narrow * narrow,
    )
    sums = trade(sums)
    d_before = lax.ppermute(last, "grp", up)
    d_after = lax.ppermute(first, "grp", down)
    input_grad, d_taps, grads_1 = call(
        functools.partial(first_back_kernel, frames),
        [wide_f32, ((rows, 3 * narrow), BF16), ((2, narrow), F32)],
        scalars, sums, stats_1, gain_1, d_act_1, pre_1, d_before, d_after, pre_before, pre_after,
        time_weight, d_summed, place, near,
        scratch=[pltpu.VMEM((rows, narrow), F32), pltpu.VMEM((rows, narrow), F32)],
        flops=6 * rows * narrow * channels,
    )

    def row_shards(part):
        return part.reshape(pos_count, part.shape[0] // pos_count, part.shape[1])

    def col_shards(part):
        wide = part.shape[1] // pos_count
        return part.reshape(part.shape[0], pos_count, wide).transpose(1, 0, 2)

    def bundle(parts):
        return jnp.concatenate([p.reshape(pos_count, -1, LANE) for p in parts], axis=1)

    share_1 = shrink(
        bundle([col_shards(dot_rows(attended, d_final)), row_shards(dot_rows(unit, d_theta))])
    )
    share_2 = shrink(
        bundle(
            [
                row_shards(dot_rows(pooled, d_pooled[:, :inner])),
                row_shards(dot_rows(pooled, d_pooled[:, inner:])),
            ]
        )
    )
    space_part = dot_rows(windows, d_second).reshape(9, narrow, narrow)
    time_part = jnp.stack(
        [dot_rows(inputs, d_taps[:, k * narrow : (k + 1) * narrow]) for k in range(3)]
    )

    def stack_shards(part):
        count, depth, wide = part.shape
        cut = part.reshape(count, pos_count, depth // pos_count, wide)
        return cut.transpose(1, 0, 2, 3)

    share_3 = shrink(
        bundle([col_shards(dot_rows(z_2, d_third)), stack_shards(space_part)])
    )
    share_4 = shrink(bundle([stack_shards(time_part)]))

    def take(share, start, shape):
        extent = int(np.prod(shape)) // LANE
        return share[start : start + extent].reshape(shape)

    deep, wide = channels // pos_count, narrow // pos_count
    half = deep * inner // LANE
    out_grad = take(share_1, 0, (inner, deep))
    query_grad = take(share_1, half, (deep, inner))
    key_grad = take(share_2, 0, (deep, inner))
    value_grad = take(share_2, half, (deep, inner))
    expand_grad = take(share_3, 0, (narrow, deep))
    space_grad = take(share_3, narrow * deep // LANE, (9, wide, narrow))
    time_grad = take(share_4, 0, (3, deep, narrow))
    return (
        output, input_grad, time_grad, grads_1[0], grads_1[1], space_grad,
        grads_2[0], grads_2[1], expand_grad, grads_3[0], grads_3[1],
        query_grad, key_grad, value_grad, out_grad, gain_final_grad, shift_final_grad,
    )


def solution(mesh):
    split = P(("pos", "grp"), None)
    in_specs = (split,) + (P(),) * 17 + (split,)
    out_specs = (
        split, split, P(None, "pos", None), P(), P(), P(None, "pos", None), P(), P(),
        P(None, "pos"), P(), P(), P("pos", None), P("pos", None), P("pos", None),
        P(None, "pos"), P(), P(),
    )
    return jax.shard_map(local, mesh=mesh, in_specs=in_specs, out_specs=out_specs, check_vma=False)
```

```python
import functools

import jax
import jax.numpy as jnp
import numpy as np
from jax import lax
from jax.experimental import pallas as pl
from jax.experimental.pallas import tpu as pltpu
from jax.sharding import PartitionSpec as P

SIDE = 14
HALF = SIDE // 2
AREA = SIDE * SIDE
LANE = 128
EDGE = 16
EPSILON = 1e-05
TEMPER = 0.2
MASKED_SCORE = -1000000000.0
PAD_SCORE = -2000000000.0
F32 = jnp.float32
BF16 = jnp.bfloat16
VMEM_BYTES = 60 * 1024 * 1024


def flip(count, bit):
    return [(i, i ^ bit) for i in range(count)]


def dot(left, right):
    return jnp.dot(left, right, preferred_element_type=F32)


def dot_rows(left, right):
    return lax.dot_general(left, right, (((0,), (0,)), ((), ())), preferred_element_type=F32)


def dot_cols(left, right):
    return lax.dot_general(left, right, (((1,), (1,)), ((), ())), preferred_element_type=F32)


def first_count():
    pos_count, grp_count = lax.axis_size("pos"), lax.axis_size("grp")
    return pos_count * grp_count if pos_count * grp_count <= 64 else pos_count


def trade(copies):
    pos_count, grp_count = lax.axis_size("pos"), lax.axis_size("grp")
    if pos_count * grp_count <= 64:
        return lax.all_to_all(copies, ("pos", "grp"), 0, 0, tiled=True)
    part = lax.all_to_all(copies, "pos", 0, 0, tiled=True).sum(0)
    copies = jnp.broadcast_to(part[None], (grp_count,) + part.shape)
    return lax.all_to_all(copies, "grp", 0, 0, tiled=True)


def tie(wanted, *others):
    return lax.optimization_barrier((wanted,) + others)


def call(kernel, outs, scalars, *arrays, scratch=(), flops=0):
    shapes = [jax.ShapeDtypeStruct(shape, kind) for shape, kind in outs]
    moved = sum(int(np.prod(s.shape)) * s.dtype.itemsize for s in shapes)
    moved += sum(a.size * a.dtype.itemsize for a in arrays)
    return pl.pallas_call(
        kernel,
        out_shape=shapes,
        in_specs=[pl.BlockSpec(memory_space=pltpu.SMEM)] * len(scalars)
        + [pl.BlockSpec(memory_space=pltpu.VMEM)] * len(arrays),
        out_specs=[pl.BlockSpec(memory_space=pltpu.VMEM)] * len(shapes),
        scratch_shapes=list(scratch),
        compiler_params=pltpu.CompilerParams(vmem_limit_bytes=VMEM_BYTES),
        cost_estimate=pl.CostEstimate(flops=flops, bytes_accessed=moved, transcendentals=0),
    )(*scalars, *arrays)


def chunks(width, step=LANE):
    return [slice(start, start + step) for start in range(0, width, step)]


def emit(copies_ref, row, where, value):
    count = copies_ref.shape[0]
    copies_ref[:, row : row + 1, where] = jnp.broadcast_to(
        value[None], (count,) + value.shape
    )


def column_sum(value):
    return jnp.sum(value, axis=0, keepdims=True)


def moments_of(sums, total):
    mean = sums[0:1] / total
    return mean, lax.rsqrt(sums[1:2] / total - mean * mean + EPSILON)


def silu_grad(pre_act, gradient):
    sig = jax.nn.sigmoid(pre_act)
    return gradient * sig * (1.0 + pre_act * (1.0 - sig))


def back_terms(gain, mean, inv, gain_grad, shift_grad, total):
    d_spread = -0.5 * gain * gain_grad * inv * inv
    d_mean = -gain * shift_grad * inv - 2.0 * mean * d_spread
    return gain * inv, d_mean / total, 2.0 * d_spread / total


def border_kernel(x, w, tap_0, tap_2, up, down):
    rows = x.shape[0]
    tap_0[...] = dot(x[...], w[0])
    tap_2[...] = dot(x[...], w[2])
    up[...] = tap_0[rows - AREA : rows, :]
    down[...] = tap_2[0:AREA, :]


def first_kernel(frames, sc, tap_0, tap_1, tap_2, before, after, place, pre, copies, last, first):
    for t in range(frames):
        here = slice(t * AREA, (t + 1) * AREA)
        prev = before[...] if t == 0 else tap_0[(t - 1) * AREA : t * AREA, :]
        following = after[...] if t == frames - 1 else tap_2[(t + 1) * AREA : (t + 2) * AREA, :]
        pre[here, :] = tap_1[here, :] + sc[1 + t] * prev + sc[1 + frames + t] * following
    last[...] = pre[(frames - 1) * AREA : frames * AREA, :]
    first[...] = pre[0:AREA, :]
    valid = place[:, 0:1]
    for c in chunks(pre.shape[1]):
        hidden = pre[:, c]
        masked = hidden * valid
        emit(copies, 0, c, column_sum(masked))
        emit(copies, 1, c, column_sum(masked * hidden))


def inside(place, down, right):
    y = place[:, 2:3] + float(down)
    x = place[:, 1:2] + float(right)
    top = float(SIDE - 1)
    ok = (y >= 0.0) & (y <= top) & (x >= 0.0) & (x <= top)
    return ok.astype(F32)


def fill_padded(padded, value):
    rows, width = value.shape
    padded[0:EDGE, :] = jnp.zeros((EDGE, width), F32)
    padded[EDGE + rows : 2 * EDGE + rows, :] = jnp.zeros((EDGE, width), F32)
    padded[EDGE : EDGE + rows, :] = value


def second_kernel(sc, copies_in, pre_1, gain, shift, w, place, pre_2, windows, copies, stats, padded):
    rows, width = pre_1.shape
    total = sc[0]
    mean, inv = moments_of(jnp.sum(copies_in[...], axis=0), total)
    stats[0:1, :] = mean
    stats[1:2, :] = inv
    act = (pre_1[...] - mean) * inv * gain[...] + shift[...]
    fill_padded(padded, (act * jax.nn.sigmoid(act)).astype(BF16).astype(F32))
    for tap in range(9):
        down, right = tap // 3 - 1, tap % 3 - 1
        start = EDGE + down * SIDE + right
        window = padded[start : start + rows, :]
        if tap != 4:
            window = window * inside(place, down, right)
        windows[:, tap * width : (tap + 1) * width] = window.astype(BF16)
    pre_2[...] = dot(windows[...], w[...])
    valid = place[:, 0:1]
    for c in chunks(width):
        hidden = pre_2[:, c]
        masked = hidden * valid
        emit(copies, 0, c, column_sum(masked))
        emit(copies, 1, c, column_sum(masked * hidden))


def third_kernel(sc, copies_in, pre_2, gain, shift, w, place, cot, z_2, pre_3, copies, stats):
    total = sc[0]
    mean, inv = moments_of(jnp.sum(copies_in[...], axis=0), total)
    stats[0:1, :] = mean
    stats[1:2, :] = inv
    act = (pre_2[...] - mean) * inv * gain[...] + shift[...]
    z_2[...] = (act * jax.nn.sigmoid(act)).astype(BF16)
    valid = place[:, 0:1]
    for c in chunks(w.shape[1], 2 * LANE):
        pre_3[:, c] = dot(z_2[...], w[:, c])
    for c in chunks(w.shape[1]):
        hidden = pre_3[:, c]
        masked = hidden * valid
        emit(copies, 0, c, column_sum(masked))
        emit(copies, 1, c, column_sum(masked * hidden))
        emit(copies, 2, c, column_sum(cot[:, c].astype(F32)))


def unit_kernel(sc, copies_in, pre_3, x, gain, shift, pool, counts, w_key, w_value, unit, pooled, kv, stats):
    total = sc[0]
    sums = jnp.sum(copies_in[...], axis=0)
    mean, inv = moments_of(sums, total)
    stats[0:1, :] = mean
    stats[1:2, :] = inv
    stats[2:3, :] = sums[2:3]
    blocks, inner = pool.shape[0], w_key.shape[1]
    for c in chunks(x.shape[1]):
        scale = inv[:, c] * gain[:, c]
        summed = x[:, c].astype(F32) + (pre_3[:, c] - mean[:, c]) * scale + shift[:, c]
        unit[:, c] = (summed * jax.nn.sigmoid(summed)).astype(BF16)
    for c in chunks(x.shape[1], 2 * LANE):
        sums_here = dot(pool[...], unit[:, c])
        high = sums_here.astype(BF16)
        pooled[0:blocks, c] = high
        pooled[blocks : 2 * blocks, c] = (sums_here - high.astype(F32)).astype(BF16)
    many = jnp.maximum(counts[:, 0:1], 1.0)
    for k, w in enumerate((w_key, w_value)):
        for c in chunks(inner, 2 * LANE):
            both = dot(pooled[...], w[:, c])
            to = slice(k * inner + c.start, k * inner + c.stop)
            kv[:, to] = ((both[:blocks] + both[blocks:]) / many).astype(BF16)


def attend_kernel(slots, sc, theta, w, cot, place, key_row, *refs):
    blocks = refs[:slots]
    kv, probs, attended, pre_4, copies = refs[slots:]
    size, inner = blocks[0].shape[0], theta.shape[1]
    for k in range(slots):
        kv[k * size : (k + 1) * size, :] = blocks[k][...]
    logits = dot_cols(theta[...], kv[:, 0:inner])
    allowed = place[:, 3:4] == key_row[0:1, :]
    scores = jnp.where(allowed, logits * TEMPER, key_row[1:2, :])
    exponent = jnp.exp(scores - jnp.max(scores, axis=1, keepdims=True))
    weights = exponent / jnp.sum(exponent, axis=1, keepdims=True)
    probs[...] = weights
    attended[...] = dot(weights.astype(BF16), kv[:, inner:]).astype(BF16)
    valid = place[:, 0:1]
    for c in chunks(w.shape[1], 2 * LANE):
        pre_4[:, c] = dot(attended[...], w[:, c])
    for c in chunks(w.shape[1]):
        hidden = pre_4[:, c]
        masked = hidden * valid
        emit(copies, 0, c, column_sum(masked))
        emit(copies, 1, c, column_sum(masked * hidden))
        emit(copies, 2, c, column_sum(cot[:, c].astype(F32) * hidden))


def attend_back_kernel(slots, sc, copies_in, stats_3, pre_4, cot, gain, w, probs, kv, theta, place, key_row, *refs):
    d_final, d_logits, stats, own = refs[:4]
    sent = refs[4:]
    total = sc[0]
    size, inner = own.shape[0], theta.shape[1]
    sums = jnp.sum(copies_in[...], axis=0)
    mean, inv = moments_of(sums, total)
    shift_grad = stats_3[2:3, :]
    gain_grad = inv * (sums[2:3] - mean * shift_grad)
    stats[0:1, :] = mean
    stats[1:2, :] = inv
    stats[2:3, :] = gain_grad
    scale, base, slope = back_terms(gain[...], mean, inv, gain_grad, shift_grad, total)
    valid = place[:, 0:1]
    for c in chunks(cot.shape[1]):
        d_final[:, c] = (
            cot[:, c].astype(F32) * scale[:, c]
            + valid * (base[:, c] + pre_4[:, c] * slope[:, c])
        ).astype(BF16)
    d_attended = dot_cols(d_final[...], w[...]).astype(BF16)
    d_probs = dot_cols(d_attended, kv[:, inner:])
    weights = probs[...]
    row_terms = jnp.sum(weights * d_probs, axis=1, keepdims=True)
    allowed = place[:, 3:4] == key_row[0:1, :]
    d_scores = jnp.where(allowed, TEMPER * weights * (d_probs - row_terms), 0.0)
    d_logits[...] = d_scores.astype(BF16)
    d_keys = dot_rows(d_logits[...], theta[...])
    d_values = dot_rows(weights.astype(BF16), d_attended)
    own[:, 0:inner] = d_keys[0:size]
    own[:, inner:] = d_values[0:size]
    for k in range(1, slots):
        here = slice(k * size, (k + 1) * size)
        sent[k - 1][:, 0:inner] = d_keys[here].astype(BF16)
        sent[k - 1][:, inner:] = d_values[here].astype(BF16)


def summed_back_kernel(slots, sc, own, d_unit_part, pre_3, x, stats_3, gain, shift, spread, counts, w_key, w_value, *refs):
    received = refs[: slots - 1]
    d_pooled, d_summed, copies, stacked = refs[slots - 1 :]
    size, inner = own.shape[0], w_key.shape[1]
    many = jnp.maximum(counts[:, 0:1], 1.0)
    whole = own[...]
    for other in received:
        whole = whole + other[...].astype(F32)
    low = (whole / many).astype(BF16)
    d_pooled[0:size, :] = low
    d_pooled[size : 2 * size, :] = low
    for c in chunks(x.shape[1], 2 * LANE):
        part = dot_cols(low[:, 0:inner], w_key[c, :]) + dot_cols(low[:, inner:], w_value[c, :])
        high = part.astype(BF16)
        stacked[0:size, c] = high
        stacked[size : 2 * size, c] = (part - high.astype(F32)).astype(BF16)
    mean, inv = stats_3[0:1, :], stats_3[1:2, :]
    for c in chunks(x.shape[1], 2 * LANE):
        d_unit = d_unit_part[:, c] + dot(spread[...], stacked[:, c])
        normed = (pre_3[:, c] - mean[:, c]) * inv[:, c]
        summed = x[:, c].astype(F32) + normed * gain[:, c] + shift[:, c]
        d_here = silu_grad(summed, d_unit)
        d_summed[:, c] = d_here
        emit(copies, 0, c, column_sum(d_here * normed))
        emit(copies, 1, c, column_sum(d_here))


def third_back_kernel(sc, copies_in, stats_3, gain_3, d_summed, pre_3, w, pre_2, stats_2, gain_2, shift_2, place, d_third, d_act, copies, grads):
    total = sc[0]
    sums = jnp.sum(copies_in[...], axis=0)
    grads[...] = sums
    scale, base, slope = back_terms(
        gain_3[...], stats_3[0:1, :], stats_3[1:2, :], sums[0:1], sums[1:2], total
    )
    valid = place[:, 0:1]
    for c in chunks(d_summed.shape[1]):
        d_third[:, c] = (
            d_summed[:, c] * scale[:, c] + valid * (base[:, c] + pre_3[:, c] * slope[:, c])
        ).astype(BF16)
    d_z = dot_cols(d_third[...], w[...])
    normed = (pre_2[...] - stats_2[0:1, :]) * stats_2[1:2, :]
    d_here = silu_grad(normed * gain_2[...] + shift_2[...], d_z)
    d_act[...] = d_here
    for c in chunks(d_here.shape[1]):
        emit(copies, 0, c, column_sum((d_here * normed)[:, c]))
        emit(copies, 1, c, column_sum(d_here[:, c]))


def second_back_kernel(frames, sc, copies_in, stats_2, gain_2, d_act_2, pre_2, w, pre_1, stats_1, gain_1, shift_1, place, d_second, d_act, copies, grads, last, first, padded):
    total = sc[0]
    rows, width = pre_1.shape
    sums = jnp.sum(copies_in[...], axis=0)
    grads[...] = sums
    scale, base, slope = back_terms(
        gain_2[...], stats_2[0:1, :], stats_2[1:2, :], sums[0:1], sums[1:2], total
    )
    low = (d_act_2[...] * scale + place[:, 0:1] * (base + pre_2[...] * slope)).astype(BF16)
    d_second[...] = low
    fill_padded(padded, low.astype(F32))
    d_z = dot_cols(low, w[4])
    for tap in range(9):
        if tap == 4:
            continue
        down, right = 1 - tap // 3, 1 - tap % 3
        start = EDGE + down * SIDE + right
        window = padded[start : start + rows, :] * inside(place, down, right)
        d_z = d_z + dot_cols(window.astype(BF16), w[tap])
    normed = (pre_1[...] - stats_1[0:1, :]) * stats_1[1:2, :]
    d_here = silu_grad(normed * gain_1[...] + shift_1[...], d_z)
    d_act[...] = d_here
    last[...] = d_act[(frames - 1) * AREA : frames * AREA, :]
    first[...] = d_act[0:AREA, :]
    for c in chunks(width):
        emit(copies, 0, c, column_sum((d_here * normed)[:, c]))
        emit(copies, 1, c, column_sum(d_here[:, c]))


def first_back_kernel(frames, sc, copies_in, stats_1, gain_1, d_act, pre_1, d_before, d_after, pre_before, pre_after, w, d_summed, place, near, input_grad, d_taps, grads, whole, moved):
    total = sc[0]
    width = pre_1.shape[1]
    sums = jnp.sum(copies_in[...], axis=0)
    grads[...] = sums
    scale, base, slope = back_terms(
        gain_1[...], stats_1[0:1, :], stats_1[1:2, :], sums[0:1], sums[1:2], total
    )
    whole[...] = d_act[...] * scale + place[:, 0:1] * (base + pre_1[...] * slope)
    d_taps[:, width : 2 * width] = whole[...].astype(BF16)
    d_prev = d_before[...] * scale + near[:, 0:1] * (base + pre_before[...] * slope)
    d_next = d_after[...] * scale + near[:, 1:2] * (base + pre_after[...] * slope)
    for t in range(frames):
        here = slice(t * AREA, (t + 1) * AREA)
        ahead = d_next if t == frames - 1 else whole[(t + 1) * AREA : (t + 2) * AREA, :]
        moved[here, :] = ahead * sc[1 + frames + t]
    d_taps[:, 0:width] = moved[...].astype(BF16)
    for t in range(frames):
        here = slice(t * AREA, (t + 1) * AREA)
        behind = d_prev if t == 0 else whole[(t - 1) * AREA : t * AREA, :]
        moved[here, :] = behind * sc[1 + t]
    d_taps[:, 2 * width :] = moved[...].astype(BF16)
    for c in chunks(d_summed.shape[1], 2 * LANE):
        value = d_summed[:, c]
        for tap in range(3):
            value = value + dot_cols(d_taps[:, tap * width : (tap + 1) * width], w[tap, c, :])
        input_grad[:, c] = value


def put(both, part, start, value):
    rows = value.shape[0]
    for k, c in enumerate(chunks(value.shape[1])):
        both[part & 1, part >> 1, start + k * rows : start + (k + 1) * rows, :] = value[:, c]


def pack(both, part, start, value):
    wide = value.shape[1]
    fold = LANE // wide
    step = LANE // fold
    for k in range(fold):
        both[part & 1, part >> 1, start : start + step, k * wide : (k + 1) * wide] = value[
            k * step : (k + 1) * step, :
        ]


def split_out(mine, start, both, low, send, keep, sems):
    rows = low.shape[1]
    kept = pltpu.make_async_copy(both.at[mine], keep.at[:, start : start + rows], sems.at[0])
    kept.start()
    low[...] = both[1 - mine].astype(BF16)
    sent = pltpu.make_async_copy(low, send.at[:, start : start + rows], sems.at[1])
    sent.start()
    kept.wait()
    sent.wait()


def attend_grads_kernel(parts, start, bits, d_logits, kv, cot, w, attended, d_final, unit, send, keep, d_unit_part, d_theta, both, low, sems):
    inner, channels = attended.shape[1], unit.shape[1]
    d_theta[...] = dot(d_logits[...], kv[:, 0:inner]).astype(BF16)
    for c in chunks(channels, 2 * LANE):
        d_unit_part[:, c] = cot[:, c].astype(F32) + dot_cols(d_theta[...], w[c, :])
    wide = channels // parts
    for p in range(parts):
        here = slice(p * wide, (p + 1) * wide)
        put(both, p, inner * wide // LANE, dot_rows(unit[:, here], d_theta[...]))
    for c in chunks(inner):
        grad = dot_rows(attended[:, c], d_final[...])
        for p in range(parts):
            pack(both, p, c.start * wide // LANE, grad[:, p * wide : (p + 1) * wide])
    split_out(bits[0], start, both, low, send, keep, sems)


def pooled_grads_kernel(parts, start, bits, send_in, keep_in, pooled, d_pooled, send, keep, both, low, sems):
    wide = pooled.shape[1] // parts
    for p in range(parts):
        put(both, p, 0, dot_rows(pooled[:, p * wide : (p + 1) * wide], d_pooled[...]))
    split_out(bits[0], start, both, low, send, keep, sems)


def expand_grads_kernel(parts, start, bits, z_2, d_third, send, keep, both, low, sems):
    wide = d_third.shape[1] // parts
    for c in chunks(z_2.shape[1]):
        grad = dot_rows(z_2[:, c], d_third[...])
        for p in range(parts):
            pack(both, p, c.start * wide // LANE, grad[:, p * wide : (p + 1) * wide])
    split_out(bits[0], start, both, low, send, keep, sems)


def space_grads_kernel(parts, start, bits, send_in, keep_in, windows, d_second, send, keep, both, low, sems):
    width = d_second.shape[1]
    wide = width // parts
    for tap in range(9):
        grad = dot_rows(windows[:, tap * width : (tap + 1) * width], d_second[...])
        for p in range(parts):
            put(both, p, tap * wide * width // LANE, grad[p * wide : (p + 1) * wide, :])
    split_out(bits[0], start, both, low, send, keep, sems)


def time_grads_kernel(parts, start, bits, send_in, keep_in, x, d_taps, send, keep, both, low, sems):
    wide = x.shape[1] // parts
    for p in range(parts):
        put(both, p, 0, dot_rows(x[:, p * wide : (p + 1) * wide], d_taps[...]))
    split_out(bits[0], start, both, low, send, keep, sems)


def core_stage_kernel(cut, low_bit, high_bit, bits, keep_in, received, send_1, keep_1, send_2, keep_2):
    count = send_1.shape[0]
    rows = keep_in.shape[1]
    for send, keep, bit, here, low in (
        (send_1, keep_1, low_bit, slice(0, cut), True),
        (send_2, keep_2, high_bit, slice(cut, rows), False),
    ):
        mine = bits[bit]
        for i in range(count):
            at = 2 * i + mine if low else i + count * mine
            off = 2 * i + 1 - mine if low else i + count * (1 - mine)
            keep[i] = keep_in[at, here, :] + received[at, here, :].astype(F32)
            send[i] = (keep_in[off, here, :] + received[off, here, :].astype(F32)).astype(BF16)


def plane_stage_kernel(low_bit, high_bit, bits, in_1, received_1, in_2, received_2, send_1, keep_1, send_2, keep_2):
    count = send_1.shape[0]
    for keep_in, received, send, keep, bit, low in (
        (in_1, received_1, send_1, keep_1, low_bit, True),
        (in_2, received_2, send_2, keep_2, high_bit, False),
    ):
        mine = bits[bit]
        for i in range(count):
            at = 2 * i + mine if low else i + count * mine
            off = 2 * i + 1 - mine if low else i + count * (1 - mine)
            keep[i] = keep_in[at] + received[at].astype(F32)
            send[i] = (keep_in[off] + received[off].astype(F32)).astype(BF16)


def layer_stage_kernel(bit, bits, in_1, received_1, in_2, received_2, send, keep):
    first = in_1[...] + received_1[...].astype(F32)
    second = in_2[...] + received_2[...].astype(F32)
    swap = bits[bit] == 1
    keep[...] = jnp.where(swap, second, first)
    send[...] = jnp.where(swap, first, second).astype(BF16)


def half_stage_kernel(bit, bits, keep_in, received, send, keep):
    mine = bits[bit]
    keep[0] = keep_in[mine] + received[mine].astype(F32)
    send[0] = (keep_in[1 - mine] + received[1 - mine].astype(F32)).astype(BF16)


def join_kernel(keep_in, received, low):
    low[...] = (keep_in[...] + received[...].astype(F32)).astype(BF16)


def exchange_kernel(low, received, final):
    final[...] = (low[...].astype(F32) + received[...].astype(F32)).astype(BF16)


def unfold(part, start, out):
    rows = out.shape[0]
    for k, c in enumerate(chunks(out.shape[1])):
        out[:, c] = part[start + k * rows : start + (k + 1) * rows, :]


def attend_outs_kernel(bit, bits, mine, other, out_grad, query_grad, key_grad, value_grad, first, second):
    swap = bits[bit] == 1
    here, there = mine[0].astype(F32), other[0].astype(F32)
    first[...] = jnp.where(swap, there, here)
    second[...] = jnp.where(swap, here, there)
    unfold(first, 0, out_grad)
    unfold(first, out_grad.shape[0], query_grad)
    unfold(second, 0, key_grad)
    unfold(second, first.shape[0] // 2, value_grad)


def bottleneck_outs_kernel(bit, bits, mine, other, expand_grad, space_grad, time_grad, first, second):
    swap = bits[bit] == 1
    here, there = mine[0].astype(F32), other[0].astype(F32)
    first[...] = jnp.where(swap, there, here)
    second[...] = jnp.where(swap, here, there)
    unfold(first, 0, expand_grad)
    taps, deep, width = space_grad.shape
    for tap in range(taps):
        start = expand_grad.shape[0] + tap * deep * width // LANE
        for k, c in enumerate(chunks(width)):
            space_grad[tap, :, c] = first[start + k * deep : start + (k + 1) * deep, :]
    taps, deep, width = time_grad.shape
    for tap in range(taps):
        for k, c in enumerate(chunks(width)):
            start = (tap * width // LANE + k) * deep
            time_grad[tap, :, c] = second[start : start + deep, :]


class Bundle:
    def __init__(self, bits, cut):
        self.bits, self.cut = bits, cut
        self.pos_count, self.grp_count = lax.axis_size("pos"), lax.axis_size("grp")
        self.pos_bits = self.pos_count.bit_length() - 1
        self.grp_bits = self.grp_count.bit_length() - 1
        self.send = self.keep = None

    def add(self, kernel, start, rows, *arrays, extra=(), flops=0):
        whole = (self.pos_count // 2, 2 * self.cut, LANE)
        half = (self.pos_count // 2, rows, LANE)
        held = () if self.send is None else (self.send, self.keep)
        anywhere = pl.BlockSpec(memory_space=pl.ANY)
        inside_vmem = pl.BlockSpec(memory_space=pltpu.VMEM)
        shapes = [jax.ShapeDtypeStruct(whole, BF16), jax.ShapeDtypeStruct(whole, F32)]
        shapes += [jax.ShapeDtypeStruct(shape, kind) for shape, kind in extra]
        moved = sum(a.size * a.dtype.itemsize for a in arrays) + 6 * int(np.prod(half))
        self.send, self.keep, *rest = pl.pallas_call(
            functools.partial(kernel, self.pos_count, start),
            out_shape=shapes,
            in_specs=[pl.BlockSpec(memory_space=pltpu.SMEM)]
            + [anywhere] * len(held)
            + [inside_vmem] * len(arrays),
            out_specs=[anywhere, anywhere] + [inside_vmem] * len(extra),
            scratch_shapes=[
                pltpu.VMEM((2,) + half, F32), pltpu.VMEM(half, BF16), pltpu.SemaphoreType.DMA((2,)),
            ],
            input_output_aliases={1: 0, 2: 1} if held else {},
            compiler_params=pltpu.CompilerParams(vmem_limit_bytes=VMEM_BYTES),
            cost_estimate=pl.CostEstimate(flops=flops, bytes_accessed=moved, transcendentals=0),
        )(self.bits, *held, *arrays)
        return rest

    def begin(self):
        self.received = lax.ppermute(self.send, "pos", flip(self.pos_count, 1))

    def plane(self):
        count = self.pos_count // 4
        bits = (1, self.pos_bits - 1)
        outs = []
        for rows in (self.cut, self.cut):
            outs += [((count, rows, LANE), BF16), ((count, rows, LANE), F32)]
        outs = call(
            functools.partial(core_stage_kernel, self.cut, *bits), outs, (self.bits,),
            self.keep, self.received,
        )
        self.parts = [list(outs[:2]), list(outs[2:])]
        self.pair = bits
        self.turn()

    def turn(self):
        for k in range(2):
            pairs = flip(self.pos_count, 1 << self.pair[k])
            self.parts[k].append(lax.ppermute(self.parts[k][0], "pos", pairs))

    def more(self):
        while self.parts[0][1].shape[0] > 1:
            count = self.parts[0][1].shape[0] // 2
            self.pair = (self.pair[0] + 1, self.pair[1] - 1)
            outs = [((count, self.cut, LANE), BF16), ((count, self.cut, LANE), F32)] * 2
            (_, keep_1, got_1), (_, keep_2, got_2) = self.parts
            outs = call(
                functools.partial(plane_stage_kernel, *self.pair), outs, (self.bits,),
                keep_1, got_1, keep_2, got_2,
            )
            self.parts = [list(outs[:2]), list(outs[2:])]
            self.turn()

    def layer(self):
        (_, keep_1, got_1), (_, keep_2, got_2) = self.parts
        shape = (1, self.cut, LANE)
        send, keep = call(
            functools.partial(layer_stage_kernel, self.pos_bits), [(shape, BF16), (shape, F32)],
            (self.bits,), keep_1, got_1, keep_2, got_2,
        )
        got = lax.ppermute(send, "grp", flip(self.grp_count, 1))
        for bit in range(1, self.grp_bits - 1):
            shape = (2, keep.shape[1] // 2, LANE)
            half = (1,) + shape[1:]
            send, keep = call(
                functools.partial(half_stage_kernel, self.pos_bits + bit),
                [(half, BF16), (half, F32)], (self.bits,), keep.reshape(shape), got.reshape(shape),
            )
            got = lax.ppermute(send, "grp", flip(self.grp_count, 1 << bit))
        (self.low,) = call(join_kernel, [(keep.shape, BF16)], (), keep, got)
        self.other = lax.ppermute(self.low, "grp", flip(self.grp_count, self.grp_count // 2))

    def finish(self):
        (final,) = call(exchange_kernel, [(self.low.shape, BF16)], (), self.low, self.other)
        for bit in reversed(range(1, self.grp_bits - 1)):
            mine = self.bits[self.pos_bits + bit]
            other = lax.ppermute(final, "grp", flip(self.grp_count, 1 << bit))
            lower = jnp.where(mine == 0, final, other)
            upper = jnp.where(mine == 0, other, final)
            final = jnp.concatenate([lower, upper], axis=1)
        self.mine = final
        self.other = lax.ppermute(final, "grp", flip(self.grp_count, 1))

    def outs(self, kernel, shapes):
        part = pltpu.VMEM((self.cut, LANE), F32)
        return call(
            functools.partial(kernel, self.pos_bits), [(shape, F32) for shape in shapes],
            (self.bits,), self.mine, self.other, scratch=[part, part],
        )

    def shares(self):
        swap = self.bits[self.pos_bits] == 1
        first = jnp.where(swap, self.other, self.mine)[0].astype(F32)
        second = jnp.where(swap, self.mine, self.other)[0].astype(F32)
        return first, second


def local(
    inputs, segment_ids, pad_mask, time_weight, gain_first, shift_first, space_weight, gain_second,
    shift_second, expand_weight, gain_third, shift_third, query_weight, key_weight, value_weight,
    out_weight, gain_final, shift_final, cotangent,
):
    rows, channels = inputs.shape
    frames = rows // AREA
    narrow = time_weight.shape[2]
    inner = query_weight.shape[1]
    pos_count, grp_count = lax.axis_size("pos"), lax.axis_size("grp")
    group_frames = frames * grp_count
    layer, block = lax.axis_index("grp"), lax.axis_index("pos")
    up = [(i, i + 1) for i in range(grp_count - 1)]
    down = [(i + 1, i) for i in range(grp_count - 1)]
    copies = first_count()
    own_keys = frames * HALF * HALF
    size = -(-own_keys // 16) * 16
    row = lambda v: v.reshape(1, -1)
    deep, wide = channels // pos_count, narrow // pos_count
    bits = jnp.stack(
        [(block >> k) & 1 for k in range(pos_count.bit_length() - 1)]
        + [(layer >> k) & 1 for k in range(grp_count.bit_length() - 1)]
    ).astype(jnp.int32)
    gain_1, shift_1, gain_2, shift_2 = map(row, (gain_first, shift_first, gain_second, shift_second))
    gain_3, shift_3, gain_4 = map(row, (gain_third, shift_third, gain_final))

    seg_group = lax.dynamic_slice_in_dim(segment_ids, block * group_frames, group_frames)
    border = jnp.full((1,), -1, jnp.int32)
    seg_padded = jnp.concatenate([border, seg_group, border])
    seg_own = lax.dynamic_slice_in_dim(seg_padded, layer * frames + 1, frames)
    seg_before = lax.dynamic_slice_in_dim(seg_padded, layer * frames, frames)
    seg_after = lax.dynamic_slice_in_dim(seg_padded, layer * frames + 2, frames)
    total = jnp.sum(pad_mask.astype(F32))
    scalars = jnp.concatenate(
        [total[None], (seg_before == seg_own).astype(F32), (seg_after == seg_own).astype(F32)]
    )
    start = (block * grp_count + layer) * rows
    valid = lax.dynamic_slice_in_dim(pad_mask, start, rows).astype(F32)
    spot = np.arange(rows)
    place = jnp.stack(
        [
            valid,
            jnp.asarray(spot % SIDE, F32),
            jnp.asarray(spot % AREA // SIDE, F32),
            jnp.broadcast_to(seg_own[:, None], (frames, AREA)).reshape(rows).astype(F32),
        ],
        axis=1,
    )
    near_start = jnp.stack([jnp.maximum(start - AREA, 0), start + rows])
    near = jnp.stack(
        [lax.dynamic_slice_in_dim(pad_mask, near_start[k], AREA) for k in range(2)], axis=1
    ).astype(F32)
    owner = (spot // AREA) * HALF * HALF + (spot % AREA // SIDE // 2) * HALF + spot % SIDE // 2
    member = np.zeros((size, rows), np.float32)
    member[owner, spot] = 1.0
    pool = (jnp.asarray(member) * valid[None, :]).astype(BF16)
    half_spread = (jnp.asarray(member.T.copy()) * valid[:, None]).astype(BF16)
    spread = jnp.concatenate([half_spread, half_spread], axis=1)
    mask_group = lax.dynamic_slice_in_dim(
        pad_mask, block * group_frames * AREA, group_frames * AREA
    ).astype(F32)
    key_counts = jnp.sum(
        mask_group.reshape(grp_count, frames, HALF, 2, HALF, 2), axis=(3, 5)
    ).reshape(grp_count, own_keys)
    key_seg = jnp.broadcast_to(
        seg_group.reshape(grp_count, frames, 1), (grp_count, frames, HALF * HALF)
    ).reshape(grp_count, own_keys)
    key_seg = jnp.where(key_counts > 0.5, key_seg.astype(F32), -1.0)
    key_seg = jnp.pad(key_seg, ((0, 0), (0, size - own_keys)), constant_values=-1.0)
    order = layer ^ np.arange(grp_count)
    floor = np.full((grp_count, size), MASKED_SCORE, np.float32)
    floor[:, own_keys:] = PAD_SCORE
    key_row = jnp.stack([key_seg[order].reshape(-1), jnp.asarray(floor.reshape(-1))])
    counts = jnp.pad(
        lax.dynamic_index_in_dim(key_counts, layer, 0, False), (0, size - own_keys)
    )[:, None]

    narrow_f32 = ((rows, narrow), F32)
    wide_f32 = ((rows, channels), F32)
    wide_bf16 = ((rows, channels), BF16)
    frame_f32 = ((AREA, narrow), F32)

    tap_0, tap_2, to_next, to_prev = call(
        border_kernel, [narrow_f32, narrow_f32, frame_f32, frame_f32], (), inputs, time_weight,
        flops=4 * rows * channels * narrow,
    )
    before = lax.ppermute(to_next, "grp", up)
    after = lax.ppermute(to_prev, "grp", down)
    tap_1 = dot(inputs, time_weight[1])
    pre_1, sums, last, first = call(
        functools.partial(first_kernel, frames),
        [narrow_f32, ((copies, 2, narrow), F32), frame_f32, frame_f32],
        (scalars,), tap_0, tap_1, tap_2, before, after, place,
    )
    sums = trade(sums)
    pre_before = lax.ppermute(last, "grp", up)
    pre_after = lax.ppermute(first, "grp", down)
    pre_2, windows, sums, stats_1 = call(
        second_kernel,
        [narrow_f32, ((rows, 9 * narrow), BF16), ((copies, 2, narrow), F32), ((2, narrow), F32)],
        (scalars,), sums, pre_1, gain_1, shift_1, space_weight.reshape(9 * narrow, narrow), place,
        scratch=[pltpu.VMEM((rows + 2 * EDGE, narrow), F32)],
        flops=18 * rows * narrow * narrow,
    )
    sums = trade(sums)
    z_2, pre_3, sums, stats_2 = call(
        third_kernel,
        [((rows, narrow), BF16), wide_f32, ((copies, 3, channels), F32), ((2, narrow), F32)],
        (scalars,), sums, pre_2, gain_2, shift_2, expand_weight, place, cotangent,
        flops=2 * rows * narrow * channels,
    )
    sums = trade(sums)
    unit, pooled, kv_own, stats_3 = call(
        unit_kernel,
        [wide_bf16, ((2 * size, channels), BF16), ((size, 2 * inner), BF16), ((3, channels), F32)],
        (scalars,), sums, pre_3, inputs, gain_3, shift_3, pool, counts, key_weight, value_weight,
        flops=2 * size * channels * (rows + 4 * inner),
    )
    kv_blocks = [kv_own] + [
        lax.ppermute(kv_own, "grp", flip(grp_count, step)) for step in range(1, grp_count)
    ]
    theta = dot(unit, query_weight).astype(BF16)
    kv, probs, attended, pre_4, sums = call(
        functools.partial(attend_kernel, grp_count),
        [
            ((grp_count * size, 2 * inner), BF16), ((rows, grp_count * size), F32),
            ((rows, inner), BF16), wide_f32, ((copies, 3, channels), F32),
        ],
        (scalars,), theta, out_weight, cotangent, place, key_row, *kv_blocks,
        flops=2 * rows * inner * (2 * grp_count * size + channels),
    )
    sums = trade(sums)

    d_final, d_logits, stats_4, d_kv, *d_sent = call(
        functools.partial(attend_back_kernel, grp_count),
        [
            wide_bf16, ((rows, grp_count * size), BF16), ((3, channels), F32),
            ((size, 2 * inner), F32),
        ]
        + [((size, 2 * inner), BF16)] * (grp_count - 1),
        (scalars,), sums, stats_3, pre_4, cotangent, gain_4, out_weight, probs, kv, theta, place, key_row,
        flops=2 * rows * inner * (3 * grp_count * size + channels),
    )
    d_received = [
        lax.ppermute(d_sent[step - 1], "grp", flip(grp_count, step)) for step in range(1, grp_count)
    ]
    gain_final_grad, shift_final_grad = stats_4[2], stats_3[2]
    output = (
        unit.astype(F32)
        + (pre_4 - stats_4[0]) * stats_4[1] * gain_final
        + shift_final
    ).astype(BF16)
    half = deep * inner // LANE
    bundle_1 = Bundle(bits, 2 * half)
    d_unit_part, _ = bundle_1.add(
        attend_grads_kernel, 0, 2 * half,
        d_logits, kv, cotangent, query_weight, attended, d_final, unit,
        extra=[wide_f32, ((rows, inner), BF16)],
        flops=2 * rows * inner * (grp_count * size + 3 * channels),
    )
    d_pooled, d_summed, sums = call(
        functools.partial(summed_back_kernel, grp_count),
        [((2 * size, 2 * inner), BF16), wide_f32, ((copies, 2, channels), F32)],
        (scalars,), d_kv, d_unit_part, pre_3, inputs, stats_3, gain_3, shift_3, spread, counts,
        key_weight, value_weight, *d_received,
        scratch=[pltpu.VMEM((2 * size, channels), BF16)],
        flops=4 * size * channels * (inner + rows),
    )
    sums = trade(sums)
    bundle_1.add(
        pooled_grads_kernel, 2 * half, 2 * half, pooled, d_pooled,
        flops=8 * size * channels * inner,
    )
    bundle_1.begin()
    sums, bundle_1.send = tie(sums, bundle_1.send)
    d_third, d_act_2, sums, grads_3 = call(
        third_back_kernel,
        [wide_bf16, narrow_f32, ((copies, 2, narrow), F32), ((2, channels), F32)],
        (scalars,), sums, stats_3, gain_3, d_summed, pre_3, expand_weight, pre_2, stats_2, gain_2,
        shift_2, place,
        flops=2 * rows * narrow * channels,
    )
    sums = trade(sums)
    tap_rows = wide * narrow // LANE
    expand_rows = narrow * deep // LANE
    bundle_2 = Bundle(bits, expand_rows + 9 * tap_rows)
    bundle_2.add(
        expand_grads_kernel, 0, expand_rows, z_2, d_third,
        flops=2 * rows * narrow * channels,
    )
    bundle_1.plane()
    sums, bundle_2.send, bundle_1.parts[0][1] = tie(sums, bundle_2.send, bundle_1.parts[0][1])
    d_second, d_act_1, sums, grads_2, last, first = call(
        functools.partial(second_back_kernel, frames),
        [
            ((rows, narrow), BF16), narrow_f32, ((copies, 2, narrow), F32), ((2, narrow), F32),
            frame_f32, frame_f32,
        ],
        (scalars,), sums, stats_2, gain_2, d_act_2, pre_2, space_weight, pre_1, stats_1, gain_1,
        shift_1, place,
        scratch=[pltpu.VMEM((rows + 2 * EDGE, narrow), F32)],
        flops=18 * rows * narrow * narrow,
    )
    sums = trade(sums)
    d_before = lax.ppermute(last, "grp", up)
    d_after = lax.ppermute(first, "grp", down)
    bundle_2.add(
        space_grads_kernel, expand_rows, 9 * tap_rows, windows, d_second,
        flops=18 * rows * narrow * narrow,
    )
    bundle_1.more()
    sums, bundle_2.send, bundle_1.parts[0][1] = tie(sums, bundle_2.send, bundle_1.parts[0][1])
    input_grad, d_taps, grads_1 = call(
        functools.partial(first_back_kernel, frames),
        [wide_f32, ((rows, 3 * narrow), BF16), ((2, narrow), F32)],
        (scalars,), sums, stats_1, gain_1, d_act_1, pre_1, d_before, d_after, pre_before, pre_after,
        time_weight, d_summed, place, near,
        scratch=[pltpu.VMEM((rows, narrow), F32), pltpu.VMEM((rows, narrow), F32)],
        flops=6 * rows * narrow * channels,
    )

    bundle_2.add(
        time_grads_kernel, bundle_2.cut, 3 * deep * narrow // LANE, inputs, d_taps,
        flops=6 * rows * narrow * channels,
    )
    bundle_2.begin()
    bundle_1.layer()
    bundle_2.plane()
    bundle_1.finish()
    bundle_2.more()
    bundle_2.layer()
    bundle_2.finish()
    if deep == LANE:
        out_grad, query_grad, key_grad, value_grad = bundle_1.outs(
            attend_outs_kernel, [(inner, deep)] + [(deep, inner)] * 3
        )
        expand_grad, space_grad, time_grad = bundle_2.outs(
            bottleneck_outs_kernel, [(narrow, deep), (9, wide, narrow), (3, deep, narrow)]
        )
    else:

        def columns(share, start, height, width):
            part = share[start : start + height * width // LANE]
            return part.reshape(width // LANE, height, LANE).transpose(1, 0, 2).reshape(height, width)

        def folded(share, start, height, width):
            part = share[start : start + height * width // LANE]
            part = part.reshape(height // LANE, width, LANE // width, width)
            return part.transpose(0, 2, 1, 3).reshape(height, width)

        first, second = bundle_1.shares()
        out_grad = folded(first, 0, inner, deep)
        query_grad = columns(first, half, deep, inner)
        key_grad = columns(second, 0, deep, inner)
        value_grad = columns(second, half, deep, inner)
        first, second = bundle_2.shares()
        expand_grad = folded(first, 0, narrow, deep)
        space_grad = jnp.stack(
            [columns(first, expand_rows + tap * tap_rows, wide, narrow) for tap in range(9)]
        )
        time_all = columns(second, 0, deep, 3 * narrow)
        time_grad = jnp.stack([time_all[:, k * narrow : (k + 1) * narrow] for k in range(3)])
    return (
        output, input_grad, time_grad, grads_1[0], grads_1[1], space_grad,
        grads_2[0], grads_2[1], expand_grad, grads_3[0], grads_3[1],
        query_grad, key_grad, value_grad, out_grad, gain_final_grad, shift_final_grad,
    )


def solution(mesh):
    split = P(("pos", "grp"), None)
    in_specs = (split,) + (P(),) * 17 + (split,)
    out_specs = (
        split, split, P(None, "pos", None), P(), P(), P(None, "pos", None), P(), P(),
        P(None, "pos"), P(), P(), P("pos", None), P("pos", None), P("pos", None),
        P(None, "pos"), P(), P(),
    )
    return jax.shard_map(local, mesh=mesh, in_specs=in_specs, out_specs=out_specs, check_vma=False)
```

```python
import functools

import jax
import jax.numpy as jnp
import numpy as np
from jax import lax
from jax.experimental import pallas as pl
from jax.experimental.pallas import tpu as pltpu
from jax.sharding import PartitionSpec as P

SIDE = 14
HALF = SIDE // 2
AREA = SIDE * SIDE
LANE = 128
EDGE = 16
EPSILON = 1e-05
TEMPER = 0.2
MASKED_SCORE = -1000000000.0
PAD_SCORE = -2000000000.0
F32 = jnp.float32
BF16 = jnp.bfloat16
VMEM_BYTES = 60 * 1024 * 1024


def flip(count, bit):
    return [(i, i ^ bit) for i in range(count)]


def dot(left, right):
    return jnp.dot(left, right, preferred_element_type=F32)


def dot_rows(left, right):
    return lax.dot_general(left, right, (((0,), (0,)), ((), ())), preferred_element_type=F32)


def dot_cols(left, right):
    return lax.dot_general(left, right, (((1,), (1,)), ((), ())), preferred_element_type=F32)


def first_count():
    pos_count, grp_count = lax.axis_size("pos"), lax.axis_size("grp")
    return pos_count * grp_count if pos_count * grp_count <= 64 else pos_count


def trade(copies):
    pos_count, grp_count = lax.axis_size("pos"), lax.axis_size("grp")
    if pos_count * grp_count <= 64:
        return lax.all_to_all(copies, ("pos", "grp"), 0, 0, tiled=True)
    part = lax.all_to_all(copies, "pos", 0, 0, tiled=True).sum(0)
    copies = jnp.broadcast_to(part[None], (grp_count,) + part.shape)
    return lax.all_to_all(copies, "grp", 0, 0, tiled=True)


def tie(wanted, *others):
    return lax.optimization_barrier((wanted,) + others)


class Stack:
    def __init__(self, arrays):
        self.arrays = arrays


def call(kernel, outs, scalars, *operands, scratch=(), flops=0):
    shapes = [jax.ShapeDtypeStruct(shape, kind) for shape, kind in outs]
    arrays, plan, stacks = [], [], []
    for operand in operands:
        if isinstance(operand, Stack):
            plan.append((len(arrays), len(operand.arrays)))
            arrays += operand.arrays
            one = operand.arrays[0]
            stacks.append(pltpu.VMEM((len(operand.arrays) * one.shape[0],) + one.shape[1:], one.dtype))
        else:
            plan.append((len(arrays), 0))
            arrays.append(operand)
    count_s, count_a = len(scalars), len(arrays)

    def body(*refs):
        scalar_refs, refs = refs[:count_s], refs[count_s:]
        in_refs, refs = refs[:count_a], refs[count_a:]
        out_refs, refs = refs[: len(shapes)], refs[len(shapes) :]
        user, stack_refs = refs[: len(scratch)], list(refs[len(scratch) :])
        seen = []
        for first, count in plan:
            if count == 0:
                seen.append(in_refs[first])
                continue
            stack = stack_refs.pop(0)
            size = in_refs[first].shape[0]
            for k in range(count):
                stack[k * size : (k + 1) * size, :] = in_refs[first + k][...]
            seen.append(stack)
        kernel(*scalar_refs, *seen, *out_refs, *user)

    moved = sum(int(np.prod(s.shape)) * s.dtype.itemsize for s in shapes)
    moved += sum(a.size * a.dtype.itemsize for a in arrays)
    near = pl.BlockSpec(memory_space=pltpu.VMEM)
    return pl.pallas_call(
        body,
        out_shape=shapes,
        in_specs=[pl.BlockSpec(memory_space=pltpu.SMEM)] * count_s + [near] * count_a,
        out_specs=[near] * len(shapes),
        scratch_shapes=list(scratch) + stacks,
        compiler_params=pltpu.CompilerParams(vmem_limit_bytes=VMEM_BYTES),
        cost_estimate=pl.CostEstimate(flops=flops, bytes_accessed=moved, transcendentals=0),
    )(*scalars, *arrays)


def chunks(width, step=LANE):
    return [slice(start, start + step) for start in range(0, width, step)]


def emit(copies_ref, start, value):
    count, _, width = copies_ref.shape
    for k in range(0, value.shape[1], LANE):
        row, lane = divmod(start + k, width)
        copies_ref[:, row : row + 1, lane : lane + LANE] = jnp.broadcast_to(
            value[None, :, k : k + LANE], (count, 1, LANE)
        )


def collect(copies_ref):
    return jnp.sum(copies_ref[...], axis=0)


def part(sums, start, size):
    width = sums.shape[1]
    pieces, end = [], start + size
    while start < end:
        row, lane = divmod(start, width)
        extent = min(width - lane, end - start)
        pieces.append(sums[row : row + 1, lane : lane + extent])
        start += extent
    return pieces[0] if len(pieces) == 1 else jnp.concatenate(pieces, axis=1)


def column_sum(value):
    return jnp.sum(value, axis=0, keepdims=True)


def project(vector, w):
    high = vector.astype(BF16).astype(F32)
    middle = (vector - high).astype(BF16).astype(F32)
    low = vector - high - middle
    blank = jnp.zeros((13, vector.shape[1]), F32)
    pieces = jnp.concatenate([high, middle, low, blank], axis=0).astype(BF16)
    return column_sum(dot(pieces, w[...]))


def moments_of(values, squares, total):
    mean = values / total
    return mean, lax.rsqrt(squares / total - mean * mean + EPSILON)


def silu_grad(pre_act, gradient):
    sig = jax.nn.sigmoid(pre_act)
    return gradient * sig * (1.0 + pre_act * (1.0 - sig))


def back_terms(gain, mean, inv, gain_grad, shift_grad, total):
    d_spread = -0.5 * gain * gain_grad * inv * inv
    d_mean = -gain * shift_grad * inv - 2.0 * mean * d_spread
    return gain * inv, d_mean / total, 2.0 * d_spread / total


def border_kernel(x, w, tap_0, tap_2, up, down):
    rows = x.shape[0]
    tap_0[...] = dot(x[...], w[0])
    up[...] = tap_0[rows - AREA : rows, :]
    tap_2[...] = dot(x[...], w[2])
    down[...] = tap_2[0:AREA, :]


def first_kernel(frames, sc, tap_0, tap_1, tap_2, place, before, after, pre, copies, last, first):
    for t in range(frames):
        here = slice(t * AREA, (t + 1) * AREA)
        prev = before[...] if t == 0 else tap_0[(t - 1) * AREA : t * AREA, :]
        following = after[...] if t == frames - 1 else tap_2[(t + 1) * AREA : (t + 2) * AREA, :]
        pre[here, :] = tap_1[here, :] + sc[1 + t] * prev + sc[1 + frames + t] * following
    last[...] = pre[(frames - 1) * AREA : frames * AREA, :].astype(BF16)
    first[...] = pre[0:AREA, :].astype(BF16)
    width = pre.shape[1]
    valid = place[:, 0:1]
    for c in chunks(width):
        hidden = pre[:, c]
        masked = hidden * valid
        emit(copies, c.start, column_sum(masked))
        emit(copies, width + c.start, column_sum(masked * hidden))


def inside(place, down, right):
    y = place[:, 2:3] + float(down)
    x = place[:, 1:2] + float(right)
    top = float(SIDE - 1)
    ok = (y >= 0.0) & (y <= top) & (x >= 0.0) & (x <= top)
    return ok.astype(F32)


def fill_padded(padded, value):
    rows, width = value.shape
    padded[0:EDGE, :] = jnp.zeros((EDGE, width), F32)
    padded[EDGE + rows : 2 * EDGE + rows, :] = jnp.zeros((EDGE, width), F32)
    padded[EDGE : EDGE + rows, :] = value


def second_kernel(sc, copies_in, pre_1, gain, shift, place, w, pre_2, windows, copies, stats, padded):
    rows, width = pre_1.shape
    total = sc[0]
    sums = collect(copies_in)
    mean, inv = moments_of(part(sums, 0, width), part(sums, width, width), total)
    stats[0:1, :] = mean
    stats[1:2, :] = inv
    act = (pre_1[...] - mean) * inv * gain[...] + shift[...]
    fill_padded(padded, (act * jax.nn.sigmoid(act)).astype(BF16).astype(F32))
    for tap in range(9):
        down, right = tap // 3 - 1, tap % 3 - 1
        start = EDGE + down * SIDE + right
        window = padded[start : start + rows, :]
        if tap != 4:
            window = window * inside(place, down, right)
        windows[:, tap * width : (tap + 1) * width] = window.astype(BF16)
    pre_2[...] = dot(windows[...], w[...])
    valid = place[:, 0:1]
    for c in chunks(width):
        hidden = pre_2[:, c]
        masked = hidden * valid
        emit(copies, c.start, column_sum(masked))
        emit(copies, width + c.start, column_sum(masked * hidden))


def third_kernel(sc, copies_in, pre_2, gain, shift, place, w, z_2, pre_3, copies, stats):
    width = pre_2.shape[1]
    total = sc[0]
    sums = collect(copies_in)
    mean, inv = moments_of(part(sums, 0, width), part(sums, width, width), total)
    stats[0:1, :] = mean
    stats[1:2, :] = inv
    valid = place[:, 0:1]
    act = (pre_2[...] - mean) * inv * gain[...] + shift[...]
    z_2[...] = (act * jax.nn.sigmoid(act)).astype(BF16)
    emit(copies, 0, column_sum(z_2[...].astype(F32) * valid))
    for c in chunks(w.shape[1], 2 * LANE):
        hidden = dot(z_2[...], w[:, c])
        pre_3[:, c] = hidden
        emit(copies, width + c.start, column_sum(hidden * hidden * valid))


def unit_kernel(sc, copies_in, w_expand, gain, shift, pre_3, x, pool, counts, w_key, w_value, unit, pooled, kv, stats):
    total = sc[0]
    narrow, channels = w_expand.shape
    sums = collect(copies_in)
    mean, inv = moments_of(
        project(part(sums, 0, narrow), w_expand), part(sums, narrow, channels), total
    )
    stats[0:1, :] = mean
    stats[1:2, :] = inv
    blocks, inner = pool.shape[0], w_key.shape[1]
    for c in chunks(channels, 2 * LANE):
        scale = inv[:, c] * gain[:, c]
        summed = x[:, c].astype(F32) + (pre_3[:, c] - mean[:, c]) * scale + shift[:, c]
        unit[:, c] = (summed * jax.nn.sigmoid(summed)).astype(BF16)
        sums_here = dot(pool[...], unit[:, c])
        high = sums_here.astype(BF16)
        pooled[0:blocks, c] = high
        pooled[blocks : 2 * blocks, c] = (sums_here - high.astype(F32)).astype(BF16)
    many = jnp.maximum(counts[:, 0:1], 1.0)
    for k, w in enumerate((w_key, w_value)):
        for c in chunks(inner, 2 * LANE):
            both = dot(pooled[...], w[:, c])
            to = slice(k * inner + c.start, k * inner + c.stop)
            kv[:, to] = ((both[:blocks] + both[blocks:]) / many).astype(BF16)


def attend_kernel(sc, theta, kv, place, key_row, w, cot, probs, attended, pre_4, copies):
    inner, channels = w.shape
    logits = dot_cols(theta[...], kv[:, 0:inner])
    allowed = place[:, 3:4] == key_row[0:1, :]
    scores = jnp.where(allowed, logits * TEMPER, key_row[1:2, :])
    exponent = jnp.exp(scores - jnp.max(scores, axis=1, keepdims=True))
    weights = exponent / jnp.sum(exponent, axis=1, keepdims=True)
    probs[...] = weights
    attended[...] = dot(weights.astype(BF16), kv[:, inner:]).astype(BF16)
    valid = place[:, 0:1]
    emit(copies, 0, column_sum(attended[...].astype(F32) * valid))
    for c in chunks(channels, 2 * LANE):
        hidden = dot(attended[...], w[:, c])
        pre_4[:, c] = hidden
        emit(copies, inner + c.start, column_sum(hidden * hidden * valid))
        emit(copies, inner + channels + c.start, column_sum(cot[:, c].astype(F32) * hidden))


def attend_back_kernel(slots, sc, copies_in, shift_copies, gain, place, key_row, w, pre_4, cot, kv, probs, theta, d_final, d_logits, mean_out, inv_out, gain_out, shift_out, own, *sent):
    total = sc[0]
    inner, channels = w.shape
    size = own.shape[0]
    sums = collect(copies_in)
    mean, inv = moments_of(
        project(part(sums, 0, inner), w), part(sums, inner, channels), total
    )
    shift_grad = part(collect(shift_copies), 0, channels)
    gain_grad = inv * (part(sums, inner + channels, channels) - mean * shift_grad)
    mean_out[...] = mean
    inv_out[...] = inv
    gain_out[...] = gain_grad
    shift_out[...] = shift_grad
    scale, base, slope = back_terms(gain[...], mean, inv, gain_grad, shift_grad, total)
    valid = place[:, 0:1]
    for c in chunks(channels, 2 * LANE):
        d_final[:, c] = (
            cot[:, c].astype(F32) * scale[:, c]
            + valid * (base[:, c] + pre_4[:, c] * slope[:, c])
        ).astype(BF16)
    d_attended = dot_cols(d_final[...], w[...]).astype(BF16)
    d_probs = dot_cols(d_attended, kv[:, inner:])
    weights = probs[...]
    row_terms = jnp.sum(weights * d_probs, axis=1, keepdims=True)
    allowed = place[:, 3:4] == key_row[0:1, :]
    d_scores = jnp.where(allowed, TEMPER * weights * (d_probs - row_terms), 0.0)
    d_logits[...] = d_scores.astype(BF16)
    d_values = dot_rows(weights.astype(BF16), d_attended)
    d_keys = dot_rows(d_logits[...], theta[...])
    own[:, 0:inner] = d_keys[0:size]
    own[:, inner:] = d_values[0:size]
    for k in range(1, slots):
        here = slice(k * size, (k + 1) * size)
        sent[k - 1][:, 0:inner] = d_keys[here].astype(BF16)
        sent[k - 1][:, inner:] = d_values[here].astype(BF16)


def summed_back_kernel(slots, sc, own, counts, w_key, w_value, stats_3, gain, shift, spread, d_unit_part, pre_3, x, *refs):
    received = refs[: slots - 1]
    d_pooled, d_summed, copies, stacked = refs[slots - 1 :]
    size, inner = own.shape[0], w_key.shape[1]
    channels = x.shape[1]
    many = jnp.maximum(counts[:, 0:1], 1.0)
    whole = own[...]
    for other in received:
        whole = whole + other[...].astype(F32)
    low = (whole / many).astype(BF16)
    d_pooled[0:size, :] = low
    d_pooled[size : 2 * size, :] = low
    mean, inv = stats_3[0:1, :], stats_3[1:2, :]
    for c in chunks(channels, 2 * LANE):
        here = dot_cols(low[:, 0:inner], w_key[c, :]) + dot_cols(low[:, inner:], w_value[c, :])
        high = here.astype(BF16)
        stacked[0:size, c] = high
        stacked[size : 2 * size, c] = (here - high.astype(F32)).astype(BF16)
        d_unit = d_unit_part[:, c] + dot(spread[...], stacked[:, c])
        normed = (pre_3[:, c] - mean[:, c]) * inv[:, c]
        summed = x[:, c].astype(F32) + normed * gain[:, c] + shift[:, c]
        d_here = silu_grad(summed, d_unit)
        d_summed[:, c] = d_here
        emit(copies, c.start, column_sum(d_here * normed))
        emit(copies, channels + c.start, column_sum(d_here))


def third_back_kernel(sc, copies_in, stats_3, gain_3, place, d_summed, pre_3, w, pre_2, stats_2, gain_2, shift_2, d_third, d_act, copies, gain_out, shift_out):
    total = sc[0]
    channels, width = pre_3.shape[1], pre_2.shape[1]
    sums = collect(copies_in)
    gain_grad, shift_grad = part(sums, 0, channels), part(sums, channels, channels)
    gain_out[...] = gain_grad
    shift_out[...] = shift_grad
    scale, base, slope = back_terms(
        gain_3[...], stats_3[0:1, :], stats_3[1:2, :], gain_grad, shift_grad, total
    )
    valid = place[:, 0:1]
    for c in chunks(channels, 2 * LANE):
        d_third[:, c] = (
            d_summed[:, c] * scale[:, c] + valid * (base[:, c] + pre_3[:, c] * slope[:, c])
        ).astype(BF16)
    d_z = dot_cols(d_third[...], w[...])
    normed = (pre_2[...] - stats_2[0:1, :]) * stats_2[1:2, :]
    d_here = silu_grad(normed * gain_2[...] + shift_2[...], d_z)
    d_act[...] = d_here
    emit(copies, 0, column_sum(d_here * normed))
    emit(copies, width, column_sum(d_here))


def second_back_kernel(frames, sc, copies_in, stats_2, gain_2, d_act_2, pre_2, place, w, pre_1, stats_1, gain_1, shift_1, d_second, d_act, copies, gain_out, shift_out, last, first, padded):
    total = sc[0]
    rows, width = pre_1.shape
    sums = collect(copies_in)
    gain_grad, shift_grad = part(sums, 0, width), part(sums, width, width)
    gain_out[...] = gain_grad
    shift_out[...] = shift_grad
    scale, base, slope = back_terms(
        gain_2[...], stats_2[0:1, :], stats_2[1:2, :], gain_grad, shift_grad, total
    )
    low = (d_act_2[...] * scale + place[:, 0:1] * (base + pre_2[...] * slope)).astype(BF16)
    d_second[...] = low
    fill_padded(padded, low.astype(F32))
    d_z = dot_cols(low, w[4])
    for tap in range(9):
        if tap == 4:
            continue
        down, right = 1 - tap // 3, 1 - tap % 3
        start = EDGE + down * SIDE + right
        window = padded[start : start + rows, :] * inside(place, down, right)
        d_z = d_z + dot_cols(window.astype(BF16), w[tap])
    normed = (pre_1[...] - stats_1[0:1, :]) * stats_1[1:2, :]
    d_here = silu_grad(normed * gain_1[...] + shift_1[...], d_z)
    d_act[...] = d_here
    last[...] = d_act[(frames - 1) * AREA : frames * AREA, :].astype(BF16)
    first[...] = d_act[0:AREA, :].astype(BF16)
    emit(copies, 0, column_sum(d_here * normed))
    emit(copies, width, column_sum(d_here))


def first_back_kernel(frames, sc, copies_in, stats_1, gain_1, d_act, pre_1, place, near, d_before, d_after, pre_before, pre_after, w, d_summed, input_grad, d_taps, gain_out, shift_out, whole, moved):
    total = sc[0]
    width = pre_1.shape[1]
    sums = collect(copies_in)
    gain_grad, shift_grad = part(sums, 0, width), part(sums, width, width)
    gain_out[...] = gain_grad
    shift_out[...] = shift_grad
    scale, base, slope = back_terms(
        gain_1[...], stats_1[0:1, :], stats_1[1:2, :], gain_grad, shift_grad, total
    )
    whole[...] = d_act[...] * scale + place[:, 0:1] * (base + pre_1[...] * slope)
    d_taps[:, width : 2 * width] = whole[...].astype(BF16)
    d_prev = d_before[...].astype(F32) * scale + near[:, 0:1] * (
        base + pre_before[...].astype(F32) * slope
    )
    d_next = d_after[...].astype(F32) * scale + near[:, 1:2] * (
        base + pre_after[...].astype(F32) * slope
    )
    for t in range(frames):
        here = slice(t * AREA, (t + 1) * AREA)
        ahead = d_next if t == frames - 1 else whole[(t + 1) * AREA : (t + 2) * AREA, :]
        moved[here, :] = ahead * sc[1 + frames + t]
    d_taps[:, 0:width] = moved[...].astype(BF16)
    for t in range(frames):
        here = slice(t * AREA, (t + 1) * AREA)
        behind = d_prev if t == 0 else whole[(t - 1) * AREA : t * AREA, :]
        moved[here, :] = behind * sc[1 + t]
    d_taps[:, 2 * width :] = moved[...].astype(BF16)
    for c in chunks(d_summed.shape[1], 2 * LANE):
        value = d_summed[:, c]
        for tap in range(3):
            value = value + dot_cols(d_taps[:, tap * width : (tap + 1) * width], w[tap, c, :])
        input_grad[:, c] = value


def put(both, part, start, value):
    rows = value.shape[0]
    for k, c in enumerate(chunks(value.shape[1])):
        both[part & 1, part >> 1, start + k * rows : start + (k + 1) * rows, :] = value[:, c]


def pack(both, part, start, value):
    wide = value.shape[1]
    fold = LANE // wide
    step = LANE // fold
    for k in range(fold):
        both[part & 1, part >> 1, start : start + step, k * wide : (k + 1) * wide] = value[
            k * step : (k + 1) * step, :
        ]


def split_out(mine, start, both, low, send, keep, sems):
    rows = low.shape[2]
    low[0] = both[mine].astype(BF16)
    kept = pltpu.make_async_copy(low.at[0], keep.at[:, start : start + rows], sems.at[0])
    kept.start()
    low[1] = both[1 - mine].astype(BF16)
    sent = pltpu.make_async_copy(low.at[1], send.at[:, start : start + rows], sems.at[1])
    sent.start()
    kept.wait()
    sent.wait()


def attend_grads_kernel(slots, parts, start, bits, d_logits, cot, w, attended, d_final, unit, *refs):
    blocks = refs[:slots]
    send, keep, d_unit_part, d_theta, both, low, sems, keys = refs[slots:]
    size = blocks[0].shape[0]
    inner, channels = attended.shape[1], unit.shape[1]
    for k in range(slots):
        keys[k * size : (k + 1) * size, :] = blocks[k][:, 0:inner]
    d_theta[...] = dot(d_logits[...], keys[...]).astype(BF16)
    for c in chunks(channels, 2 * LANE):
        d_unit_part[:, c] = cot[:, c].astype(F32) + dot_cols(d_theta[...], w[c, :])
    wide = channels // parts
    for p in range(parts):
        here = slice(p * wide, (p + 1) * wide)
        put(both, p, inner * wide // LANE, dot_rows(unit[:, here], d_theta[...]))
    for c in chunks(inner):
        grad = dot_rows(attended[:, c], d_final[...])
        for p in range(parts):
            pack(both, p, c.start * wide // LANE, grad[:, p * wide : (p + 1) * wide])
    split_out(bits[0], start, both, low, send, keep, sems)


def pooled_grads_kernel(parts, start, bits, send_in, keep_in, pooled, d_pooled, send, keep, both, low, sems):
    wide = pooled.shape[1] // parts
    for p in range(parts):
        put(both, p, 0, dot_rows(pooled[:, p * wide : (p + 1) * wide], d_pooled[...]))
    split_out(bits[0], start, both, low, send, keep, sems)


def expand_grads_kernel(parts, start, bits, z_2, d_third, send, keep, both, low, sems):
    wide = d_third.shape[1] // parts
    for c in chunks(z_2.shape[1]):
        grad = dot_rows(z_2[:, c], d_third[...])
        for p in range(parts):
            pack(both, p, c.start * wide // LANE, grad[:, p * wide : (p + 1) * wide])
    split_out(bits[0], start, both, low, send, keep, sems)


def space_grads_kernel(parts, start, bits, send_in, keep_in, windows, d_second, send, keep, both, low, sems):
    width = d_second.shape[1]
    wide = width // parts
    for tap in range(9):
        grad = dot_rows(windows[:, tap * width : (tap + 1) * width], d_second[...])
        for p in range(parts):
            put(both, p, tap * wide * width // LANE, grad[p * wide : (p + 1) * wide, :])
    split_out(bits[0], start, both, low, send, keep, sems)


def time_grads_kernel(parts, start, bits, send_in, keep_in, x, d_taps, send, keep, both, low, sems):
    wide = x.shape[1] // parts
    for p in range(parts):
        put(both, p, 0, dot_rows(x[:, p * wide : (p + 1) * wide], d_taps[...]))
    split_out(bits[0], start, both, low, send, keep, sems)


def core_stage_kernel(cut, low_bit, high_bit, bits, keep_in, received, send_1, keep_1, send_2, keep_2):
    count = send_1.shape[0]
    rows = keep_in.shape[1]
    for send, keep, bit, here, low in (
        (send_1, keep_1, low_bit, slice(0, cut), True),
        (send_2, keep_2, high_bit, slice(cut, rows), False),
    ):
        mine = bits[bit]
        for i in range(count):
            at = 2 * i + mine if low else i + count * mine
            off = 2 * i + 1 - mine if low else i + count * (1 - mine)
            keep[i] = (keep_in[at, here, :].astype(F32) + received[at, here, :].astype(F32)).astype(BF16)
            send[i] = (keep_in[off, here, :].astype(F32) + received[off, here, :].astype(F32)).astype(BF16)


def plane_stage_kernel(low_bit, high_bit, bits, in_1, received_1, in_2, received_2, send_1, keep_1, send_2, keep_2):
    count = send_1.shape[0]
    for keep_in, received, send, keep, bit, low in (
        (in_1, received_1, send_1, keep_1, low_bit, True),
        (in_2, received_2, send_2, keep_2, high_bit, False),
    ):
        mine = bits[bit]
        for i in range(count):
            at = 2 * i + mine if low else i + count * mine
            off = 2 * i + 1 - mine if low else i + count * (1 - mine)
            keep[i] = (keep_in[at].astype(F32) + received[at].astype(F32)).astype(BF16)
            send[i] = (keep_in[off].astype(F32) + received[off].astype(F32)).astype(BF16)


def half_stage_kernel(bit, bits, keep_in, received, send, keep):
    mine = bits[bit]
    keep[0] = (keep_in[mine].astype(F32) + received[mine].astype(F32)).astype(BF16)
    send[0] = (keep_in[1 - mine].astype(F32) + received[1 - mine].astype(F32)).astype(BF16)


def unfold(part, start, out):
    rows = out.shape[0]
    for k, c in enumerate(chunks(out.shape[1])):
        out[:, c] = part[start + k * rows : start + (k + 1) * rows, :]


def attend_outs_kernel(bit, bits, mine, other, out_grad, query_grad, key_grad, value_grad, first, second):
    swap = bits[bit] == 1
    here, there = mine[0].astype(F32), other[0].astype(F32)
    first[...] = jnp.where(swap, there, here)
    second[...] = jnp.where(swap, here, there)
    unfold(first, 0, out_grad)
    unfold(first, out_grad.shape[0], query_grad)
    unfold(second, 0, key_grad)
    unfold(second, first.shape[0] // 2, value_grad)


def bottleneck_outs_kernel(bit, bits, mine, other, expand_grad, space_grad, time_grad, first, second):
    swap = bits[bit] == 1
    here, there = mine[0].astype(F32), other[0].astype(F32)
    first[...] = jnp.where(swap, there, here)
    second[...] = jnp.where(swap, here, there)
    unfold(first, 0, expand_grad)
    taps, deep, width = space_grad.shape
    for tap in range(taps):
        start = expand_grad.shape[0] + tap * deep * width // LANE
        for k, c in enumerate(chunks(width)):
            space_grad[tap, :, c] = first[start + k * deep : start + (k + 1) * deep, :]
    taps, deep, width = time_grad.shape
    for tap in range(taps):
        for k, c in enumerate(chunks(width)):
            start = (tap * width // LANE + k) * deep
            time_grad[tap, :, c] = second[start : start + deep, :]


class Bundle:
    def __init__(self, bits, cut):
        self.bits, self.cut = bits, cut
        self.pos_count, self.grp_count = lax.axis_size("pos"), lax.axis_size("grp")
        self.pos_bits = self.pos_count.bit_length() - 1
        self.grp_bits = self.grp_count.bit_length() - 1
        self.send = self.keep = None

    def add(self, kernel, start, rows, *arrays, extra=(), scratch=(), flops=0):
        whole = (self.pos_count // 2, 2 * self.cut, LANE)
        half = (self.pos_count // 2, rows, LANE)
        held = () if self.send is None else (self.send, self.keep)
        anywhere = pl.BlockSpec(memory_space=pl.ANY)
        inside_vmem = pl.BlockSpec(memory_space=pltpu.VMEM)
        shapes = [jax.ShapeDtypeStruct(whole, BF16)] * 2
        shapes += [jax.ShapeDtypeStruct(shape, kind) for shape, kind in extra]
        moved = sum(a.size * a.dtype.itemsize for a in arrays) + 6 * int(np.prod(half))
        self.send, self.keep, *rest = pl.pallas_call(
            functools.partial(kernel, self.pos_count, start),
            out_shape=shapes,
            in_specs=[pl.BlockSpec(memory_space=pltpu.SMEM)]
            + [anywhere] * len(held)
            + [inside_vmem] * len(arrays),
            out_specs=[anywhere, anywhere] + [inside_vmem] * len(extra),
            scratch_shapes=[
                pltpu.VMEM((2,) + half, F32), pltpu.VMEM((2,) + half, BF16),
                pltpu.SemaphoreType.DMA((2,)),
            ]
            + list(scratch),
            input_output_aliases={1: 0, 2: 1} if held else {},
            compiler_params=pltpu.CompilerParams(vmem_limit_bytes=VMEM_BYTES),
            cost_estimate=pl.CostEstimate(flops=flops, bytes_accessed=moved, transcendentals=0),
        )(self.bits, *held, *arrays)
        return rest

    def begin(self):
        self.received = lax.ppermute(self.send, "pos", flip(self.pos_count, 1))

    def plane(self):
        count = self.pos_count // 4
        bits = (1, self.pos_bits - 1)
        outs = []
        for rows in (self.cut, self.cut):
            outs += [((count, rows, LANE), BF16)] * 2
        outs = call(
            functools.partial(core_stage_kernel, self.cut, *bits), outs, (self.bits,),
            self.keep, self.received,
        )
        self.parts = [list(outs[:2]), list(outs[2:])]
        self.pair = bits

    def turn(self):
        for k in range(2):
            pairs = flip(self.pos_count, 1 << self.pair[k])
            self.parts[k].append(lax.ppermute(self.parts[k][0], "pos", pairs))

    def hold(self, value):
        value, self.parts[0][0], self.parts[1][0] = tie(
            value, self.parts[0][0], self.parts[1][0]
        )
        return value

    def more(self, last=True):
        while self.parts[0][1].shape[0] > 1:
            count = self.parts[0][1].shape[0] // 2
            self.pair = (self.pair[0] + 1, self.pair[1] - 1)
            outs = [((count, self.cut, LANE), BF16)] * 4
            (_, keep_1, got_1), (_, keep_2, got_2) = self.parts
            outs = call(
                functools.partial(plane_stage_kernel, *self.pair), outs, (self.bits,),
                keep_1, got_1, keep_2, got_2,
            )
            self.parts = [list(outs[:2]), list(outs[2:])]
            if self.parts[0][1].shape[0] > 1 or last:
                self.turn()

    def after(self, others):
        for k, other in enumerate(others):
            self.parts[k][2], _ = tie(self.parts[k][2], other)

    def layer(self):
        (_, keep_1, got_1), (_, keep_2, got_2) = self.parts
        first = keep_1.astype(F32) + got_1.astype(F32)
        second = keep_2.astype(F32) + got_2.astype(F32)
        swap = self.bits[self.pos_bits] == 1
        keep = jnp.where(swap, second, first).astype(BF16)
        send = jnp.where(swap, first, second).astype(BF16)
        self.keep = keep
        self.got = lax.ppermute(send, "grp", flip(self.grp_count, 1))

    def exchange(self):
        keep, got = self.keep, self.got
        for bit in range(1, self.grp_bits - 1):
            shape = (2, keep.shape[1] // 2, LANE)
            half = (1,) + shape[1:]
            send, keep = call(
                functools.partial(half_stage_kernel, self.pos_bits + bit),
                [(half, BF16), (half, BF16)], (self.bits,), keep.reshape(shape), got.reshape(shape),
            )
            got = lax.ppermute(send, "grp", flip(self.grp_count, 1 << bit))
        self.low = (keep.astype(F32) + got.astype(F32)).astype(BF16)
        self.other = lax.ppermute(self.low, "grp", flip(self.grp_count, self.grp_count // 2))

    def finish(self):
        final = (self.low.astype(F32) + self.other.astype(F32)).astype(BF16)
        for bit in reversed(range(1, self.grp_bits - 1)):
            mine = self.bits[self.pos_bits + bit]
            other = lax.ppermute(final, "grp", flip(self.grp_count, 1 << bit))
            lower = jnp.where(mine == 0, final, other)
            upper = jnp.where(mine == 0, other, final)
            final = jnp.concatenate([lower, upper], axis=1)
        self.mine = final
        self.other = lax.ppermute(final, "grp", flip(self.grp_count, 1))

    def outs(self, kernel, shapes):
        part = pltpu.VMEM((self.cut, LANE), F32)
        return call(
            functools.partial(kernel, self.pos_bits), [(shape, F32) for shape in shapes],
            (self.bits,), self.mine, self.other, scratch=[part, part],
        )

    def shares(self):
        swap = self.bits[self.pos_bits] == 1
        first = jnp.where(swap, self.other, self.mine)[0].astype(F32)
        second = jnp.where(swap, self.mine, self.other)[0].astype(F32)
        return first, second


def local(
    inputs, segment_ids, pad_mask, time_weight, gain_first, shift_first, space_weight, gain_second,
    shift_second, expand_weight, gain_third, shift_third, query_weight, key_weight, value_weight,
    out_weight, gain_final, shift_final, cotangent,
):
    rows, channels = inputs.shape
    frames = rows // AREA
    narrow = time_weight.shape[2]
    inner = query_weight.shape[1]
    pos_count, grp_count = lax.axis_size("pos"), lax.axis_size("grp")
    group_frames = frames * grp_count
    layer, block = lax.axis_index("grp"), lax.axis_index("pos")
    up = [(i, i + 1) for i in range(grp_count - 1)]
    down = [(i + 1, i) for i in range(grp_count - 1)]
    copies = first_count()
    own_keys = frames * HALF * HALF
    size = -(-own_keys // 16) * 16
    row = lambda v: v.reshape(1, -1)
    deep, wide = channels // pos_count, narrow // pos_count
    bits = jnp.stack(
        [(block >> k) & 1 for k in range(pos_count.bit_length() - 1)]
        + [(layer >> k) & 1 for k in range(grp_count.bit_length() - 1)]
    ).astype(jnp.int32)
    gain_1, shift_1, gain_2, shift_2 = map(row, (gain_first, shift_first, gain_second, shift_second))
    gain_3, shift_3, gain_4 = map(row, (gain_third, shift_third, gain_final))

    seg_group = lax.dynamic_slice_in_dim(segment_ids, block * group_frames, group_frames)
    border = jnp.full((1,), -1, jnp.int32)
    seg_padded = jnp.concatenate([border, seg_group, border])
    seg_own = lax.dynamic_slice_in_dim(seg_padded, layer * frames + 1, frames)
    seg_before = lax.dynamic_slice_in_dim(seg_padded, layer * frames, frames)
    seg_after = lax.dynamic_slice_in_dim(seg_padded, layer * frames + 2, frames)
    total = jnp.sum(pad_mask.astype(F32))
    scalars = jnp.concatenate(
        [total[None], (seg_before == seg_own).astype(F32), (seg_after == seg_own).astype(F32)]
    )
    start = (block * grp_count + layer) * rows
    valid = lax.dynamic_slice_in_dim(pad_mask, start, rows).astype(F32)
    spot = np.arange(rows)
    place = jnp.stack(
        [
            valid,
            jnp.asarray(spot % SIDE, F32),
            jnp.asarray(spot % AREA // SIDE, F32),
            jnp.broadcast_to(seg_own[:, None], (frames, AREA)).reshape(rows).astype(F32),
        ],
        axis=1,
    )
    near_start = jnp.stack([jnp.maximum(start - AREA, 0), start + rows])
    near = jnp.stack(
        [lax.dynamic_slice_in_dim(pad_mask, near_start[k], AREA) for k in range(2)], axis=1
    ).astype(F32)
    owner = (spot // AREA) * HALF * HALF + (spot % AREA // SIDE // 2) * HALF + spot % SIDE // 2
    member = np.zeros((size, rows), np.float32)
    member[owner, spot] = 1.0
    pool = (jnp.asarray(member) * valid[None, :]).astype(BF16)
    half_spread = (jnp.asarray(member.T.copy()) * valid[:, None]).astype(BF16)
    spread = jnp.concatenate([half_spread, half_spread], axis=1)
    mask_group = lax.dynamic_slice_in_dim(
        pad_mask, block * group_frames * AREA, group_frames * AREA
    ).astype(F32)
    key_counts = jnp.sum(
        mask_group.reshape(grp_count, frames, HALF, 2, HALF, 2), axis=(3, 5)
    ).reshape(grp_count, own_keys)
    key_seg = jnp.broadcast_to(
        seg_group.reshape(grp_count, frames, 1), (grp_count, frames, HALF * HALF)
    ).reshape(grp_count, own_keys)
    key_seg = jnp.where(key_counts > 0.5, key_seg.astype(F32), -1.0)
    key_seg = jnp.pad(key_seg, ((0, 0), (0, size - own_keys)), constant_values=-1.0)
    order = layer ^ np.arange(grp_count)
    floor = np.full((grp_count, size), MASKED_SCORE, np.float32)
    floor[:, own_keys:] = PAD_SCORE
    key_row = jnp.stack([key_seg[order].reshape(-1), jnp.asarray(floor.reshape(-1))])
    counts = jnp.pad(
        lax.dynamic_index_in_dim(key_counts, layer, 0, False), (0, size - own_keys)
    )[:, None]

    narrow_f32 = ((rows, narrow), F32)
    wide_f32 = ((rows, channels), F32)
    wide_bf16 = ((rows, channels), BF16)
    frame_f32 = ((AREA, narrow), F32)
    frame_bf16 = ((AREA, narrow), BF16)

    small = (copies, 2, narrow)
    shift_sums = jnp.sum(cotangent.astype(F32), axis=0).reshape(1, 2, channels // 2)
    shift_sums = jnp.broadcast_to(shift_sums, (copies, 2, channels // 2))
    tap_0, tap_2, to_next, to_prev = call(
        border_kernel, [narrow_f32, narrow_f32, frame_f32, frame_f32], (),
        inputs, time_weight,
        flops=4 * rows * channels * narrow,
    )
    before = lax.ppermute(to_next, "grp", up)
    after = lax.ppermute(to_prev, "grp", down)
    tap_1 = dot(inputs, time_weight[1])
    pre_1, sums, last, first = call(
        functools.partial(first_kernel, frames),
        [narrow_f32, (small, F32), frame_bf16, frame_bf16],
        (scalars,), tap_0, tap_1, tap_2, place, before, after,
    )
    sums = trade(sums)
    pre_before = lax.ppermute(last, "grp", up)
    pre_after = lax.ppermute(first, "grp", down)
    pre_2, windows, sums, stats_1 = call(
        second_kernel,
        [narrow_f32, ((rows, 9 * narrow), BF16), (small, F32), ((2, narrow), F32)],
        (scalars,), sums, pre_1, gain_1, shift_1, place,
        space_weight.reshape(9 * narrow, narrow),
        scratch=[pltpu.VMEM((rows + 2 * EDGE, narrow), F32)],
        flops=18 * rows * narrow * narrow,
    )
    sums = trade(sums)
    sums, pre_before, pre_after = tie(sums, pre_before, pre_after)
    z_2, pre_3, sums, stats_2 = call(
        third_kernel,
        [
            ((rows, narrow), BF16), wide_f32, ((copies, 2, (narrow + channels) // 2), F32),
            ((2, narrow), F32),
        ],
        (scalars,), sums, pre_2, gain_2, shift_2, place, expand_weight,
        flops=2 * rows * narrow * channels,
    )
    sums = trade(sums)
    unit, pooled, kv_own, stats_3 = call(
        unit_kernel,
        [wide_bf16, ((2 * size, channels), BF16), ((size, 2 * inner), BF16), ((2, channels), F32)],
        (scalars,), sums, expand_weight, gain_3, shift_3, pre_3, inputs, pool, counts,
        key_weight, value_weight,
        flops=2 * size * channels * (rows + 4 * inner),
    )
    shift_sums, _ = tie(shift_sums, kv_own)
    shift_sums = trade(shift_sums)
    kv = [kv_own] + [
        lax.ppermute(kv_own, "grp", flip(grp_count, step)) for step in range(1, grp_count)
    ]
    theta = dot(unit, query_weight).astype(BF16)
    probs, attended, pre_4, sums = call(
        attend_kernel,
        [
            ((rows, grp_count * size), F32), ((rows, inner), BF16), wide_f32,
            ((copies, 4, (inner + 2 * channels) // 4), F32),
        ],
        (scalars,), theta, Stack(kv), place, key_row, out_weight, cotangent,
        flops=2 * rows * inner * (2 * grp_count * size + channels),
    )
    sums = trade(sums)

    d_final, d_logits, mean_4, inv_4, gain_final_grad, shift_final_grad, d_kv, *d_sent = call(
        functools.partial(attend_back_kernel, grp_count),
        [
            wide_bf16, ((rows, grp_count * size), BF16),
        ]
        + [((1, channels), F32)] * 4
        + [((size, 2 * inner), F32)]
        + [((size, 2 * inner), BF16)] * (grp_count - 1),
        (scalars,), sums, shift_sums, gain_4, place, key_row, out_weight, pre_4,
        cotangent, Stack(kv), probs, theta,
        flops=2 * rows * inner * (3 * grp_count * size + channels),
    )
    d_received = [
        lax.ppermute(d_sent[step - 1], "grp", flip(grp_count, step)) for step in range(1, grp_count)
    ]
    output = (
        unit.astype(F32)
        + (pre_4 - mean_4) * inv_4 * gain_final
        + shift_final
    ).astype(BF16)
    half = deep * inner // LANE
    bundle_1 = Bundle(bits, 2 * half)
    d_unit_part, _ = bundle_1.add(
        functools.partial(attend_grads_kernel, grp_count), 0, 2 * half,
        d_logits, cotangent, query_weight, attended, d_final, unit, *kv,
        extra=[wide_f32, ((rows, inner), BF16)],
        scratch=[pltpu.VMEM((grp_count * size, inner), BF16)],
        flops=2 * rows * inner * (grp_count * size + 3 * channels),
    )
    d_pooled, d_summed, sums = call(
        functools.partial(summed_back_kernel, grp_count),
        [((2 * size, 2 * inner), BF16), wide_f32, ((copies, 8, channels // 4), F32)],
        (scalars,), d_kv, counts, key_weight, value_weight, stats_3, gain_3,
        shift_3, spread, d_unit_part, pre_3, inputs, *d_received,
        scratch=[pltpu.VMEM((2 * size, channels), BF16)],
        flops=4 * size * channels * (inner + rows),
    )
    sums = trade(sums)
    bundle_1.add(
        pooled_grads_kernel, 2 * half, 2 * half, pooled, d_pooled,
        flops=8 * size * channels * inner,
    )
    sums, bundle_1.send = tie(sums, bundle_1.send)
    bundle_1.begin()
    d_third, d_act_2, sums, gain_third_grad, shift_third_grad = call(
        third_back_kernel,
        [wide_bf16, narrow_f32, (small, F32), ((1, channels), F32), ((1, channels), F32)],
        (scalars,), sums, stats_3, gain_3, place, d_summed, pre_3, expand_weight,
        pre_2, stats_2, gain_2, shift_2,
        flops=2 * rows * narrow * channels,
    )
    sums, bundle_1.received = tie(sums, bundle_1.received)
    sums = trade(sums)
    tap_rows = wide * narrow // LANE
    expand_rows = narrow * deep // LANE
    bundle_2 = Bundle(bits, expand_rows + 9 * tap_rows)
    bundle_2.add(
        expand_grads_kernel, 0, expand_rows, z_2, d_third,
        flops=2 * rows * narrow * channels,
    )
    bundle_1.plane()
    sums, _ = tie(sums, bundle_2.send)
    sums = bundle_1.hold(sums)
    bundle_1.turn()
    d_second, d_act_1, sums, gain_second_grad, shift_second_grad, last, first = call(
        functools.partial(second_back_kernel, frames),
        [
            ((rows, narrow), BF16), narrow_f32, (small, F32), ((1, narrow), F32), ((1, narrow), F32),
            frame_bf16, frame_bf16,
        ],
        (scalars,), sums, stats_2, gain_2, d_act_2, pre_2, place, space_weight, pre_1, stats_1,
        gain_1, shift_1,
        scratch=[pltpu.VMEM((rows + 2 * EDGE, narrow), F32)],
        flops=18 * rows * narrow * narrow,
    )
    sums = trade(sums)
    d_before = lax.ppermute(last, "grp", up)
    d_after = lax.ppermute(first, "grp", down)
    bundle_2.add(
        space_grads_kernel, expand_rows, 9 * tap_rows, windows, d_second,
        flops=18 * rows * narrow * narrow,
    )
    (_, _, got_1), (_, _, got_2) = bundle_1.parts
    sums, bundle_2.send, got_1, got_2 = tie(sums, bundle_2.send, got_1, got_2)
    bundle_1.parts[0][2], bundle_1.parts[1][2] = got_1, got_2
    input_grad, d_taps, gain_first_grad, shift_first_grad = call(
        functools.partial(first_back_kernel, frames),
        [wide_f32, ((rows, 3 * narrow), BF16), ((1, narrow), F32), ((1, narrow), F32)],
        (scalars,), sums, stats_1, gain_1, d_act_1, pre_1, place, near, d_before, d_after,
        pre_before, pre_after, time_weight, d_summed,
        scratch=[pltpu.VMEM((rows, narrow), F32), pltpu.VMEM((rows, narrow), F32)],
        flops=6 * rows * narrow * channels,
    )

    bundle_1.after([d_taps, d_taps])
    bundle_2.add(
        time_grads_kernel, bundle_2.cut, 3 * deep * narrow // LANE, inputs, d_taps,
        flops=6 * rows * narrow * channels,
    )
    bundle_2.begin()
    bundle_1.more()
    bundle_2.plane()
    bundle_2.turn()
    bundle_1.layer()
    bundle_2.more(last=False)
    bundle_1.got = bundle_2.hold(bundle_1.got)
    bundle_2.turn()
    bundle_1.exchange()
    bundle_2.layer()
    bundle_2.got, bundle_1.other = tie(bundle_2.got, bundle_1.other)
    bundle_2.exchange()
    bundle_1.finish()
    bundle_2.other, bundle_1.other = tie(bundle_2.other, bundle_1.other)
    bundle_2.finish()
    if deep == LANE:
        out_grad, query_grad, key_grad, value_grad = bundle_1.outs(
            attend_outs_kernel, [(inner, deep)] + [(deep, inner)] * 3
        )
        expand_grad, space_grad, time_grad = bundle_2.outs(
            bottleneck_outs_kernel, [(narrow, deep), (9, wide, narrow), (3, deep, narrow)]
        )
    else:

        def columns(share, start, height, width):
            part = share[start : start + height * width // LANE]
            return part.reshape(width // LANE, height, LANE).transpose(1, 0, 2).reshape(height, width)

        def folded(share, start, height, width):
            part = share[start : start + height * width // LANE]
            part = part.reshape(height // LANE, width, LANE // width, width)
            return part.transpose(0, 2, 1, 3).reshape(height, width)

        first, second = bundle_1.shares()
        out_grad = folded(first, 0, inner, deep)
        query_grad = columns(first, half, deep, inner)
        key_grad = columns(second, 0, deep, inner)
        value_grad = columns(second, half, deep, inner)
        first, second = bundle_2.shares()
        expand_grad = folded(first, 0, narrow, deep)
        space_grad = jnp.stack(
            [columns(first, expand_rows + tap * tap_rows, wide, narrow) for tap in range(9)]
        )
        time_all = columns(second, 0, deep, 3 * narrow)
        time_grad = jnp.stack([time_all[:, k * narrow : (k + 1) * narrow] for k in range(3)])
    return (
        output, input_grad, time_grad, gain_first_grad[0], shift_first_grad[0], space_grad,
        gain_second_grad[0], shift_second_grad[0], expand_grad, gain_third_grad[0], shift_third_grad[0],
        query_grad, key_grad, value_grad, out_grad, gain_final_grad[0], shift_final_grad[0],
    )


def solution(mesh):
    split = P(("pos", "grp"), None)
    in_specs = (split,) + (P(),) * 17 + (split,)
    out_specs = (
        split, split, P(None, "pos", None), P(), P(), P(None, "pos", None), P(), P(),
        P(None, "pos"), P(), P(), P("pos", None), P("pos", None), P("pos", None),
        P(None, "pos"), P(), P(),
    )
    return jax.shard_map(local, mesh=mesh, in_specs=in_specs, out_specs=out_specs, check_vma=False)
```

```python
import functools

import jax
import jax.numpy as jnp
import numpy as np
from jax import lax
from jax.experimental import pallas as pl
from jax.experimental.pallas import tpu as pltpu
from jax.sharding import PartitionSpec as P

SIDE = 14
HALF = SIDE // 2
AREA = SIDE * SIDE
LANE = 128
EDGE = 16
EPSILON = 1e-05
TEMPER = 0.2
MASKED_SCORE = -1000000000.0
PAD_SCORE = -2000000000.0
F32 = jnp.float32
BF16 = jnp.bfloat16
VMEM_BYTES = 60 * 1024 * 1024


def flip(count, bit):
    return [(i, i ^ bit) for i in range(count)]


def dot(left, right):
    return jnp.dot(left, right, preferred_element_type=F32)


def dot_rows(left, right):
    return lax.dot_general(left, right, (((0,), (0,)), ((), ())), preferred_element_type=F32)


def dot_cols(left, right):
    return lax.dot_general(left, right, (((1,), (1,)), ((), ())), preferred_element_type=F32)


def first_count():
    pos_count, grp_count = lax.axis_size("pos"), lax.axis_size("grp")
    return pos_count * grp_count if pos_count * grp_count <= 64 else pos_count


def trade(copies):
    pos_count, grp_count = lax.axis_size("pos"), lax.axis_size("grp")
    if pos_count * grp_count <= 64:
        return lax.all_to_all(copies, ("pos", "grp"), 0, 0, tiled=True)
    part = lax.all_to_all(copies, "pos", 0, 0, tiled=True).sum(0)
    copies = jnp.broadcast_to(part[None], (grp_count,) + part.shape)
    return lax.all_to_all(copies, "grp", 0, 0, tiled=True)


def tie(wanted, *others):
    return lax.optimization_barrier((wanted,) + others)


def call(kernel, outs, scalars, *arrays, scratch=(), flops=0):
    shapes = [jax.ShapeDtypeStruct(shape, kind) for shape, kind in outs]
    moved = sum(int(np.prod(s.shape)) * s.dtype.itemsize for s in shapes)
    moved += sum(a.size * a.dtype.itemsize for a in arrays)
    near = pl.BlockSpec(memory_space=pltpu.VMEM)
    return pl.pallas_call(
        kernel,
        out_shape=shapes,
        in_specs=[pl.BlockSpec(memory_space=pltpu.SMEM)] * len(scalars) + [near] * len(arrays),
        out_specs=[near] * len(shapes),
        scratch_shapes=list(scratch),
        compiler_params=pltpu.CompilerParams(vmem_limit_bytes=VMEM_BYTES),
        cost_estimate=pl.CostEstimate(flops=flops, bytes_accessed=moved, transcendentals=0),
    )(*scalars, *arrays)


def chunks(width, step=LANE):
    return [slice(start, start + step) for start in range(0, width, step)]


def emit(copies_ref, start, value):
    count, _, width = copies_ref.shape
    for k in range(0, value.shape[1], LANE):
        row, lane = divmod(start + k, width)
        copies_ref[:, row : row + 1, lane : lane + LANE] = jnp.broadcast_to(
            value[None, :, k : k + LANE], (count, 1, LANE)
        )


def collect(copies_ref):
    return jnp.sum(copies_ref[...], axis=0)


def part(sums, start, size):
    width = sums.shape[1]
    pieces, end = [], start + size
    while start < end:
        row, lane = divmod(start, width)
        extent = min(width - lane, end - start)
        pieces.append(sums[row : row + 1, lane : lane + extent])
        start += extent
    return pieces[0] if len(pieces) == 1 else jnp.concatenate(pieces, axis=1)


def column_sum(value):
    return jnp.sum(value, axis=0, keepdims=True)


def project(vector, w):
    high = vector.astype(BF16).astype(F32)
    middle = (vector - high).astype(BF16).astype(F32)
    low = vector - high - middle
    blank = jnp.zeros((13, vector.shape[1]), F32)
    pieces = jnp.concatenate([high, middle, low, blank], axis=0).astype(BF16)
    return column_sum(dot(pieces, w[...]))


def moments_of(values, squares, total):
    mean = values / total
    return mean, lax.rsqrt(squares / total - mean * mean + EPSILON)


def silu_grad(pre_act, gradient):
    sig = jax.nn.sigmoid(pre_act)
    return gradient * sig * (1.0 + pre_act * (1.0 - sig))


def back_terms(gain, mean, inv, gain_grad, shift_grad, total):
    d_spread = -0.5 * gain * gain_grad * inv * inv
    d_mean = -gain * shift_grad * inv - 2.0 * mean * d_spread
    return gain * inv, d_mean / total, 2.0 * d_spread / total


def pack_rows(value, rows, packed):
    for k, c in enumerate(chunks(value.shape[1])):
        packed[k * rows : (k + 1) * rows, :] = value[0:rows, c]


def unpack_rows(packed, rows, size, k):
    return packed[k * rows : k * rows + size, :]


def border_kernel(x, w, tap_0, tap_2, up, down):
    rows = x.shape[0]
    tap_0[...] = dot(x[...], w[0])
    up[...] = tap_0[rows - AREA : rows, :]
    tap_2[...] = dot(x[...], w[2])
    down[...] = tap_2[0:AREA, :]


def first_kernel(frames, sc, tap_0, tap_1, tap_2, place, before, after, pre, copies, last, first):
    for t in range(frames):
        here = slice(t * AREA, (t + 1) * AREA)
        prev = before[...] if t == 0 else tap_0[(t - 1) * AREA : t * AREA, :]
        following = after[...] if t == frames - 1 else tap_2[(t + 1) * AREA : (t + 2) * AREA, :]
        pre[here, :] = tap_1[here, :] + sc[1 + t] * prev + sc[1 + frames + t] * following
    last[...] = pre[(frames - 1) * AREA : frames * AREA, :].astype(BF16)
    first[...] = pre[0:AREA, :].astype(BF16)
    width = pre.shape[1]
    valid = place[:, 0:1]
    for c in chunks(width):
        hidden = pre[:, c]
        masked = hidden * valid
        emit(copies, c.start, column_sum(masked))
        emit(copies, width + c.start, column_sum(masked * hidden))


def inside(place, down, right):
    y = place[:, 2:3] + float(down)
    x = place[:, 1:2] + float(right)
    top = float(SIDE - 1)
    ok = (y >= 0.0) & (y <= top) & (x >= 0.0) & (x <= top)
    return ok.astype(F32)


def fill_padded(padded, value):
    rows, width = value.shape
    padded[0:EDGE, :] = jnp.zeros((EDGE, width), F32)
    padded[EDGE + rows : 2 * EDGE + rows, :] = jnp.zeros((EDGE, width), F32)
    padded[EDGE : EDGE + rows, :] = value


def second_kernel(sc, copies_in, pre_1, gain, shift, place, w, pre_2, windows, copies, stats, padded):
    rows, width = pre_1.shape
    total = sc[0]
    sums = collect(copies_in)
    mean, inv = moments_of(part(sums, 0, width), part(sums, width, width), total)
    stats[0:1, :] = mean
    stats[1:2, :] = inv
    act = (pre_1[...] - mean) * inv * gain[...] + shift[...]
    fill_padded(padded, (act * jax.nn.sigmoid(act)).astype(BF16).astype(F32))
    for tap in range(9):
        down, right = tap // 3 - 1, tap % 3 - 1
        start = EDGE + down * SIDE + right
        window = padded[start : start + rows, :]
        if tap != 4:
            window = window * inside(place, down, right)
        windows[:, tap * width : (tap + 1) * width] = window.astype(BF16)
    pre_2[...] = dot(windows[...], w[...])
    valid = place[:, 0:1]
    for c in chunks(width):
        hidden = pre_2[:, c]
        masked = hidden * valid
        emit(copies, c.start, column_sum(masked))
        emit(copies, width + c.start, column_sum(masked * hidden))


def third_kernel(sc, copies_in, pre_2, gain, shift, place, w, z_2, pre_3, copies, stats):
    width = pre_2.shape[1]
    total = sc[0]
    sums = collect(copies_in)
    mean, inv = moments_of(part(sums, 0, width), part(sums, width, width), total)
    stats[0:1, :] = mean
    stats[1:2, :] = inv
    valid = place[:, 0:1]
    act = (pre_2[...] - mean) * inv * gain[...] + shift[...]
    z_2[...] = (act * jax.nn.sigmoid(act)).astype(BF16)
    emit(copies, 0, column_sum(z_2[...].astype(F32) * valid))
    for c in chunks(w.shape[1], 2 * LANE):
        hidden = dot(z_2[...], w[:, c])
        pre_3[:, c] = hidden
        emit(copies, width + c.start, column_sum(hidden * hidden * valid))


def unit_kernel(keys, sc, copies_in, w_expand, gain, shift, pre_3, x, pool, counts, w_key, w_value, unit, pooled, kv, stats, packed):
    total = sc[0]
    narrow, channels = w_expand.shape
    sums = collect(copies_in)
    mean, inv = moments_of(
        project(part(sums, 0, narrow), w_expand), part(sums, narrow, channels), total
    )
    stats[0:1, :] = mean
    stats[1:2, :] = inv
    blocks, inner = pool.shape[0], w_key.shape[1]
    for c in chunks(channels, 2 * LANE):
        scale = inv[:, c] * gain[:, c]
        summed = x[:, c].astype(F32) + (pre_3[:, c] - mean[:, c]) * scale + shift[:, c]
        unit[:, c] = (summed * jax.nn.sigmoid(summed)).astype(BF16)
        sums_here = dot(pool[...], unit[:, c])
        high = sums_here.astype(BF16)
        pooled[0:blocks, c] = high
        pooled[blocks : 2 * blocks, c] = (sums_here - high.astype(F32)).astype(BF16)
    many = jnp.maximum(counts[:, 0:1], 1.0)
    for k, w in enumerate((w_key, w_value)):
        for c in chunks(inner, 2 * LANE):
            both = dot(pooled[...], w[:, c])
            start = (k * inner + c.start) // LANE * keys
            pack_rows((both[:blocks] + both[blocks:]) / many, keys, packed.at[start : start + 2 * keys])
    kv[...] = packed[...].astype(BF16)


def attend_kernel(slots, keys, sc, theta, place, key_row, w, cot, *refs):
    blocks = refs[:slots]
    kv, probs, attended, pre_4, copies, packed = refs[slots:]
    inner, channels = w.shape
    size, lines = kv.shape[0] // slots, blocks[0].shape[0]
    packed[lines:, :] = jnp.zeros((packed.shape[0] - lines, LANE), F32)
    for k in range(slots):
        packed[0:lines, :] = blocks[k][...].astype(F32)
        for j, c in enumerate(chunks(2 * inner)):
            kv[k * size : (k + 1) * size, c] = unpack_rows(packed, keys, size, j).astype(BF16)
    logits = dot_cols(theta[...], kv[:, 0:inner])
    allowed = place[:, 3:4] == key_row[0:1, :]
    scores = jnp.where(allowed, logits * TEMPER, key_row[1:2, :])
    exponent = jnp.exp(scores - jnp.max(scores, axis=1, keepdims=True))
    weights = exponent / jnp.sum(exponent, axis=1, keepdims=True)
    probs[...] = weights
    attended[...] = dot(weights.astype(BF16), kv[:, inner:]).astype(BF16)
    valid = place[:, 0:1]
    emit(copies, 0, column_sum(attended[...].astype(F32) * valid))
    for c in chunks(channels, 2 * LANE):
        hidden = dot(attended[...], w[:, c])
        pre_4[:, c] = hidden
        emit(copies, inner + c.start, column_sum(hidden * hidden * valid))
        emit(copies, inner + channels + c.start, column_sum(cot[:, c].astype(F32) * hidden))


def attend_back_kernel(slots, keys, sc, copies_in, shift_copies, gain, place, key_row, w, pre_4, cot, kv, probs, theta, d_final, d_logits, mean_out, inv_out, gain_out, shift_out, own, *refs):
    sent, packed = refs[:-1], refs[-1]
    total = sc[0]
    inner, channels = w.shape
    size = own.shape[0]
    sums = collect(copies_in)
    mean, inv = moments_of(
        project(part(sums, 0, inner), w), part(sums, inner, channels), total
    )
    shift_grad = part(collect(shift_copies), 0, channels)
    gain_grad = inv * (part(sums, inner + channels, channels) - mean * shift_grad)
    mean_out[...] = mean
    inv_out[...] = inv
    gain_out[...] = gain_grad
    shift_out[...] = shift_grad
    scale, base, slope = back_terms(gain[...], mean, inv, gain_grad, shift_grad, total)
    valid = place[:, 0:1]
    for c in chunks(channels, 2 * LANE):
        d_final[:, c] = (
            cot[:, c].astype(F32) * scale[:, c]
            + valid * (base[:, c] + pre_4[:, c] * slope[:, c])
        ).astype(BF16)
    d_attended = dot_cols(d_final[...], w[...]).astype(BF16)
    d_probs = dot_cols(d_attended, kv[:, inner:])
    weights = probs[...]
    row_terms = jnp.sum(weights * d_probs, axis=1, keepdims=True)
    allowed = place[:, 3:4] == key_row[0:1, :]
    d_scores = jnp.where(allowed, TEMPER * weights * (d_probs - row_terms), 0.0)
    d_logits[...] = d_scores.astype(BF16)
    d_values = dot_rows(weights.astype(BF16), d_attended)
    d_keys = dot_rows(d_logits[...], theta[...])
    own[:, 0:inner] = d_keys[0:size]
    own[:, inner:] = d_values[0:size]
    for k in range(1, slots):
        here = slice(k * size, (k + 1) * size)
        half = inner // LANE * keys
        pack_rows(d_keys[here], keys, packed.at[0:half])
        pack_rows(d_values[here], keys, packed.at[half : 2 * half])
        sent[k - 1][...] = packed[...].astype(BF16)


def summed_back_kernel(slots, keys, sc, own, counts, w_key, w_value, stats_3, gain, shift, spread, d_unit_part, pre_3, x, *refs):
    received = refs[: slots - 1]
    d_pooled, d_summed, copies, stacked, packed, low = refs[slots - 1 :]
    size, inner = own.shape[0], w_key.shape[1]
    channels = x.shape[1]
    many = jnp.maximum(counts[:, 0:1], 1.0)
    lines = received[0].shape[0]
    others = received[0][...].astype(F32)
    for other in received[1:]:
        others = others + other[...].astype(F32)
    packed[0:lines, :] = others
    packed[lines:, :] = jnp.zeros((packed.shape[0] - lines, LANE), F32)
    for k, c in enumerate(chunks(2 * inner)):
        low[:, c] = ((own[:, c] + unpack_rows(packed, keys, size, k)) / many).astype(BF16)
    d_pooled[0:size, :] = low[...]
    d_pooled[size : 2 * size, :] = low[...]
    mean, inv = stats_3[0:1, :], stats_3[1:2, :]
    for c in chunks(channels, 2 * LANE):
        here = dot_cols(low[:, 0:inner], w_key[c, :]) + dot_cols(low[:, inner:], w_value[c, :])
        high = here.astype(BF16)
        stacked[0:size, c] = high
        stacked[size : 2 * size, c] = (here - high.astype(F32)).astype(BF16)
        d_unit = d_unit_part[:, c] + dot(spread[...], stacked[:, c])
        normed = (pre_3[:, c] - mean[:, c]) * inv[:, c]
        summed = x[:, c].astype(F32) + normed * gain[:, c] + shift[:, c]
        d_here = silu_grad(summed, d_unit)
        d_summed[:, c] = d_here
        emit(copies, c.start, column_sum(d_here * normed))
        emit(copies, channels + c.start, column_sum(d_here))


def third_back_kernel(sc, copies_in, stats_3, gain_3, place, d_summed, pre_3, w, pre_2, stats_2, gain_2, shift_2, d_third, d_act, copies, gain_out, shift_out):
    total = sc[0]
    channels, width = pre_3.shape[1], pre_2.shape[1]
    sums = collect(copies_in)
    gain_grad, shift_grad = part(sums, 0, channels), part(sums, channels, channels)
    gain_out[...] = gain_grad
    shift_out[...] = shift_grad
    scale, base, slope = back_terms(
        gain_3[...], stats_3[0:1, :], stats_3[1:2, :], gain_grad, shift_grad, total
    )
    valid = place[:, 0:1]
    for c in chunks(channels, 2 * LANE):
        d_third[:, c] = (
            d_summed[:, c] * scale[:, c] + valid * (base[:, c] + pre_3[:, c] * slope[:, c])
        ).astype(BF16)
    d_z = dot_cols(d_third[...], w[...])
    normed = (pre_2[...] - stats_2[0:1, :]) * stats_2[1:2, :]
    d_here = silu_grad(normed * gain_2[...] + shift_2[...], d_z)
    d_act[...] = d_here
    emit(copies, 0, column_sum(d_here * normed))
    emit(copies, width, column_sum(d_here))


def second_back_kernel(frames, sc, copies_in, stats_2, gain_2, d_act_2, pre_2, place, w, pre_1, stats_1, gain_1, shift_1, d_second, d_act, copies, gain_out, shift_out, last, first, padded):
    total = sc[0]
    rows, width = pre_1.shape
    sums = collect(copies_in)
    gain_grad, shift_grad = part(sums, 0, width), part(sums, width, width)
    gain_out[...] = gain_grad
    shift_out[...] = shift_grad
    scale, base, slope = back_terms(
        gain_2[...], stats_2[0:1, :], stats_2[1:2, :], gain_grad, shift_grad, total
    )
    low = (d_act_2[...] * scale + place[:, 0:1] * (base + pre_2[...] * slope)).astype(BF16)
    d_second[...] = low
    fill_padded(padded, low.astype(F32))
    d_z = dot_cols(low, w[4])
    for tap in range(9):
        if tap == 4:
            continue
        down, right = 1 - tap // 3, 1 - tap % 3
        start = EDGE + down * SIDE + right
        window = padded[start : start + rows, :] * inside(place, down, right)
        d_z = d_z + dot_cols(window.astype(BF16), w[tap])
    normed = (pre_1[...] - stats_1[0:1, :]) * stats_1[1:2, :]
    d_here = silu_grad(normed * gain_1[...] + shift_1[...], d_z)
    d_act[...] = d_here
    last[...] = d_act[(frames - 1) * AREA : frames * AREA, :].astype(BF16)
    first[...] = d_act[0:AREA, :].astype(BF16)
    emit(copies, 0, column_sum(d_here * normed))
    emit(copies, width, column_sum(d_here))


def first_back_kernel(frames, sc, copies_in, stats_1, gain_1, d_act, pre_1, place, near, d_before, d_after, pre_before, pre_after, w, d_summed, input_grad, d_taps, gain_out, shift_out, whole, moved):
    total = sc[0]
    width = pre_1.shape[1]
    sums = collect(copies_in)
    gain_grad, shift_grad = part(sums, 0, width), part(sums, width, width)
    gain_out[...] = gain_grad
    shift_out[...] = shift_grad
    scale, base, slope = back_terms(
        gain_1[...], stats_1[0:1, :], stats_1[1:2, :], gain_grad, shift_grad, total
    )
    whole[...] = d_act[...] * scale + place[:, 0:1] * (base + pre_1[...] * slope)
    d_taps[:, width : 2 * width] = whole[...].astype(BF16)
    d_prev = d_before[...].astype(F32) * scale + near[:, 0:1] * (
        base + pre_before[...].astype(F32) * slope
    )
    d_next = d_after[...].astype(F32) * scale + near[:, 1:2] * (
        base + pre_after[...].astype(F32) * slope
    )
    for t in range(frames):
        here = slice(t * AREA, (t + 1) * AREA)
        ahead = d_next if t == frames - 1 else whole[(t + 1) * AREA : (t + 2) * AREA, :]
        moved[here, :] = ahead * sc[1 + frames + t]
    d_taps[:, 0:width] = moved[...].astype(BF16)
    for t in range(frames):
        here = slice(t * AREA, (t + 1) * AREA)
        behind = d_prev if t == 0 else whole[(t - 1) * AREA : t * AREA, :]
        moved[here, :] = behind * sc[1 + t]
    d_taps[:, 2 * width :] = moved[...].astype(BF16)
    for c in chunks(d_summed.shape[1], 2 * LANE):
        value = d_summed[:, c]
        for tap in range(3):
            value = value + dot_cols(d_taps[:, tap * width : (tap + 1) * width], w[tap, c, :])
        input_grad[:, c] = value


def put(both, part, start, value):
    rows = value.shape[0]
    for k, c in enumerate(chunks(value.shape[1])):
        both[part & 1, part >> 1, start + k * rows : start + (k + 1) * rows, :] = value[:, c]


def pack(both, part, start, value):
    wide = value.shape[1]
    fold = LANE // wide
    step = LANE // fold
    for k in range(fold):
        both[part & 1, part >> 1, start : start + step, k * wide : (k + 1) * wide] = value[
            k * step : (k + 1) * step, :
        ]


def split_out(mine, start, both, low, send, keep, sems):
    rows = low.shape[2]
    low[0] = both[mine].astype(BF16)
    kept = pltpu.make_async_copy(low.at[0], keep.at[:, start : start + rows], sems.at[0])
    kept.start()
    low[1] = both[1 - mine].astype(BF16)
    sent = pltpu.make_async_copy(low.at[1], send.at[:, start : start + rows], sems.at[1])
    sent.start()
    kept.wait()
    sent.wait()


def attend_grads_kernel(parts, start, bits, d_logits, cot, w, attended, d_final, unit, kv, send, keep, d_unit_part, d_theta, both, low, sems):
    inner, channels = attended.shape[1], unit.shape[1]
    d_theta[...] = dot(d_logits[...], kv[:, 0:inner]).astype(BF16)
    for c in chunks(channels, 2 * LANE):
        d_unit_part[:, c] = cot[:, c].astype(F32) + dot_cols(d_theta[...], w[c, :])
    wide = channels // parts
    for p in range(parts):
        here = slice(p * wide, (p + 1) * wide)
        put(both, p, inner * wide // LANE, dot_rows(unit[:, here], d_theta[...]))
    for c in chunks(inner):
        grad = dot_rows(attended[:, c], d_final[...])
        for p in range(parts):
            pack(both, p, c.start * wide // LANE, grad[:, p * wide : (p + 1) * wide])
    split_out(bits[0], start, both, low, send, keep, sems)


def pooled_grads_kernel(parts, start, bits, send_in, keep_in, pooled, d_pooled, send, keep, both, low, sems):
    wide = pooled.shape[1] // parts
    for p in range(parts):
        put(both, p, 0, dot_rows(pooled[:, p * wide : (p + 1) * wide], d_pooled[...]))
    split_out(bits[0], start, both, low, send, keep, sems)


def expand_grads_kernel(parts, start, bits, z_2, d_third, send, keep, both, low, sems):
    wide = d_third.shape[1] // parts
    for c in chunks(z_2.shape[1]):
        grad = dot_rows(z_2[:, c], d_third[...])
        for p in range(parts):
            pack(both, p, c.start * wide // LANE, grad[:, p * wide : (p + 1) * wide])
    split_out(bits[0], start, both, low, send, keep, sems)


def space_grads_kernel(parts, start, bits, send_in, keep_in, windows, d_second, send, keep, both, low, sems):
    width = d_second.shape[1]
    wide = width // parts
    for tap in range(9):
        grad = dot_rows(windows[:, tap * width : (tap + 1) * width], d_second[...])
        for p in range(parts):
            put(both, p, tap * wide * width // LANE, grad[p * wide : (p + 1) * wide, :])
    split_out(bits[0], start, both, low, send, keep, sems)


def time_grads_kernel(parts, start, bits, send_in, keep_in, x, d_taps, send, keep, both, low, sems):
    wide = x.shape[1] // parts
    for p in range(parts):
        put(both, p, 0, dot_rows(x[:, p * wide : (p + 1) * wide], d_taps[...]))
    split_out(bits[0], start, both, low, send, keep, sems)


def core_stage_kernel(cut, low_bit, high_bit, bits, keep_in, received, send_1, keep_1, send_2, keep_2):
    count = send_1.shape[0]
    rows = keep_in.shape[1]
    for send, keep, bit, here, low in (
        (send_1, keep_1, low_bit, slice(0, cut), True),
        (send_2, keep_2, high_bit, slice(cut, rows), False),
    ):
        mine = bits[bit]
        for i in range(count):
            at = 2 * i + mine if low else i + count * mine
            off = 2 * i + 1 - mine if low else i + count * (1 - mine)
            keep[i] = (keep_in[at, here, :].astype(F32) + received[at, here, :].astype(F32)).astype(BF16)
            send[i] = (keep_in[off, here, :].astype(F32) + received[off, here, :].astype(F32)).astype(BF16)


def plane_stage_kernel(low_bit, high_bit, bits, in_1, received_1, in_2, received_2, send_1, keep_1, send_2, keep_2):
    count = send_1.shape[0]
    for keep_in, received, send, keep, bit, low in (
        (in_1, received_1, send_1, keep_1, low_bit, True),
        (in_2, received_2, send_2, keep_2, high_bit, False),
    ):
        mine = bits[bit]
        for i in range(count):
            at = 2 * i + mine if low else i + count * mine
            off = 2 * i + 1 - mine if low else i + count * (1 - mine)
            keep[i] = (keep_in[at].astype(F32) + received[at].astype(F32)).astype(BF16)
            send[i] = (keep_in[off].astype(F32) + received[off].astype(F32)).astype(BF16)


def half_stage_kernel(bit, bits, keep_in, received, send, keep):
    mine = bits[bit]
    keep[0] = (keep_in[mine].astype(F32) + received[mine].astype(F32)).astype(BF16)
    send[0] = (keep_in[1 - mine].astype(F32) + received[1 - mine].astype(F32)).astype(BF16)


def unfold(part, start, out):
    rows = out.shape[0]
    for k, c in enumerate(chunks(out.shape[1])):
        out[:, c] = part[start + k * rows : start + (k + 1) * rows, :]


def attend_outs_kernel(bit, bits, mine, other, out_grad, query_grad, key_grad, value_grad, first, second):
    swap = bits[bit] == 1
    here, there = mine[0].astype(F32), other[0].astype(F32)
    first[...] = jnp.where(swap, there, here)
    second[...] = jnp.where(swap, here, there)
    unfold(first, 0, out_grad)
    unfold(first, out_grad.shape[0], query_grad)
    unfold(second, 0, key_grad)
    unfold(second, first.shape[0] // 2, value_grad)


def bottleneck_outs_kernel(bit, bits, mine, other, expand_grad, space_grad, time_grad, first, second):
    swap = bits[bit] == 1
    here, there = mine[0].astype(F32), other[0].astype(F32)
    first[...] = jnp.where(swap, there, here)
    second[...] = jnp.where(swap, here, there)
    unfold(first, 0, expand_grad)
    taps, deep, width = space_grad.shape
    for tap in range(taps):
        start = expand_grad.shape[0] + tap * deep * width // LANE
        for k, c in enumerate(chunks(width)):
            space_grad[tap, :, c] = first[start + k * deep : start + (k + 1) * deep, :]
    taps, deep, width = time_grad.shape
    for tap in range(taps):
        for k, c in enumerate(chunks(width)):
            start = (tap * width // LANE + k) * deep
            time_grad[tap, :, c] = second[start : start + deep, :]


class Bundle:
    def __init__(self, bits, cut):
        self.bits, self.cut = bits, cut
        self.pos_count, self.grp_count = lax.axis_size("pos"), lax.axis_size("grp")
        self.pos_bits = self.pos_count.bit_length() - 1
        self.grp_bits = self.grp_count.bit_length() - 1
        self.send = self.keep = None

    def add(self, kernel, start, rows, *arrays, extra=(), scratch=(), flops=0):
        whole = (self.pos_count // 2, 2 * self.cut, LANE)
        half = (self.pos_count // 2, rows, LANE)
        held = () if self.send is None else (self.send, self.keep)
        anywhere = pl.BlockSpec(memory_space=pl.ANY)
        inside_vmem = pl.BlockSpec(memory_space=pltpu.VMEM)
        shapes = [jax.ShapeDtypeStruct(whole, BF16)] * 2
        shapes += [jax.ShapeDtypeStruct(shape, kind) for shape, kind in extra]
        moved = sum(a.size * a.dtype.itemsize for a in arrays) + 6 * int(np.prod(half))
        self.send, self.keep, *rest = pl.pallas_call(
            functools.partial(kernel, self.pos_count, start),
            out_shape=shapes,
            in_specs=[pl.BlockSpec(memory_space=pltpu.SMEM)]
            + [anywhere] * len(held)
            + [inside_vmem] * len(arrays),
            out_specs=[anywhere, anywhere] + [inside_vmem] * len(extra),
            scratch_shapes=[
                pltpu.VMEM((2,) + half, F32), pltpu.VMEM((2,) + half, BF16),
                pltpu.SemaphoreType.DMA((2,)),
            ]
            + list(scratch),
            input_output_aliases={1: 0, 2: 1} if held else {},
            compiler_params=pltpu.CompilerParams(vmem_limit_bytes=VMEM_BYTES),
            cost_estimate=pl.CostEstimate(flops=flops, bytes_accessed=moved, transcendentals=0),
        )(self.bits, *held, *arrays)
        return rest

    def begin(self):
        self.received = lax.ppermute(self.send, "pos", flip(self.pos_count, 1))

    def plane(self):
        count = self.pos_count // 4
        bits = (1, self.pos_bits - 1)
        outs = []
        for rows in (self.cut, self.cut):
            outs += [((count, rows, LANE), BF16)] * 2
        outs = call(
            functools.partial(core_stage_kernel, self.cut, *bits), outs, (self.bits,),
            self.keep, self.received,
        )
        self.parts = [list(outs[:2]), list(outs[2:])]
        self.pair = bits

    def turn(self):
        for k in range(2):
            pairs = flip(self.pos_count, 1 << self.pair[k])
            self.parts[k].append(lax.ppermute(self.parts[k][0], "pos", pairs))

    def hold(self, value):
        value, self.parts[0][0], self.parts[1][0] = tie(
            value, self.parts[0][0], self.parts[1][0]
        )
        return value

    def more(self, last=True):
        while self.parts[0][1].shape[0] > 1:
            count = self.parts[0][1].shape[0] // 2
            self.pair = (self.pair[0] + 1, self.pair[1] - 1)
            outs = [((count, self.cut, LANE), BF16)] * 4
            (_, keep_1, got_1), (_, keep_2, got_2) = self.parts
            outs = call(
                functools.partial(plane_stage_kernel, *self.pair), outs, (self.bits,),
                keep_1, got_1, keep_2, got_2,
            )
            self.parts = [list(outs[:2]), list(outs[2:])]
            if self.parts[0][1].shape[0] > 1 or last:
                self.turn()

    def after(self, others):
        for k, other in enumerate(others):
            self.parts[k][2], _ = tie(self.parts[k][2], other)

    def layer(self):
        (_, keep_1, got_1), (_, keep_2, got_2) = self.parts
        first = keep_1.astype(F32) + got_1.astype(F32)
        second = keep_2.astype(F32) + got_2.astype(F32)
        swap = self.bits[self.pos_bits] == 1
        keep = jnp.where(swap, second, first).astype(BF16)
        send = jnp.where(swap, first, second).astype(BF16)
        self.keep = keep
        self.got = lax.ppermute(send, "grp", flip(self.grp_count, 1))

    def exchange(self):
        keep, got = self.keep, self.got
        for bit in range(1, self.grp_bits - 1):
            shape = (2, keep.shape[1] // 2, LANE)
            half = (1,) + shape[1:]
            send, keep = call(
                functools.partial(half_stage_kernel, self.pos_bits + bit),
                [(half, BF16), (half, BF16)], (self.bits,), keep.reshape(shape), got.reshape(shape),
            )
            got = lax.ppermute(send, "grp", flip(self.grp_count, 1 << bit))
        self.low = (keep.astype(F32) + got.astype(F32)).astype(BF16)
        self.other = lax.ppermute(self.low, "grp", flip(self.grp_count, self.grp_count // 2))

    def finish(self):
        final = (self.low.astype(F32) + self.other.astype(F32)).astype(BF16)
        for bit in reversed(range(1, self.grp_bits - 1)):
            mine = self.bits[self.pos_bits + bit]
            other = lax.ppermute(final, "grp", flip(self.grp_count, 1 << bit))
            lower = jnp.where(mine == 0, final, other)
            upper = jnp.where(mine == 0, other, final)
            final = jnp.concatenate([lower, upper], axis=1)
        self.mine = final
        self.other = lax.ppermute(final, "grp", flip(self.grp_count, 1))

    def outs(self, kernel, shapes):
        part = pltpu.VMEM((self.cut, LANE), F32)
        return call(
            functools.partial(kernel, self.pos_bits), [(shape, F32) for shape in shapes],
            (self.bits,), self.mine, self.other, scratch=[part, part],
        )

    def shares(self):
        swap = self.bits[self.pos_bits] == 1
        first = jnp.where(swap, self.other, self.mine)[0].astype(F32)
        second = jnp.where(swap, self.mine, self.other)[0].astype(F32)
        return first, second


def local(
    inputs, segment_ids, pad_mask, time_weight, gain_first, shift_first, space_weight, gain_second,
    shift_second, expand_weight, gain_third, shift_third, query_weight, key_weight, value_weight,
    out_weight, gain_final, shift_final, cotangent,
):
    rows, channels = inputs.shape
    frames = rows // AREA
    narrow = time_weight.shape[2]
    inner = query_weight.shape[1]
    pos_count, grp_count = lax.axis_size("pos"), lax.axis_size("grp")
    group_frames = frames * grp_count
    layer, block = lax.axis_index("grp"), lax.axis_index("pos")
    up = [(i, i + 1) for i in range(grp_count - 1)]
    down = [(i + 1, i) for i in range(grp_count - 1)]
    copies = first_count()
    own_keys = frames * HALF * HALF
    size = -(-own_keys // 16) * 16
    row = lambda v: v.reshape(1, -1)
    deep, wide = channels // pos_count, narrow // pos_count
    bits = jnp.stack(
        [(block >> k) & 1 for k in range(pos_count.bit_length() - 1)]
        + [(layer >> k) & 1 for k in range(grp_count.bit_length() - 1)]
    ).astype(jnp.int32)
    gain_1, shift_1, gain_2, shift_2 = map(row, (gain_first, shift_first, gain_second, shift_second))
    gain_3, shift_3, gain_4 = map(row, (gain_third, shift_third, gain_final))

    seg_group = lax.dynamic_slice_in_dim(segment_ids, block * group_frames, group_frames)
    border = jnp.full((1,), -1, jnp.int32)
    seg_padded = jnp.concatenate([border, seg_group, border])
    seg_own = lax.dynamic_slice_in_dim(seg_padded, layer * frames + 1, frames)
    seg_before = lax.dynamic_slice_in_dim(seg_padded, layer * frames, frames)
    seg_after = lax.dynamic_slice_in_dim(seg_padded, layer * frames + 2, frames)
    total = jnp.sum(pad_mask.astype(F32))
    scalars = jnp.concatenate(
        [total[None], (seg_before == seg_own).astype(F32), (seg_after == seg_own).astype(F32)]
    )
    start = (block * grp_count + layer) * rows
    valid = lax.dynamic_slice_in_dim(pad_mask, start, rows).astype(F32)
    spot = np.arange(rows)
    place = jnp.stack(
        [
            valid,
            jnp.asarray(spot % SIDE, F32),
            jnp.asarray(spot % AREA // SIDE, F32),
            jnp.broadcast_to(seg_own[:, None], (frames, AREA)).reshape(rows).astype(F32),
        ],
        axis=1,
    )
    near_start = jnp.stack([jnp.maximum(start - AREA, 0), start + rows])
    near = jnp.stack(
        [lax.dynamic_slice_in_dim(pad_mask, near_start[k], AREA) for k in range(2)], axis=1
    ).astype(F32)
    owner = (spot // AREA) * HALF * HALF + (spot % AREA // SIDE // 2) * HALF + spot % SIDE // 2
    member = np.zeros((size, rows), np.float32)
    member[owner, spot] = 1.0
    pool = (jnp.asarray(member) * valid[None, :]).astype(BF16)
    half_spread = (jnp.asarray(member.T.copy()) * valid[:, None]).astype(BF16)
    spread = jnp.concatenate([half_spread, half_spread], axis=1)
    mask_group = lax.dynamic_slice_in_dim(
        pad_mask, block * group_frames * AREA, group_frames * AREA
    ).astype(F32)
    key_counts = jnp.sum(
        mask_group.reshape(grp_count, frames, HALF, 2, HALF, 2), axis=(3, 5)
    ).reshape(grp_count, own_keys)
    key_seg = jnp.broadcast_to(
        seg_group.reshape(grp_count, frames, 1), (grp_count, frames, HALF * HALF)
    ).reshape(grp_count, own_keys)
    key_seg = jnp.where(key_counts > 0.5, key_seg.astype(F32), -1.0)
    key_seg = jnp.pad(key_seg, ((0, 0), (0, size - own_keys)), constant_values=-1.0)
    order = layer ^ np.arange(grp_count)
    floor = np.full((grp_count, size), MASKED_SCORE, np.float32)
    floor[:, own_keys:] = PAD_SCORE
    key_row = jnp.stack([key_seg[order].reshape(-1), jnp.asarray(floor.reshape(-1))])
    counts = jnp.pad(
        lax.dynamic_index_in_dim(key_counts, layer, 0, False), (0, size - own_keys)
    )[:, None]

    narrow_f32 = ((rows, narrow), F32)
    wide_f32 = ((rows, channels), F32)
    wide_bf16 = ((rows, channels), BF16)
    frame_f32 = ((AREA, narrow), F32)
    frame_bf16 = ((AREA, narrow), BF16)

    small = (copies, 2, narrow)
    shift_sums = jnp.sum(cotangent.astype(F32), axis=0).reshape(1, 2, channels // 2)
    shift_sums = jnp.broadcast_to(shift_sums, (copies, 2, channels // 2))
    tap_0, tap_2, to_next, to_prev = call(
        border_kernel, [narrow_f32, narrow_f32, frame_f32, frame_f32], (),
        inputs, time_weight,
        flops=4 * rows * channels * narrow,
    )
    before = lax.ppermute(to_next, "grp", up)
    after = lax.ppermute(to_prev, "grp", down)
    tap_1 = dot(inputs, time_weight[1])
    pre_1, sums, last, first = call(
        functools.partial(first_kernel, frames),
        [narrow_f32, (small, F32), frame_bf16, frame_bf16],
        (scalars,), tap_0, tap_1, tap_2, place, before, after,
    )
    sums = trade(sums)
    pre_before = lax.ppermute(last, "grp", up)
    pre_after = lax.ppermute(first, "grp", down)
    pre_2, windows, sums, stats_1 = call(
        second_kernel,
        [narrow_f32, ((rows, 9 * narrow), BF16), (small, F32), ((2, narrow), F32)],
        (scalars,), sums, pre_1, gain_1, shift_1, place,
        space_weight.reshape(9 * narrow, narrow),
        scratch=[pltpu.VMEM((rows + 2 * EDGE, narrow), F32)],
        flops=18 * rows * narrow * narrow,
    )
    sums = trade(sums)
    sums, pre_before, pre_after = tie(sums, pre_before, pre_after)
    z_2, pre_3, sums, stats_2 = call(
        third_kernel,
        [
            ((rows, narrow), BF16), wide_f32, ((copies, 2, (narrow + channels) // 2), F32),
            ((2, narrow), F32),
        ],
        (scalars,), sums, pre_2, gain_2, shift_2, place, expand_weight,
        flops=2 * rows * narrow * channels,
    )
    sums = trade(sums)
    lines = own_keys * 2 * inner // LANE
    packed_bf16 = ((lines, LANE), BF16)
    unit, pooled, kv_own, stats_3 = call(
        functools.partial(unit_kernel, own_keys),
        [wide_bf16, ((2 * size, channels), BF16), packed_bf16, ((2, channels), F32)],
        (scalars,), sums, expand_weight, gain_3, shift_3, pre_3, inputs, pool, counts,
        key_weight, value_weight,
        scratch=[pltpu.VMEM((lines, LANE), F32)],
        flops=2 * size * channels * (rows + 4 * inner),
    )
    shift_sums, _ = tie(shift_sums, kv_own)
    shift_sums = trade(shift_sums)
    kv = [kv_own] + [
        lax.ppermute(kv_own, "grp", flip(grp_count, step)) for step in range(1, grp_count)
    ]
    theta = dot(unit, query_weight).astype(BF16)
    kv_all, probs, attended, pre_4, sums = call(
        functools.partial(attend_kernel, grp_count, own_keys),
        [
            ((grp_count * size, 2 * inner), BF16), ((rows, grp_count * size), F32), ((rows, inner), BF16), wide_f32,
            ((copies, 4, (inner + 2 * channels) // 4), F32),
        ],
        (scalars,), theta, place, key_row, out_weight, cotangent, *kv,
        scratch=[pltpu.VMEM((lines + 16, LANE), F32)],
        flops=2 * rows * inner * (2 * grp_count * size + channels),
    )
    sums = trade(sums)

    d_final, d_logits, mean_4, inv_4, gain_final_grad, shift_final_grad, d_kv, *d_sent = call(
        functools.partial(attend_back_kernel, grp_count, own_keys),
        [
            wide_bf16, ((rows, grp_count * size), BF16),
        ]
        + [((1, channels), F32)] * 4
        + [((size, 2 * inner), F32)]
        + [packed_bf16] * (grp_count - 1),
        (scalars,), sums, shift_sums, gain_4, place, key_row, out_weight, pre_4,
        cotangent, kv_all, probs, theta,
        scratch=[pltpu.VMEM((lines, LANE), F32)],
        flops=2 * rows * inner * (3 * grp_count * size + channels),
    )
    d_received = [
        lax.ppermute(d_sent[step - 1], "grp", flip(grp_count, step)) for step in range(1, grp_count)
    ]
    output = (
        unit.astype(F32)
        + (pre_4 - mean_4) * inv_4 * gain_final
        + shift_final
    ).astype(BF16)
    half = deep * inner // LANE
    bundle_1 = Bundle(bits, 2 * half)
    d_unit_part, _ = bundle_1.add(
        attend_grads_kernel, 0, 2 * half,
        d_logits, cotangent, query_weight, attended, d_final, unit, kv_all,
        extra=[wide_f32, ((rows, inner), BF16)],
        flops=2 * rows * inner * (grp_count * size + 3 * channels),
    )
    d_pooled, d_summed, sums = call(
        functools.partial(summed_back_kernel, grp_count, own_keys),
        [((2 * size, 2 * inner), BF16), wide_f32, ((copies, 8, channels // 4), F32)],
        (scalars,), d_kv, counts, key_weight, value_weight, stats_3, gain_3,
        shift_3, spread, d_unit_part, pre_3, inputs, *d_received,
        scratch=[
            pltpu.VMEM((2 * size, channels), BF16), pltpu.VMEM((lines + 16, LANE), F32),
            pltpu.VMEM((size, 2 * inner), BF16),
        ],
        flops=4 * size * channels * (inner + rows),
    )
    sums = trade(sums)
    bundle_1.add(
        pooled_grads_kernel, 2 * half, 2 * half, pooled, d_pooled,
        flops=8 * size * channels * inner,
    )
    sums, bundle_1.send = tie(sums, bundle_1.send)
    bundle_1.begin()
    d_third, d_act_2, sums, gain_third_grad, shift_third_grad = call(
        third_back_kernel,
        [wide_bf16, narrow_f32, (small, F32), ((1, channels), F32), ((1, channels), F32)],
        (scalars,), sums, stats_3, gain_3, place, d_summed, pre_3, expand_weight,
        pre_2, stats_2, gain_2, shift_2,
        flops=2 * rows * narrow * channels,
    )
    sums, bundle_1.received = tie(sums, bundle_1.received)
    sums = trade(sums)
    tap_rows = wide * narrow // LANE
    expand_rows = narrow * deep // LANE
    bundle_2 = Bundle(bits, expand_rows + 9 * tap_rows)
    bundle_2.add(
        expand_grads_kernel, 0, expand_rows, z_2, d_third,
        flops=2 * rows * narrow * channels,
    )
    bundle_1.plane()
    sums, _ = tie(sums, bundle_2.send)
    sums = bundle_1.hold(sums)
    bundle_1.turn()
    d_second, d_act_1, sums, gain_second_grad, shift_second_grad, last, first = call(
        functools.partial(second_back_kernel, frames),
        [
            ((rows, narrow), BF16), narrow_f32, (small, F32), ((1, narrow), F32), ((1, narrow), F32),
            frame_bf16, frame_bf16,
        ],
        (scalars,), sums, stats_2, gain_2, d_act_2, pre_2, place, space_weight, pre_1, stats_1,
        gain_1, shift_1,
        scratch=[pltpu.VMEM((rows + 2 * EDGE, narrow), F32)],
        flops=18 * rows * narrow * narrow,
    )
    sums = trade(sums)
    d_before = lax.ppermute(last, "grp", up)
    d_after = lax.ppermute(first, "grp", down)
    bundle_2.add(
        space_grads_kernel, expand_rows, 9 * tap_rows, windows, d_second,
        flops=18 * rows * narrow * narrow,
    )
    (_, _, got_1), (_, _, got_2) = bundle_1.parts
    sums, bundle_2.send, got_1, got_2 = tie(sums, bundle_2.send, got_1, got_2)
    bundle_1.parts[0][2], bundle_1.parts[1][2] = got_1, got_2
    input_grad, d_taps, gain_first_grad, shift_first_grad = call(
        functools.partial(first_back_kernel, frames),
        [wide_f32, ((rows, 3 * narrow), BF16), ((1, narrow), F32), ((1, narrow), F32)],
        (scalars,), sums, stats_1, gain_1, d_act_1, pre_1, place, near, d_before, d_after,
        pre_before, pre_after, time_weight, d_summed,
        scratch=[pltpu.VMEM((rows, narrow), F32), pltpu.VMEM((rows, narrow), F32)],
        flops=6 * rows * narrow * channels,
    )

    bundle_1.after([d_taps, d_taps])
    bundle_2.add(
        time_grads_kernel, bundle_2.cut, 3 * deep * narrow // LANE, inputs, d_taps,
        flops=6 * rows * narrow * channels,
    )
    bundle_2.begin()
    bundle_1.more()
    bundle_2.plane()
    bundle_2.turn()
    bundle_1.layer()
    bundle_2.more(last=False)
    bundle_1.got = bundle_2.hold(bundle_1.got)
    bundle_2.turn()
    bundle_1.exchange()
    bundle_2.layer()
    bundle_2.got, bundle_1.other = tie(bundle_2.got, bundle_1.other)
    bundle_2.exchange()
    bundle_1.finish()
    bundle_2.other, bundle_1.other = tie(bundle_2.other, bundle_1.other)
    bundle_2.finish()
    if deep == LANE:
        out_grad, query_grad, key_grad, value_grad = bundle_1.outs(
            attend_outs_kernel, [(inner, deep)] + [(deep, inner)] * 3
        )
        expand_grad, space_grad, time_grad = bundle_2.outs(
            bottleneck_outs_kernel, [(narrow, deep), (9, wide, narrow), (3, deep, narrow)]
        )
    else:

        def columns(share, start, height, width):
            part = share[start : start + height * width // LANE]
            return part.reshape(width // LANE, height, LANE).transpose(1, 0, 2).reshape(height, width)

        def folded(share, start, height, width):
            part = share[start : start + height * width // LANE]
            part = part.reshape(height // LANE, width, LANE // width, width)
            return part.transpose(0, 2, 1, 3).reshape(height, width)

        first, second = bundle_1.shares()
        out_grad = folded(first, 0, inner, deep)
        query_grad = columns(first, half, deep, inner)
        key_grad = columns(second, 0, deep, inner)
        value_grad = columns(second, half, deep, inner)
        first, second = bundle_2.shares()
        expand_grad = folded(first, 0, narrow, deep)
        space_grad = jnp.stack(
            [columns(first, expand_rows + tap * tap_rows, wide, narrow) for tap in range(9)]
        )
        time_all = columns(second, 0, deep, 3 * narrow)
        time_grad = jnp.stack([time_all[:, k * narrow : (k + 1) * narrow] for k in range(3)])
    return (
        output, input_grad, time_grad, gain_first_grad[0], shift_first_grad[0], space_grad,
        gain_second_grad[0], shift_second_grad[0], expand_grad, gain_third_grad[0], shift_third_grad[0],
        query_grad, key_grad, value_grad, out_grad, gain_final_grad[0], shift_final_grad[0],
    )


def solution(mesh):
    split = P(("pos", "grp"), None)
    in_specs = (split,) + (P(),) * 17 + (split,)
    out_specs = (
        split, split, P(None, "pos", None), P(), P(), P(None, "pos", None), P(), P(),
        P(None, "pos"), P(), P(), P("pos", None), P("pos", None), P("pos", None),
        P(None, "pos"), P(), P(),
    )
    return jax.shard_map(local, mesh=mesh, in_specs=in_specs, out_specs=out_specs, check_vma=False)
```

```python
import functools

import jax
import jax.numpy as jnp
import numpy as np
from jax import lax
from jax.experimental import pallas as pl
from jax.experimental.pallas import tpu as pltpu
from jax.sharding import PartitionSpec as P

SIDE = 14
HALF = SIDE // 2
AREA = SIDE * SIDE
LANE = 128
EDGE = 16
EPSILON = 1e-05
TEMPER = 0.2
MASKED_SCORE = -1000000000.0
PAD_SCORE = -2000000000.0
F32 = jnp.float32
BF16 = jnp.bfloat16
VMEM_BYTES = 60 * 1024 * 1024


def flip(count, bit):
    return [(i, i ^ bit) for i in range(count)]


def dot(left, right):
    return jnp.dot(left, right, preferred_element_type=F32)


def dot_rows(left, right):
    return lax.dot_general(left, right, (((0,), (0,)), ((), ())), preferred_element_type=F32)


def dot_cols(left, right):
    return lax.dot_general(left, right, (((1,), (1,)), ((), ())), preferred_element_type=F32)


def first_count():
    pos_count, grp_count = lax.axis_size("pos"), lax.axis_size("grp")
    return pos_count * grp_count if pos_count * grp_count <= 64 else pos_count


def trade(copies):
    pos_count, grp_count = lax.axis_size("pos"), lax.axis_size("grp")
    if pos_count * grp_count <= 64:
        return lax.all_to_all(copies, ("pos", "grp"), 0, 0, tiled=True)
    part = lax.all_to_all(copies, "pos", 0, 0, tiled=True).sum(0)
    copies = jnp.broadcast_to(part[None], (grp_count,) + part.shape)
    return lax.all_to_all(copies, "grp", 0, 0, tiled=True)


def tie(wanted, *others):
    return lax.optimization_barrier((wanted,) + others)


def call(kernel, outs, scalars, *arrays, scratch=(), flops=0):
    shapes = [jax.ShapeDtypeStruct(shape, kind) for shape, kind in outs]
    moved = sum(int(np.prod(s.shape)) * s.dtype.itemsize for s in shapes)
    moved += sum(a.size * a.dtype.itemsize for a in arrays)
    near = pl.BlockSpec(memory_space=pltpu.VMEM)
    return pl.pallas_call(
        kernel,
        out_shape=shapes,
        in_specs=[pl.BlockSpec(memory_space=pltpu.SMEM)] * len(scalars) + [near] * len(arrays),
        out_specs=[near] * len(shapes),
        scratch_shapes=list(scratch),
        compiler_params=pltpu.CompilerParams(vmem_limit_bytes=VMEM_BYTES),
        cost_estimate=pl.CostEstimate(flops=flops, bytes_accessed=moved, transcendentals=0),
    )(*scalars, *arrays)


def chunks(width, step=LANE):
    return [slice(start, start + step) for start in range(0, width, step)]


def emit(copies_ref, start, value):
    count, _, width = copies_ref.shape
    for k in range(0, value.shape[1], LANE):
        row, lane = divmod(start + k, width)
        copies_ref[:, row : row + 1, lane : lane + LANE] = jnp.broadcast_to(
            value[None, :, k : k + LANE], (count, 1, LANE)
        )


def collect(copies_ref):
    return jnp.sum(copies_ref[...], axis=0)


def part(sums, start, size):
    width = sums.shape[1]
    pieces, end = [], start + size
    while start < end:
        row, lane = divmod(start, width)
        extent = min(width - lane, end - start)
        pieces.append(sums[row : row + 1, lane : lane + extent])
        start += extent
    return pieces[0] if len(pieces) == 1 else jnp.concatenate(pieces, axis=1)


def column_sum(value):
    return jnp.sum(value, axis=0, keepdims=True)


def project(vector, w):
    high = vector.astype(BF16).astype(F32)
    middle = (vector - high).astype(BF16).astype(F32)
    low = vector - high - middle
    blank = jnp.zeros((13, vector.shape[1]), F32)
    pieces = jnp.concatenate([high, middle, low, blank], axis=0).astype(BF16)
    return column_sum(dot(pieces, w[...]))


def moments_of(values, squares, total):
    mean = values / total
    return mean, lax.rsqrt(squares / total - mean * mean + EPSILON)


def silu_grad(pre_act, gradient):
    sig = jax.nn.sigmoid(pre_act)
    return gradient * sig * (1.0 + pre_act * (1.0 - sig))


def back_terms(gain, mean, inv, gain_grad, shift_grad, total):
    d_spread = -0.5 * gain * gain_grad * inv * inv
    d_mean = -gain * shift_grad * inv - 2.0 * mean * d_spread
    return gain * inv, d_mean / total, 2.0 * d_spread / total


def pack_rows(value, rows, packed):
    for k, c in enumerate(chunks(value.shape[1])):
        packed[k * rows : (k + 1) * rows, :] = value[0:rows, c]


def unpack_rows(packed, rows, size, k):
    return packed[k * rows : k * rows + size, :]


def border_kernel(x, w, tap_0, tap_2, up, down):
    rows = x.shape[0]
    tap_0[...] = dot(x[...], w[0])
    up[...] = tap_0[rows - AREA : rows, :]
    tap_2[...] = dot(x[...], w[2])
    down[...] = tap_2[0:AREA, :]


def first_kernel(frames, sc, tap_0, tap_1, tap_2, place, before, after, pre, copies, last, first):
    for t in range(frames):
        here = slice(t * AREA, (t + 1) * AREA)
        prev = before[...] if t == 0 else tap_0[(t - 1) * AREA : t * AREA, :]
        following = after[...] if t == frames - 1 else tap_2[(t + 1) * AREA : (t + 2) * AREA, :]
        pre[here, :] = tap_1[here, :] + sc[1 + t] * prev + sc[1 + frames + t] * following
    last[...] = pre[(frames - 1) * AREA : frames * AREA, :].astype(BF16)
    first[...] = pre[0:AREA, :].astype(BF16)
    width = pre.shape[1]
    valid = place[:, 0:1]
    for c in chunks(width):
        hidden = pre[:, c]
        masked = hidden * valid
        emit(copies, c.start, column_sum(masked))
        emit(copies, width + c.start, column_sum(masked * hidden))


def inside(place, down, right):
    y = place[:, 2:3] + float(down)
    x = place[:, 1:2] + float(right)
    top = float(SIDE - 1)
    ok = (y >= 0.0) & (y <= top) & (x >= 0.0) & (x <= top)
    return ok.astype(F32)


def fill_padded(padded, value):
    rows, width = value.shape
    padded[0:EDGE, :] = jnp.zeros((EDGE, width), F32)
    padded[EDGE + rows : 2 * EDGE + rows, :] = jnp.zeros((EDGE, width), F32)
    padded[EDGE : EDGE + rows, :] = value


def second_kernel(sc, copies_in, pre_1, gain, shift, place, w, pre_2, windows, copies, stats, padded):
    rows, width = pre_1.shape
    total = sc[0]
    sums = collect(copies_in)
    mean, inv = moments_of(part(sums, 0, width), part(sums, width, width), total)
    stats[0:1, :] = mean
    stats[1:2, :] = inv
    act = (pre_1[...] - mean) * inv * gain[...] + shift[...]
    fill_padded(padded, (act * jax.nn.sigmoid(act)).astype(BF16).astype(F32))
    for tap in range(9):
        down, right = tap // 3 - 1, tap % 3 - 1
        start = EDGE + down * SIDE + right
        window = padded[start : start + rows, :]
        if tap != 4:
            window = window * inside(place, down, right)
        windows[:, tap * width : (tap + 1) * width] = window.astype(BF16)
    pre_2[...] = dot(windows[...], w[...])
    valid = place[:, 0:1]
    for c in chunks(width):
        hidden = pre_2[:, c]
        masked = hidden * valid
        emit(copies, c.start, column_sum(masked))
        emit(copies, width + c.start, column_sum(masked * hidden))


def third_kernel(sc, copies_in, pre_2, gain, shift, place, w, z_2, pre_3, copies, stats):
    width = pre_2.shape[1]
    total = sc[0]
    sums = collect(copies_in)
    mean, inv = moments_of(part(sums, 0, width), part(sums, width, width), total)
    stats[0:1, :] = mean
    stats[1:2, :] = inv
    valid = place[:, 0:1]
    act = (pre_2[...] - mean) * inv * gain[...] + shift[...]
    z_2[...] = (act * jax.nn.sigmoid(act)).astype(BF16)
    emit(copies, 0, column_sum(z_2[...].astype(F32) * valid))
    for c in chunks(w.shape[1], 2 * LANE):
        hidden = dot(z_2[...], w[:, c])
        pre_3[:, c] = hidden
        emit(copies, width + c.start, column_sum(hidden * hidden * valid))


def unit_kernel(keys, sc, copies_in, w_expand, gain, shift, pre_3, x, pool, counts, w_key, w_value, unit, pooled, kv, stats, packed):
    total = sc[0]
    narrow, channels = w_expand.shape
    sums = collect(copies_in)
    mean, inv = moments_of(
        project(part(sums, 0, narrow), w_expand), part(sums, narrow, channels), total
    )
    stats[0:1, :] = mean
    stats[1:2, :] = inv
    blocks, inner = pool.shape[0], w_key.shape[1]
    for c in chunks(channels, 2 * LANE):
        scale = inv[:, c] * gain[:, c]
        summed = x[:, c].astype(F32) + (pre_3[:, c] - mean[:, c]) * scale + shift[:, c]
        unit[:, c] = (summed * jax.nn.sigmoid(summed)).astype(BF16)
        sums_here = dot(pool[...], unit[:, c])
        high = sums_here.astype(BF16)
        pooled[0:blocks, c] = high
        pooled[blocks : 2 * blocks, c] = (sums_here - high.astype(F32)).astype(BF16)
    many = jnp.maximum(counts[:, 0:1], 1.0)
    for k, w in enumerate((w_key, w_value)):
        for c in chunks(inner, 2 * LANE):
            both = dot(pooled[...], w[:, c])
            start = (k * inner + c.start) // LANE * keys
            pack_rows((both[:blocks] + both[blocks:]) / many, keys, packed.at[start : start + 2 * keys])
    kv[...] = packed[...].astype(BF16)


def attend_kernel(slots, keys, sc, theta, place, key_row, w, cot, *refs):
    blocks = refs[:slots]
    kv, probs, attended, pre_4, copies, packed = refs[slots:]
    inner, channels = w.shape
    size, lines = kv.shape[0] // slots, blocks[0].shape[0]
    packed[lines:, :] = jnp.zeros((packed.shape[0] - lines, LANE), F32)
    for k in range(slots):
        packed[0:lines, :] = blocks[k][...].astype(F32)
        for j, c in enumerate(chunks(2 * inner)):
            kv[k * size : (k + 1) * size, c] = unpack_rows(packed, keys, size, j).astype(BF16)
    logits = dot_cols(theta[...], kv[:, 0:inner])
    allowed = place[:, 3:4] == key_row[0:1, :]
    scores = jnp.where(allowed, logits * TEMPER, key_row[1:2, :])
    exponent = jnp.exp(scores - jnp.max(scores, axis=1, keepdims=True))
    weights = exponent / jnp.sum(exponent, axis=1, keepdims=True)
    probs[...] = weights
    attended[...] = dot(weights.astype(BF16), kv[:, inner:]).astype(BF16)
    valid = place[:, 0:1]
    emit(copies, 0, column_sum(attended[...].astype(F32) * valid))
    for c in chunks(channels, 2 * LANE):
        hidden = dot(attended[...], w[:, c])
        pre_4[:, c] = hidden
        emit(copies, inner + c.start, column_sum(hidden * hidden * valid))
        emit(copies, inner + channels + c.start, column_sum(cot[:, c].astype(F32) * hidden))


def attend_back_kernel(slots, keys, sc, copies_in, shift_copies, gain, place, key_row, w, pre_4, cot, kv, probs, theta, d_final, d_logits, mean_out, inv_out, gain_out, shift_out, own, *refs):
    sent, packed = refs[:-1], refs[-1]
    total = sc[0]
    inner, channels = w.shape
    size = own.shape[0]
    sums = collect(copies_in)
    mean, inv = moments_of(
        project(part(sums, 0, inner), w), part(sums, inner, channels), total
    )
    shift_grad = part(collect(shift_copies), 0, channels)
    gain_grad = inv * (part(sums, inner + channels, channels) - mean * shift_grad)
    mean_out[...] = mean
    inv_out[...] = inv
    gain_out[...] = gain_grad
    shift_out[...] = shift_grad
    scale, base, slope = back_terms(gain[...], mean, inv, gain_grad, shift_grad, total)
    valid = place[:, 0:1]
    for c in chunks(channels, 2 * LANE):
        d_final[:, c] = (
            cot[:, c].astype(F32) * scale[:, c]
            + valid * (base[:, c] + pre_4[:, c] * slope[:, c])
        ).astype(BF16)
    d_attended = dot_cols(d_final[...], w[...]).astype(BF16)
    d_probs = dot_cols(d_attended, kv[:, inner:])
    weights = probs[...]
    row_terms = jnp.sum(weights * d_probs, axis=1, keepdims=True)
    allowed = place[:, 3:4] == key_row[0:1, :]
    d_scores = jnp.where(allowed, TEMPER * weights * (d_probs - row_terms), 0.0)
    d_logits[...] = d_scores.astype(BF16)
    d_values = dot_rows(weights.astype(BF16), d_attended)
    d_keys = dot_rows(d_logits[...], theta[...])
    own[:, 0:inner] = d_keys[0:size]
    own[:, inner:] = d_values[0:size]
    for k in range(1, slots):
        here = slice(k * size, (k + 1) * size)
        half = inner // LANE * keys
        pack_rows(d_keys[here], keys, packed.at[0:half])
        pack_rows(d_values[here], keys, packed.at[half : 2 * half])
        sent[k - 1][...] = packed[...].astype(BF16)


def summed_back_kernel(slots, keys, sc, own, counts, w_key, w_value, stats_3, gain, shift, spread, d_unit_part, pre_3, x, *refs):
    received = refs[: slots - 1]
    d_pooled, d_summed, copies, stacked, packed, low = refs[slots - 1 :]
    size, inner = own.shape[0], w_key.shape[1]
    channels = x.shape[1]
    many = jnp.maximum(counts[:, 0:1], 1.0)
    lines = received[0].shape[0]
    others = received[0][...].astype(F32)
    for other in received[1:]:
        others = others + other[...].astype(F32)
    packed[0:lines, :] = others
    packed[lines:, :] = jnp.zeros((packed.shape[0] - lines, LANE), F32)
    for k, c in enumerate(chunks(2 * inner)):
        low[:, c] = ((own[:, c] + unpack_rows(packed, keys, size, k)) / many).astype(BF16)
    d_pooled[0:size, :] = low[...]
    d_pooled[size : 2 * size, :] = low[...]
    mean, inv = stats_3[0:1, :], stats_3[1:2, :]
    for c in chunks(channels, 2 * LANE):
        here = dot_cols(low[:, 0:inner], w_key[c, :]) + dot_cols(low[:, inner:], w_value[c, :])
        high = here.astype(BF16)
        stacked[0:size, c] = high
        stacked[size : 2 * size, c] = (here - high.astype(F32)).astype(BF16)
        d_unit = d_unit_part[:, c] + dot(spread[...], stacked[:, c])
        normed = (pre_3[:, c] - mean[:, c]) * inv[:, c]
        summed = x[:, c].astype(F32) + normed * gain[:, c] + shift[:, c]
        d_here = silu_grad(summed, d_unit)
        d_summed[:, c] = d_here
        emit(copies, c.start, column_sum(d_here * normed))
        emit(copies, channels + c.start, column_sum(d_here))


def third_back_kernel(sc, copies_in, stats_3, gain_3, place, d_summed, pre_3, w, pre_2, stats_2, gain_2, shift_2, d_third, d_act, copies, gain_out, shift_out):
    total = sc[0]
    channels, width = pre_3.shape[1], pre_2.shape[1]
    sums = collect(copies_in)
    gain_grad, shift_grad = part(sums, 0, channels), part(sums, channels, channels)
    gain_out[...] = gain_grad
    shift_out[...] = shift_grad
    scale, base, slope = back_terms(
        gain_3[...], stats_3[0:1, :], stats_3[1:2, :], gain_grad, shift_grad, total
    )
    valid = place[:, 0:1]
    for c in chunks(channels, 2 * LANE):
        d_third[:, c] = (
            d_summed[:, c] * scale[:, c] + valid * (base[:, c] + pre_3[:, c] * slope[:, c])
        ).astype(BF16)
    d_z = dot_cols(d_third[...], w[...])
    normed = (pre_2[...] - stats_2[0:1, :]) * stats_2[1:2, :]
    d_here = silu_grad(normed * gain_2[...] + shift_2[...], d_z)
    d_act[...] = d_here
    emit(copies, 0, column_sum(d_here * normed))
    emit(copies, width, column_sum(d_here))


def second_back_kernel(frames, sc, copies_in, stats_2, gain_2, d_act_2, pre_2, place, w, pre_1, stats_1, gain_1, shift_1, d_second, d_act, copies, gain_out, shift_out, last, first, padded):
    total = sc[0]
    rows, width = pre_1.shape
    sums = collect(copies_in)
    gain_grad, shift_grad = part(sums, 0, width), part(sums, width, width)
    gain_out[...] = gain_grad
    shift_out[...] = shift_grad
    scale, base, slope = back_terms(
        gain_2[...], stats_2[0:1, :], stats_2[1:2, :], gain_grad, shift_grad, total
    )
    low = (d_act_2[...] * scale + place[:, 0:1] * (base + pre_2[...] * slope)).astype(BF16)
    d_second[...] = low
    fill_padded(padded, low.astype(F32))
    d_z = dot_cols(low, w[4])
    for tap in range(9):
        if tap == 4:
            continue
        down, right = 1 - tap // 3, 1 - tap % 3
        start = EDGE + down * SIDE + right
        window = padded[start : start + rows, :] * inside(place, down, right)
        d_z = d_z + dot_cols(window.astype(BF16), w[tap])
    normed = (pre_1[...] - stats_1[0:1, :]) * stats_1[1:2, :]
    d_here = silu_grad(normed * gain_1[...] + shift_1[...], d_z)
    d_act[...] = d_here
    last[...] = d_act[(frames - 1) * AREA : frames * AREA, :].astype(BF16)
    first[...] = d_act[0:AREA, :].astype(BF16)
    emit(copies, 0, column_sum(d_here * normed))
    emit(copies, width, column_sum(d_here))


def input_back_kernel(d_taps, w, d_summed, input_grad):
    width = w.shape[2]
    for c in chunks(d_summed.shape[1], 2 * LANE):
        value = d_summed[:, c]
        for tap in range(3):
            value = value + dot_cols(d_taps[:, tap * width : (tap + 1) * width], w[tap, c, :])
        input_grad[:, c] = value


def put(both, part, start, value):
    rows = value.shape[0]
    for k, c in enumerate(chunks(value.shape[1])):
        both[part & 1, part >> 1, start + k * rows : start + (k + 1) * rows, :] = value[:, c]


def pack(both, part, start, value):
    wide = value.shape[1]
    fold = LANE // wide
    step = LANE // fold
    for k in range(fold):
        both[part & 1, part >> 1, start : start + step, k * wide : (k + 1) * wide] = value[
            k * step : (k + 1) * step, :
        ]


def split_out(mine, start, both, low, send, keep, sems):
    rows = low.shape[2]
    low[0] = both[mine].astype(BF16)
    kept = pltpu.make_async_copy(low.at[0], keep.at[:, start : start + rows], sems.at[0])
    kept.start()
    low[1] = both[1 - mine].astype(BF16)
    sent = pltpu.make_async_copy(low.at[1], send.at[:, start : start + rows], sems.at[1])
    sent.start()
    kept.wait()
    sent.wait()


def attend_grads_kernel(parts, start, bits, d_logits, cot, w, attended, d_final, unit, kv, send, keep, d_unit_part, d_theta, both, low, sems):
    inner, channels = attended.shape[1], unit.shape[1]
    d_theta[...] = dot(d_logits[...], kv[:, 0:inner]).astype(BF16)
    for c in chunks(channels, 2 * LANE):
        d_unit_part[:, c] = cot[:, c].astype(F32) + dot_cols(d_theta[...], w[c, :])
    wide = channels // parts
    for p in range(parts):
        here = slice(p * wide, (p + 1) * wide)
        put(both, p, inner * wide // LANE, dot_rows(unit[:, here], d_theta[...]))
    for c in chunks(inner):
        grad = dot_rows(attended[:, c], d_final[...])
        for p in range(parts):
            pack(both, p, c.start * wide // LANE, grad[:, p * wide : (p + 1) * wide])
    split_out(bits[0], start, both, low, send, keep, sems)


def pooled_grads_kernel(parts, start, bits, send_in, keep_in, pooled, d_pooled, send, keep, both, low, sems):
    wide = pooled.shape[1] // parts
    for p in range(parts):
        put(both, p, 0, dot_rows(pooled[:, p * wide : (p + 1) * wide], d_pooled[...]))
    split_out(bits[0], start, both, low, send, keep, sems)


def expand_grads_kernel(parts, start, bits, z_2, d_third, send, keep, both, low, sems):
    wide = d_third.shape[1] // parts
    for c in chunks(z_2.shape[1]):
        grad = dot_rows(z_2[:, c], d_third[...])
        for p in range(parts):
            pack(both, p, c.start * wide // LANE, grad[:, p * wide : (p + 1) * wide])
    split_out(bits[0], start, both, low, send, keep, sems)


def space_grads_kernel(parts, start, bits, send_in, keep_in, windows, d_second, send, keep, both, low, sems):
    width = d_second.shape[1]
    wide = width // parts
    for tap in range(9):
        grad = dot_rows(windows[:, tap * width : (tap + 1) * width], d_second[...])
        for p in range(parts):
            put(both, p, tap * wide * width // LANE, grad[p * wide : (p + 1) * wide, :])
    split_out(bits[0], start, both, low, send, keep, sems)


def time_grads_kernel(frames, parts, start, bits, sc, send_in, keep_in, x, copies_in, stats_1, gain_1, d_act, pre_1, place, near, d_before, d_after, pre_before, pre_after, send, keep, d_taps, gain_out, shift_out, both, low, sems, whole, moved):
    total = sc[0]
    width = pre_1.shape[1]
    sums = collect(copies_in)
    gain_grad, shift_grad = part(sums, 0, width), part(sums, width, width)
    gain_out[...] = gain_grad
    shift_out[...] = shift_grad
    scale, base, slope = back_terms(
        gain_1[...], stats_1[0:1, :], stats_1[1:2, :], gain_grad, shift_grad, total
    )
    whole[...] = d_act[...] * scale + place[:, 0:1] * (base + pre_1[...] * slope)
    d_taps[:, width : 2 * width] = whole[...].astype(BF16)
    d_prev = d_before[...].astype(F32) * scale + near[:, 0:1] * (
        base + pre_before[...].astype(F32) * slope
    )
    d_next = d_after[...].astype(F32) * scale + near[:, 1:2] * (
        base + pre_after[...].astype(F32) * slope
    )
    for t in range(frames):
        here = slice(t * AREA, (t + 1) * AREA)
        ahead = d_next if t == frames - 1 else whole[(t + 1) * AREA : (t + 2) * AREA, :]
        moved[here, :] = ahead * sc[1 + frames + t]
    d_taps[:, 0:width] = moved[...].astype(BF16)
    for t in range(frames):
        here = slice(t * AREA, (t + 1) * AREA)
        behind = d_prev if t == 0 else whole[(t - 1) * AREA : t * AREA, :]
        moved[here, :] = behind * sc[1 + t]
    d_taps[:, 2 * width :] = moved[...].astype(BF16)
    wide = x.shape[1] // parts
    for p in range(parts):
        put(both, p, 0, dot_rows(x[:, p * wide : (p + 1) * wide], d_taps[...]))
    split_out(bits[0], start, both, low, send, keep, sems)


def core_stage_kernel(cut, low_bit, high_bit, bits, keep_in, received, send_1, keep_1, send_2, keep_2):
    count = send_1.shape[0]
    rows = keep_in.shape[1]
    for send, keep, bit, here, low in (
        (send_1, keep_1, low_bit, slice(0, cut), True),
        (send_2, keep_2, high_bit, slice(cut, rows), False),
    ):
        mine = bits[bit]
        for i in range(count):
            at = 2 * i + mine if low else i + count * mine
            off = 2 * i + 1 - mine if low else i + count * (1 - mine)
            keep[i] = (keep_in[at, here, :].astype(F32) + received[at, here, :].astype(F32)).astype(BF16)
            send[i] = (keep_in[off, here, :].astype(F32) + received[off, here, :].astype(F32)).astype(BF16)


def plane_stage_kernel(low_bit, high_bit, bits, in_1, received_1, in_2, received_2, send_1, keep_1, send_2, keep_2):
    count = send_1.shape[0]
    for keep_in, received, send, keep, bit, low in (
        (in_1, received_1, send_1, keep_1, low_bit, True),
        (in_2, received_2, send_2, keep_2, high_bit, False),
    ):
        mine = bits[bit]
        for i in range(count):
            at = 2 * i + mine if low else i + count * mine
            off = 2 * i + 1 - mine if low else i + count * (1 - mine)
            keep[i] = (keep_in[at].astype(F32) + received[at].astype(F32)).astype(BF16)
            send[i] = (keep_in[off].astype(F32) + received[off].astype(F32)).astype(BF16)


def half_stage_kernel(bit, bits, keep_in, received, send, keep):
    mine = bits[bit]
    keep[0] = (keep_in[mine].astype(F32) + received[mine].astype(F32)).astype(BF16)
    send[0] = (keep_in[1 - mine].astype(F32) + received[1 - mine].astype(F32)).astype(BF16)


def unfold(part, start, out):
    rows = out.shape[0]
    for k, c in enumerate(chunks(out.shape[1])):
        out[:, c] = part[start + k * rows : start + (k + 1) * rows, :]


def attend_outs_kernel(bit, bits, mine, other, out_grad, query_grad, key_grad, value_grad, both):
    swap = bits[bit] == 1
    here, there = mine[0].astype(F32), other[0].astype(F32)
    cut = here.shape[0]
    both[0:cut, :] = jnp.where(swap, there, here)
    both[cut : 2 * cut, :] = jnp.where(swap, here, there)
    unfold(both, 0, out_grad)
    unfold(both, cut // 2, query_grad)
    unfold(both, cut, key_grad)
    unfold(both, cut + cut // 2, value_grad)


def bottleneck_outs_kernel(bit, bits, mine, other, expand_grad, space_grad, time_grad, both):
    swap = bits[bit] == 1
    here, there = mine[0].astype(F32), other[0].astype(F32)
    cut = here.shape[0]
    both[0:cut, :] = jnp.where(swap, there, here)
    both[cut : 2 * cut, :] = jnp.where(swap, here, there)
    unfold(both, 0, expand_grad)
    start = expand_grad.shape[0]
    for grad in (space_grad, time_grad):
        taps, deep, width = grad.shape
        for tap in range(taps):
            for c in chunks(width):
                grad[tap, :, c] = both[start : start + deep, :]
                start += deep


class Bundle:
    def __init__(self, bits, cut):
        self.bits, self.cut = bits, cut
        self.pos_count, self.grp_count = lax.axis_size("pos"), lax.axis_size("grp")
        self.pos_bits = self.pos_count.bit_length() - 1
        self.grp_bits = self.grp_count.bit_length() - 1
        self.send = self.keep = None

    def add(self, kernel, start, rows, *arrays, extra=(), scratch=(), scalars=(), flops=0):
        whole = (self.pos_count // 2, 2 * self.cut, LANE)
        half = (self.pos_count // 2, rows, LANE)
        held = () if self.send is None else (self.send, self.keep)
        anywhere = pl.BlockSpec(memory_space=pl.ANY)
        inside_vmem = pl.BlockSpec(memory_space=pltpu.VMEM)
        shapes = [jax.ShapeDtypeStruct(whole, BF16)] * 2
        shapes += [jax.ShapeDtypeStruct(shape, kind) for shape, kind in extra]
        moved = sum(a.size * a.dtype.itemsize for a in arrays) + 6 * int(np.prod(half))
        self.send, self.keep, *rest = pl.pallas_call(
            functools.partial(kernel, self.pos_count, start),
            out_shape=shapes,
            in_specs=[pl.BlockSpec(memory_space=pltpu.SMEM)] * (1 + len(scalars))
            + [anywhere] * len(held)
            + [inside_vmem] * len(arrays),
            out_specs=[anywhere, anywhere] + [inside_vmem] * len(extra),
            scratch_shapes=[
                pltpu.VMEM((2,) + half, F32), pltpu.VMEM((2,) + half, BF16),
                pltpu.SemaphoreType.DMA((2,)),
            ]
            + list(scratch),
            input_output_aliases={1 + len(scalars): 0, 2 + len(scalars): 1} if held else {},
            compiler_params=pltpu.CompilerParams(vmem_limit_bytes=VMEM_BYTES),
            cost_estimate=pl.CostEstimate(flops=flops, bytes_accessed=moved, transcendentals=0),
        )(self.bits, *scalars, *held, *arrays)
        return rest

    def begin(self):
        self.received = lax.ppermute(self.send, "pos", flip(self.pos_count, 1))

    def plane(self):
        count = self.pos_count // 4
        bits = (1, self.pos_bits - 1)
        outs = []
        for rows in (self.cut, self.cut):
            outs += [((count, rows, LANE), BF16)] * 2
        outs = call(
            functools.partial(core_stage_kernel, self.cut, *bits), outs, (self.bits,),
            self.keep, self.received,
        )
        self.parts = [list(outs[:2]), list(outs[2:])]
        self.pair = bits

    def turn(self):
        for k in range(2):
            pairs = flip(self.pos_count, 1 << self.pair[k])
            self.parts[k].append(lax.ppermute(self.parts[k][0], "pos", pairs))

    def hold(self, value):
        value, self.parts[0][0], self.parts[1][0] = tie(
            value, self.parts[0][0], self.parts[1][0]
        )
        return value

    def more(self, last=True):
        while self.parts[0][1].shape[0] > 1:
            count = self.parts[0][1].shape[0] // 2
            self.pair = (self.pair[0] + 1, self.pair[1] - 1)
            outs = [((count, self.cut, LANE), BF16)] * 4
            (_, keep_1, got_1), (_, keep_2, got_2) = self.parts
            outs = call(
                functools.partial(plane_stage_kernel, *self.pair), outs, (self.bits,),
                keep_1, got_1, keep_2, got_2,
            )
            self.parts = [list(outs[:2]), list(outs[2:])]
            if self.parts[0][1].shape[0] > 1 or last:
                self.turn()

    def after(self, others):
        for k, other in enumerate(others):
            self.parts[k][2], _ = tie(self.parts[k][2], other)

    def layer(self):
        (_, keep_1, got_1), (_, keep_2, got_2) = self.parts
        first = keep_1.astype(F32) + got_1.astype(F32)
        second = keep_2.astype(F32) + got_2.astype(F32)
        swap = self.bits[self.pos_bits] == 1
        keep = jnp.where(swap, second, first).astype(BF16)
        send = jnp.where(swap, first, second).astype(BF16)
        self.keep = keep
        self.got = lax.ppermute(send, "grp", flip(self.grp_count, 1))

    def exchange(self):
        keep, got = self.keep, self.got
        for bit in range(1, self.grp_bits - 1):
            shape = (2, keep.shape[1] // 2, LANE)
            half = (1,) + shape[1:]
            send, keep = call(
                functools.partial(half_stage_kernel, self.pos_bits + bit),
                [(half, BF16), (half, BF16)], (self.bits,), keep.reshape(shape), got.reshape(shape),
            )
            got = lax.ppermute(send, "grp", flip(self.grp_count, 1 << bit))
        self.low = (keep.astype(F32) + got.astype(F32)).astype(BF16)
        self.other = lax.ppermute(self.low, "grp", flip(self.grp_count, self.grp_count // 2))

    def finish(self):
        final = (self.low.astype(F32) + self.other.astype(F32)).astype(BF16)
        for bit in reversed(range(1, self.grp_bits - 1)):
            mine = self.bits[self.pos_bits + bit]
            other = lax.ppermute(final, "grp", flip(self.grp_count, 1 << bit))
            lower = jnp.where(mine == 0, final, other)
            upper = jnp.where(mine == 0, other, final)
            final = jnp.concatenate([lower, upper], axis=1)
        self.mine = final
        self.other = lax.ppermute(final, "grp", flip(self.grp_count, 1))

    def outs(self, kernel, shapes):
        return call(
            functools.partial(kernel, self.pos_bits), [(shape, F32) for shape in shapes],
            (self.bits,), self.mine, self.other, scratch=[pltpu.VMEM((2 * self.cut, LANE), F32)],
        )

    def shares(self):
        swap = self.bits[self.pos_bits] == 1
        first = jnp.where(swap, self.other, self.mine)[0].astype(F32)
        second = jnp.where(swap, self.mine, self.other)[0].astype(F32)
        return first, second


def local(
    inputs, segment_ids, pad_mask, time_weight, gain_first, shift_first, space_weight, gain_second,
    shift_second, expand_weight, gain_third, shift_third, query_weight, key_weight, value_weight,
    out_weight, gain_final, shift_final, cotangent,
):
    rows, channels = inputs.shape
    frames = rows // AREA
    narrow = time_weight.shape[2]
    inner = query_weight.shape[1]
    pos_count, grp_count = lax.axis_size("pos"), lax.axis_size("grp")
    group_frames = frames * grp_count
    layer, block = lax.axis_index("grp"), lax.axis_index("pos")
    up = [(i, i + 1) for i in range(grp_count - 1)]
    down = [(i + 1, i) for i in range(grp_count - 1)]
    copies = first_count()
    own_keys = frames * HALF * HALF
    size = -(-own_keys // 16) * 16
    row = lambda v: v.reshape(1, -1)
    deep, wide = channels // pos_count, narrow // pos_count
    bits = jnp.stack(
        [(block >> k) & 1 for k in range(pos_count.bit_length() - 1)]
        + [(layer >> k) & 1 for k in range(grp_count.bit_length() - 1)]
    ).astype(jnp.int32)
    gain_1, shift_1, gain_2, shift_2 = map(row, (gain_first, shift_first, gain_second, shift_second))
    gain_3, shift_3, gain_4 = map(row, (gain_third, shift_third, gain_final))

    seg_group = lax.dynamic_slice_in_dim(segment_ids, block * group_frames, group_frames)
    border = jnp.full((1,), -1, jnp.int32)
    seg_padded = jnp.concatenate([border, seg_group, border])
    seg_own = lax.dynamic_slice_in_dim(seg_padded, layer * frames + 1, frames)
    seg_before = lax.dynamic_slice_in_dim(seg_padded, layer * frames, frames)
    seg_after = lax.dynamic_slice_in_dim(seg_padded, layer * frames + 2, frames)
    total = jnp.sum(pad_mask.astype(F32))
    scalars = jnp.concatenate(
        [total[None], (seg_before == seg_own).astype(F32), (seg_after == seg_own).astype(F32)]
    )
    start = (block * grp_count + layer) * rows
    valid = lax.dynamic_slice_in_dim(pad_mask, start, rows).astype(F32)
    spot = np.arange(rows)
    place = jnp.stack(
        [
            valid,
            jnp.asarray(spot % SIDE, F32),
            jnp.asarray(spot % AREA // SIDE, F32),
            jnp.broadcast_to(seg_own[:, None], (frames, AREA)).reshape(rows).astype(F32),
        ],
        axis=1,
    )
    near_start = jnp.stack([jnp.maximum(start - AREA, 0), start + rows])
    near = jnp.stack(
        [lax.dynamic_slice_in_dim(pad_mask, near_start[k], AREA) for k in range(2)], axis=1
    ).astype(F32)
    owner = (spot // AREA) * HALF * HALF + (spot % AREA // SIDE // 2) * HALF + spot % SIDE // 2
    member = np.zeros((size, rows), np.float32)
    member[owner, spot] = 1.0
    pool = (jnp.asarray(member) * valid[None, :]).astype(BF16)
    half_spread = (jnp.asarray(member.T.copy()) * valid[:, None]).astype(BF16)
    spread = jnp.concatenate([half_spread, half_spread], axis=1)
    mask_group = lax.dynamic_slice_in_dim(
        pad_mask, block * group_frames * AREA, group_frames * AREA
    ).astype(F32)
    key_counts = jnp.sum(
        mask_group.reshape(grp_count, frames, HALF, 2, HALF, 2), axis=(3, 5)
    ).reshape(grp_count, own_keys)
    key_seg = jnp.broadcast_to(
        seg_group.reshape(grp_count, frames, 1), (grp_count, frames, HALF * HALF)
    ).reshape(grp_count, own_keys)
    key_seg = jnp.where(key_counts > 0.5, key_seg.astype(F32), -1.0)
    key_seg = jnp.pad(key_seg, ((0, 0), (0, size - own_keys)), constant_values=-1.0)
    order = layer ^ np.arange(grp_count)
    floor = np.full((grp_count, size), MASKED_SCORE, np.float32)
    floor[:, own_keys:] = PAD_SCORE
    key_row = jnp.stack([key_seg[order].reshape(-1), jnp.asarray(floor.reshape(-1))])
    counts = jnp.pad(
        lax.dynamic_index_in_dim(key_counts, layer, 0, False), (0, size - own_keys)
    )[:, None]

    narrow_f32 = ((rows, narrow), F32)
    wide_f32 = ((rows, channels), F32)
    wide_bf16 = ((rows, channels), BF16)
    frame_f32 = ((AREA, narrow), F32)
    frame_bf16 = ((AREA, narrow), BF16)

    small = (copies, 2, narrow)
    shift_sums = jnp.sum(cotangent.astype(F32), axis=0).reshape(1, 2, channels // 2)
    shift_sums = jnp.broadcast_to(shift_sums, (copies, 2, channels // 2))
    tap_0, tap_2, to_next, to_prev = call(
        border_kernel, [narrow_f32, narrow_f32, frame_f32, frame_f32], (),
        inputs, time_weight,
        flops=4 * rows * channels * narrow,
    )
    before = lax.ppermute(to_next, "grp", up)
    after = lax.ppermute(to_prev, "grp", down)
    tap_1 = dot(inputs, time_weight[1])
    pre_1, sums, last, first = call(
        functools.partial(first_kernel, frames),
        [narrow_f32, (small, F32), frame_bf16, frame_bf16],
        (scalars,), tap_0, tap_1, tap_2, place, before, after,
    )
    sums = trade(sums)
    pre_before = lax.ppermute(last, "grp", up)
    pre_after = lax.ppermute(first, "grp", down)
    pre_2, windows, sums, stats_1 = call(
        second_kernel,
        [narrow_f32, ((rows, 9 * narrow), BF16), (small, F32), ((2, narrow), F32)],
        (scalars,), sums, pre_1, gain_1, shift_1, place,
        space_weight.reshape(9 * narrow, narrow),
        scratch=[pltpu.VMEM((rows + 2 * EDGE, narrow), F32)],
        flops=18 * rows * narrow * narrow,
    )
    sums = trade(sums)
    sums, pre_before, pre_after = tie(sums, pre_before, pre_after)
    z_2, pre_3, sums, stats_2 = call(
        third_kernel,
        [
            ((rows, narrow), BF16), wide_f32, ((copies, 2, (narrow + channels) // 2), F32),
            ((2, narrow), F32),
        ],
        (scalars,), sums, pre_2, gain_2, shift_2, place, expand_weight,
        flops=2 * rows * narrow * channels,
    )
    sums = trade(sums)
    lines = own_keys * 2 * inner // LANE
    packed_bf16 = ((lines, LANE), BF16)
    unit, pooled, kv_own, stats_3 = call(
        functools.partial(unit_kernel, own_keys),
        [wide_bf16, ((2 * size, channels), BF16), packed_bf16, ((2, channels), F32)],
        (scalars,), sums, expand_weight, gain_3, shift_3, pre_3, inputs, pool, counts,
        key_weight, value_weight,
        scratch=[pltpu.VMEM((lines, LANE), F32)],
        flops=2 * size * channels * (rows + 4 * inner),
    )
    shift_sums, _ = tie(shift_sums, kv_own)
    shift_sums = trade(shift_sums)
    kv = [kv_own] + [
        lax.ppermute(kv_own, "grp", flip(grp_count, step)) for step in range(1, grp_count)
    ]
    theta = dot(unit, query_weight).astype(BF16)
    kv_all, probs, attended, pre_4, sums = call(
        functools.partial(attend_kernel, grp_count, own_keys),
        [
            ((grp_count * size, 2 * inner), BF16), ((rows, grp_count * size), F32), ((rows, inner), BF16), wide_f32,
            ((copies, 4, (inner + 2 * channels) // 4), F32),
        ],
        (scalars,), theta, place, key_row, out_weight, cotangent, *kv,
        scratch=[pltpu.VMEM((lines + 16, LANE), F32)],
        flops=2 * rows * inner * (2 * grp_count * size + channels),
    )
    sums = trade(sums)

    d_final, d_logits, mean_4, inv_4, gain_final_grad, shift_final_grad, d_kv, *d_sent = call(
        functools.partial(attend_back_kernel, grp_count, own_keys),
        [
            wide_bf16, ((rows, grp_count * size), BF16),
        ]
        + [((1, channels), F32)] * 4
        + [((size, 2 * inner), F32)]
        + [packed_bf16] * (grp_count - 1),
        (scalars,), sums, shift_sums, gain_4, place, key_row, out_weight, pre_4,
        cotangent, kv_all, probs, theta,
        scratch=[pltpu.VMEM((lines, LANE), F32)],
        flops=2 * rows * inner * (3 * grp_count * size + channels),
    )
    d_received = [
        lax.ppermute(d_sent[step - 1], "grp", flip(grp_count, step)) for step in range(1, grp_count)
    ]
    output = (
        unit.astype(F32)
        + (pre_4 - mean_4) * inv_4 * gain_final
        + shift_final
    ).astype(BF16)
    half = deep * inner // LANE
    bundle_1 = Bundle(bits, 2 * half)
    d_unit_part, _ = bundle_1.add(
        attend_grads_kernel, 0, 2 * half,
        d_logits, cotangent, query_weight, attended, d_final, unit, kv_all,
        extra=[wide_f32, ((rows, inner), BF16)],
        flops=2 * rows * inner * (grp_count * size + 3 * channels),
    )
    d_pooled, d_summed, sums = call(
        functools.partial(summed_back_kernel, grp_count, own_keys),
        [((2 * size, 2 * inner), BF16), wide_f32, ((copies, 8, channels // 4), F32)],
        (scalars,), d_kv, counts, key_weight, value_weight, stats_3, gain_3,
        shift_3, spread, d_unit_part, pre_3, inputs, *d_received,
        scratch=[
            pltpu.VMEM((2 * size, channels), BF16), pltpu.VMEM((lines + 16, LANE), F32),
            pltpu.VMEM((size, 2 * inner), BF16),
        ],
        flops=4 * size * channels * (inner + rows),
    )
    sums = trade(sums)
    bundle_1.add(
        pooled_grads_kernel, 2 * half, 2 * half, pooled, d_pooled,
        flops=8 * size * channels * inner,
    )
    sums, bundle_1.send = tie(sums, bundle_1.send)
    bundle_1.begin()
    d_third, d_act_2, sums, gain_third_grad, shift_third_grad = call(
        third_back_kernel,
        [wide_bf16, narrow_f32, (small, F32), ((1, channels), F32), ((1, channels), F32)],
        (scalars,), sums, stats_3, gain_3, place, d_summed, pre_3, expand_weight,
        pre_2, stats_2, gain_2, shift_2,
        flops=2 * rows * narrow * channels,
    )
    sums, bundle_1.received = tie(sums, bundle_1.received)
    sums = trade(sums)
    tap_rows = wide * narrow // LANE
    expand_rows = narrow * deep // LANE
    time_start = expand_rows + 9 * tap_rows
    cut = -(-(time_start + 3 * deep * narrow // LANE) // 32) * 16
    bundle_2 = Bundle(bits, cut)
    bundle_2.add(
        expand_grads_kernel, 0, expand_rows, z_2, d_third,
        flops=2 * rows * narrow * channels,
    )
    bundle_1.plane()
    sums, _ = tie(sums, bundle_2.send)
    sums = bundle_1.hold(sums)
    bundle_1.turn()
    d_second, d_act_1, sums, gain_second_grad, shift_second_grad, last, first = call(
        functools.partial(second_back_kernel, frames),
        [
            ((rows, narrow), BF16), narrow_f32, (small, F32), ((1, narrow), F32), ((1, narrow), F32),
            frame_bf16, frame_bf16,
        ],
        (scalars,), sums, stats_2, gain_2, d_act_2, pre_2, place, space_weight, pre_1, stats_1,
        gain_1, shift_1,
        scratch=[pltpu.VMEM((rows + 2 * EDGE, narrow), F32)],
        flops=18 * rows * narrow * narrow,
    )
    sums = trade(sums)
    d_before = lax.ppermute(last, "grp", up)
    d_after = lax.ppermute(first, "grp", down)
    bundle_2.add(
        space_grads_kernel, expand_rows, 9 * tap_rows, windows, d_second,
        flops=18 * rows * narrow * narrow,
    )
    (_, _, got_1), (_, _, got_2) = bundle_1.parts
    sums, bundle_2.send, got_1, got_2 = tie(sums, bundle_2.send, got_1, got_2)
    bundle_1.parts[0][2], bundle_1.parts[1][2] = got_1, got_2
    d_taps, gain_first_grad, shift_first_grad = bundle_2.add(
        functools.partial(time_grads_kernel, frames), time_start, 3 * deep * narrow // LANE,
        inputs, sums, stats_1, gain_1, d_act_1, pre_1, place, near, d_before, d_after,
        pre_before, pre_after,
        extra=[((rows, 3 * narrow), BF16), ((1, narrow), F32), ((1, narrow), F32)],
        scratch=[pltpu.VMEM((rows, narrow), F32), pltpu.VMEM((rows, narrow), F32)],
        scalars=(scalars,),
        flops=6 * rows * narrow * channels,
    )

    bundle_1.after([d_taps, d_taps])
    bundle_2.begin()
    bundle_1.more()
    bundle_2.plane()
    bundle_2.turn()
    d_taps, _ = tie(d_taps, bundle_2.parts[0][1])
    (input_grad,) = call(
        input_back_kernel, [wide_f32], (), d_taps, time_weight, d_summed,
        flops=6 * rows * narrow * channels,
    )
    bundle_1.layer()
    bundle_2.after([input_grad])
    bundle_2.more(last=False)
    bundle_1.got = bundle_2.hold(bundle_1.got)
    bundle_2.turn()
    bundle_1.exchange()
    bundle_2.layer()
    bundle_2.got, bundle_1.other = tie(bundle_2.got, bundle_1.other)
    bundle_2.exchange()
    bundle_1.finish()
    bundle_2.other, bundle_1.other = tie(bundle_2.other, bundle_1.other)
    bundle_2.finish()
    if deep == LANE:
        out_grad, query_grad, key_grad, value_grad = bundle_1.outs(
            attend_outs_kernel, [(inner, deep)] + [(deep, inner)] * 3
        )
        expand_grad, space_grad, time_grad = bundle_2.outs(
            bottleneck_outs_kernel, [(narrow, deep), (9, wide, narrow), (3, deep, narrow)]
        )
    else:

        def columns(share, start, height, width):
            part = share[start : start + height * width // LANE]
            return part.reshape(width // LANE, height, LANE).transpose(1, 0, 2).reshape(height, width)

        def folded(share, start, height, width):
            part = share[start : start + height * width // LANE]
            part = part.reshape(height // LANE, width, LANE // width, width)
            return part.transpose(0, 2, 1, 3).reshape(height, width)

        first, second = bundle_1.shares()
        out_grad = folded(first, 0, inner, deep)
        query_grad = columns(first, half, deep, inner)
        key_grad = columns(second, 0, deep, inner)
        value_grad = columns(second, half, deep, inner)
        both = jnp.concatenate(bundle_2.shares(), axis=0)
        expand_grad = folded(both, 0, narrow, deep)
        space_grad = jnp.stack(
            [columns(both, expand_rows + tap * tap_rows, wide, narrow) for tap in range(9)]
        )
        time_all = columns(both, time_start, deep, 3 * narrow)
        time_grad = jnp.stack([time_all[:, k * narrow : (k + 1) * narrow] for k in range(3)])
    return (
        output, input_grad, time_grad, gain_first_grad[0], shift_first_grad[0], space_grad,
        gain_second_grad[0], shift_second_grad[0], expand_grad, gain_third_grad[0], shift_third_grad[0],
        query_grad, key_grad, value_grad, out_grad, gain_final_grad[0], shift_final_grad[0],
    )


def solution(mesh):
    split = P(("pos", "grp"), None)
    in_specs = (split,) + (P(),) * 17 + (split,)
    out_specs = (
        split, split, P(None, "pos", None), P(), P(), P(None, "pos", None), P(), P(),
        P(None, "pos"), P(), P(), P("pos", None), P("pos", None), P("pos", None),
        P(None, "pos"), P(), P(),
    )
    return jax.shard_map(local, mesh=mesh, in_specs=in_specs, out_specs=out_specs, check_vma=False)
```

```python
import functools

import jax
import jax.numpy as jnp
import numpy as np
from jax import lax
from jax.experimental import pallas as pl
from jax.experimental.pallas import tpu as pltpu
from jax.sharding import PartitionSpec as P

SIDE = 14
HALF = SIDE // 2
AREA = SIDE * SIDE
LANE = 128
EDGE = 16
EPSILON = 1e-05
TEMPER = 0.2
MASKED_SCORE = -1000000000.0
PAD_SCORE = -2000000000.0
F32 = jnp.float32
BF16 = jnp.bfloat16
VMEM_BYTES = 60 * 1024 * 1024


def flip(count, bit):
    return [(i, i ^ bit) for i in range(count)]


def dot(left, right):
    return jnp.dot(left, right, preferred_element_type=F32)


def dot_rows(left, right):
    return lax.dot_general(left, right, (((0,), (0,)), ((), ())), preferred_element_type=F32)


def dot_cols(left, right):
    return lax.dot_general(left, right, (((1,), (1,)), ((), ())), preferred_element_type=F32)


def first_count():
    pos_count, grp_count = lax.axis_size("pos"), lax.axis_size("grp")
    return pos_count * grp_count if pos_count * grp_count <= 64 else pos_count


def trade(copies):
    pos_count, grp_count = lax.axis_size("pos"), lax.axis_size("grp")
    if pos_count * grp_count <= 64:
        return lax.all_to_all(copies, ("pos", "grp"), 0, 0, tiled=True)
    part = lax.all_to_all(copies, "pos", 0, 0, tiled=True).sum(0)
    copies = jnp.broadcast_to(part[None], (grp_count,) + part.shape)
    return lax.all_to_all(copies, "grp", 0, 0, tiled=True)


def tie(wanted, *others):
    return lax.optimization_barrier((wanted,) + others)


def call(kernel, outs, scalars, *arrays, scratch=(), flops=0):
    shapes = [jax.ShapeDtypeStruct(shape, kind) for shape, kind in outs]
    moved = sum(int(np.prod(s.shape)) * s.dtype.itemsize for s in shapes)
    moved += sum(a.size * a.dtype.itemsize for a in arrays)
    near = pl.BlockSpec(memory_space=pltpu.VMEM)
    return pl.pallas_call(
        kernel,
        out_shape=shapes,
        in_specs=[pl.BlockSpec(memory_space=pltpu.SMEM)] * len(scalars) + [near] * len(arrays),
        out_specs=[near] * len(shapes),
        scratch_shapes=list(scratch),
        compiler_params=pltpu.CompilerParams(vmem_limit_bytes=VMEM_BYTES),
        cost_estimate=pl.CostEstimate(flops=flops, bytes_accessed=moved, transcendentals=0),
    )(*scalars, *arrays)


def chunks(width, step=LANE):
    return [slice(start, start + step) for start in range(0, width, step)]


def emit(copies_ref, start, value):
    count, _, width = copies_ref.shape
    for k in range(0, value.shape[1], LANE):
        row, lane = divmod(start + k, width)
        copies_ref[:, row : row + 1, lane : lane + LANE] = jnp.broadcast_to(
            value[None, :, k : k + LANE], (count, 1, LANE)
        )


def collect(copies_ref):
    return jnp.sum(copies_ref[...], axis=0)


def part(sums, start, size):
    width = sums.shape[1]
    pieces, end = [], start + size
    while start < end:
        row, lane = divmod(start, width)
        extent = min(width - lane, end - start)
        pieces.append(sums[row : row + 1, lane : lane + extent])
        start += extent
    return pieces[0] if len(pieces) == 1 else jnp.concatenate(pieces, axis=1)


def column_sum(value):
    return jnp.sum(value, axis=0, keepdims=True)


def project(vector, w):
    high = vector.astype(BF16).astype(F32)
    middle = (vector - high).astype(BF16).astype(F32)
    low = vector - high - middle
    blank = jnp.zeros((13, vector.shape[1]), F32)
    pieces = jnp.concatenate([high, middle, low, blank], axis=0).astype(BF16)
    return column_sum(dot(pieces, w[...]))


def moments_of(values, squares, total):
    mean = values / total
    return mean, lax.rsqrt(squares / total - mean * mean + EPSILON)


def silu_grad(pre_act, gradient):
    sig = jax.nn.sigmoid(pre_act)
    return gradient * sig * (1.0 + pre_act * (1.0 - sig))


def back_terms(gain, mean, inv, gain_grad, shift_grad, total):
    d_spread = -0.5 * gain * gain_grad * inv * inv
    d_mean = -gain * shift_grad * inv - 2.0 * mean * d_spread
    return gain * inv, d_mean / total, 2.0 * d_spread / total


def pack_rows(value, rows, packed):
    for k, c in enumerate(chunks(value.shape[1])):
        packed[k * rows : (k + 1) * rows, :] = value[0:rows, c]


def unpack_rows(packed, rows, size, k):
    return packed[k * rows : k * rows + size, :]


def border_kernel(x, w, tap_0, tap_2, up, down):
    rows = x.shape[0]
    tap_0[...] = dot(x[...], w[0])
    up[...] = tap_0[rows - AREA : rows, :]
    tap_2[...] = dot(x[...], w[2])
    down[...] = tap_2[0:AREA, :]


def first_kernel(frames, sc, tap_0, tap_1, tap_2, place, before, after, pre, copies, last, first):
    for t in range(frames):
        here = slice(t * AREA, (t + 1) * AREA)
        prev = before[...] if t == 0 else tap_0[(t - 1) * AREA : t * AREA, :]
        following = after[...] if t == frames - 1 else tap_2[(t + 1) * AREA : (t + 2) * AREA, :]
        pre[here, :] = tap_1[here, :] + sc[1 + t] * prev + sc[1 + frames + t] * following
    last[...] = pre[(frames - 1) * AREA : frames * AREA, :].astype(BF16)
    first[...] = pre[0:AREA, :].astype(BF16)
    width = pre.shape[1]
    valid = place[:, 0:1]
    for c in chunks(width):
        hidden = pre[:, c]
        masked = hidden * valid
        emit(copies, c.start, column_sum(masked))
        emit(copies, width + c.start, column_sum(masked * hidden))


def inside(place, down, right):
    y = place[:, 2:3] + float(down)
    x = place[:, 1:2] + float(right)
    top = float(SIDE - 1)
    ok = (y >= 0.0) & (y <= top) & (x >= 0.0) & (x <= top)
    return ok.astype(F32)


def fill_padded(padded, value):
    rows, width = value.shape
    padded[0:EDGE, :] = jnp.zeros((EDGE, width), F32)
    padded[EDGE + rows : 2 * EDGE + rows, :] = jnp.zeros((EDGE, width), F32)
    padded[EDGE : EDGE + rows, :] = value


def fill_windows(value, place, padded, windows):
    rows, width = value.shape
    fill_padded(padded, value.astype(F32))
    for tap in range(9):
        down, right = tap // 3 - 1, tap % 3 - 1
        start = EDGE + down * SIDE + right
        window = padded[start : start + rows, :]
        if tap != 4:
            window = window * inside(place, down, right)
        windows[:, tap * width : (tap + 1) * width] = window.astype(BF16)


def windows_kernel(z_1, place, windows, padded):
    fill_windows(z_1[...], place, padded, windows)


def second_kernel(sc, copies_in, pre_1, gain, shift, place, w, pre_2, z_1, copies, stats, padded, windows):
    rows, width = pre_1.shape
    total = sc[0]
    sums = collect(copies_in)
    mean, inv = moments_of(part(sums, 0, width), part(sums, width, width), total)
    stats[0:1, :] = mean
    stats[1:2, :] = inv
    act = (pre_1[...] - mean) * inv * gain[...] + shift[...]
    low = (act * jax.nn.sigmoid(act)).astype(BF16)
    z_1[...] = low
    fill_windows(low, place, padded, windows)
    pre_2[...] = dot(windows[...], w[...])
    valid = place[:, 0:1]
    for c in chunks(width):
        hidden = pre_2[:, c]
        masked = hidden * valid
        emit(copies, c.start, column_sum(masked))
        emit(copies, width + c.start, column_sum(masked * hidden))


def third_kernel(sc, copies_in, pre_2, gain, shift, place, w, z_2, pre_3, copies, stats):
    width = pre_2.shape[1]
    total = sc[0]
    sums = collect(copies_in)
    mean, inv = moments_of(part(sums, 0, width), part(sums, width, width), total)
    stats[0:1, :] = mean
    stats[1:2, :] = inv
    valid = place[:, 0:1]
    act = (pre_2[...] - mean) * inv * gain[...] + shift[...]
    z_2[...] = (act * jax.nn.sigmoid(act)).astype(BF16)
    emit(copies, 0, column_sum(z_2[...].astype(F32) * valid))
    for c in chunks(w.shape[1], 2 * LANE):
        hidden = dot(z_2[...], w[:, c])
        pre_3[:, c] = hidden
        emit(copies, width + c.start, column_sum(hidden * hidden * valid))


def unit_kernel(keys, sc, copies_in, w_expand, gain, shift, pre_3, x, pool, counts, w_key, w_value, unit, pooled, kv, stats, packed):
    total = sc[0]
    narrow, channels = w_expand.shape
    sums = collect(copies_in)
    mean, inv = moments_of(
        project(part(sums, 0, narrow), w_expand), part(sums, narrow, channels), total
    )
    stats[0:1, :] = mean
    stats[1:2, :] = inv
    blocks, inner = pool.shape[0], w_key.shape[1]
    for c in chunks(channels, 2 * LANE):
        scale = inv[:, c] * gain[:, c]
        summed = x[:, c].astype(F32) + (pre_3[:, c] - mean[:, c]) * scale + shift[:, c]
        unit[:, c] = (summed * jax.nn.sigmoid(summed)).astype(BF16)
        sums_here = dot(pool[...], unit[:, c])
        high = sums_here.astype(BF16)
        pooled[0:blocks, c] = high
        pooled[blocks : 2 * blocks, c] = (sums_here - high.astype(F32)).astype(BF16)
    many = jnp.maximum(counts[:, 0:1], 1.0)
    for k, w in enumerate((w_key, w_value)):
        for c in chunks(inner, 2 * LANE):
            both = dot(pooled[...], w[:, c])
            start = (k * inner + c.start) // LANE * keys
            pack_rows((both[:blocks] + both[blocks:]) / many, keys, packed.at[start : start + 2 * keys])
    kv[...] = packed[...].astype(BF16)


def attend_kernel(slots, keys, sc, theta, place, key_row, w, cot, *refs):
    blocks = refs[:slots]
    kv, probs, attended, copies, packed = refs[slots:]
    inner, channels = w.shape
    size, lines = kv.shape[0] // slots, blocks[0].shape[0]
    packed[lines:, :] = jnp.zeros((packed.shape[0] - lines, LANE), F32)
    for k in range(slots):
        packed[0:lines, :] = blocks[k][...].astype(F32)
        for j, c in enumerate(chunks(2 * inner)):
            kv[k * size : (k + 1) * size, c] = unpack_rows(packed, keys, size, j).astype(BF16)
    logits = dot_cols(theta[...], kv[:, 0:inner])
    allowed = place[:, 3:4] == key_row[0:1, :]
    scores = jnp.where(allowed, logits * TEMPER, key_row[1:2, :])
    exponent = jnp.exp(scores - jnp.max(scores, axis=1, keepdims=True))
    weights = exponent / jnp.sum(exponent, axis=1, keepdims=True)
    probs[...] = weights
    attended[...] = dot(weights.astype(BF16), kv[:, inner:]).astype(BF16)
    valid = place[:, 0:1]
    emit(copies, 0, column_sum(attended[...].astype(F32) * valid))
    for c in chunks(channels, 2 * LANE):
        hidden = dot(attended[...], w[:, c])
        emit(copies, inner + c.start, column_sum(hidden * hidden * valid))
        emit(copies, inner + channels + c.start, column_sum(cot[:, c].astype(F32) * hidden))


def attend_back_kernel(slots, keys, sc, copies_in, shift_copies, gain, place, key_row, w, pre_4, cot, kv, probs, theta, d_final, d_logits, mean_out, inv_out, gain_out, shift_out, own, *refs):
    sent, packed = refs[:-1], refs[-1]
    total = sc[0]
    inner, channels = w.shape
    size = own.shape[0]
    sums = collect(copies_in)
    mean, inv = moments_of(
        project(part(sums, 0, inner), w), part(sums, inner, channels), total
    )
    shift_grad = part(collect(shift_copies), 0, channels)
    gain_grad = inv * (part(sums, inner + channels, channels) - mean * shift_grad)
    mean_out[...] = mean
    inv_out[...] = inv
    gain_out[...] = gain_grad
    shift_out[...] = shift_grad
    scale, base, slope = back_terms(gain[...], mean, inv, gain_grad, shift_grad, total)
    valid = place[:, 0:1]
    for c in chunks(channels, 2 * LANE):
        d_final[:, c] = (
            cot[:, c].astype(F32) * scale[:, c]
            + valid * (base[:, c] + pre_4[:, c] * slope[:, c])
        ).astype(BF16)
    d_attended = dot_cols(d_final[...], w[...]).astype(BF16)
    d_probs = dot_cols(d_attended, kv[:, inner:])
    weights = probs[...]
    row_terms = jnp.sum(weights * d_probs, axis=1, keepdims=True)
    allowed = place[:, 3:4] == key_row[0:1, :]
    d_scores = jnp.where(allowed, TEMPER * weights * (d_probs - row_terms), 0.0)
    d_logits[...] = d_scores.astype(BF16)
    d_values = dot_rows(weights.astype(BF16), d_attended)
    d_keys = dot_rows(d_logits[...], theta[...])
    own[:, 0:inner] = d_keys[0:size]
    own[:, inner:] = d_values[0:size]
    for k in range(1, slots):
        here = slice(k * size, (k + 1) * size)
        half = inner // LANE * keys
        pack_rows(d_keys[here], keys, packed.at[0:half])
        pack_rows(d_values[here], keys, packed.at[half : 2 * half])
        sent[k - 1][...] = packed[...].astype(BF16)


def summed_back_kernel(slots, keys, sc, own, counts, w_key, w_value, stats_3, gain, shift, spread, d_unit_part, pre_3, x, *refs):
    received = refs[: slots - 1]
    d_pooled, d_summed, copies, stacked, packed, low = refs[slots - 1 :]
    size, inner = own.shape[0], w_key.shape[1]
    channels = x.shape[1]
    many = jnp.maximum(counts[:, 0:1], 1.0)
    lines = received[0].shape[0]
    others = received[0][...].astype(F32)
    for other in received[1:]:
        others = others + other[...].astype(F32)
    packed[0:lines, :] = others
    packed[lines:, :] = jnp.zeros((packed.shape[0] - lines, LANE), F32)
    for k, c in enumerate(chunks(2 * inner)):
        low[:, c] = ((own[:, c] + unpack_rows(packed, keys, size, k)) / many).astype(BF16)
    d_pooled[0:size, :] = low[...]
    d_pooled[size : 2 * size, :] = low[...]
    mean, inv = stats_3[0:1, :], stats_3[1:2, :]
    for c in chunks(channels, 2 * LANE):
        here = dot_cols(low[:, 0:inner], w_key[c, :]) + dot_cols(low[:, inner:], w_value[c, :])
        high = here.astype(BF16)
        stacked[0:size, c] = high
        stacked[size : 2 * size, c] = (here - high.astype(F32)).astype(BF16)
        d_unit = d_unit_part[:, c] + dot(spread[...], stacked[:, c])
        normed = (pre_3[:, c] - mean[:, c]) * inv[:, c]
        summed = x[:, c].astype(F32) + normed * gain[:, c] + shift[:, c]
        d_here = silu_grad(summed, d_unit)
        d_summed[:, c] = d_here
        emit(copies, c.start, column_sum(d_here * normed))
        emit(copies, channels + c.start, column_sum(d_here))


def third_back_kernel(sc, copies_in, stats_3, gain_3, place, d_summed, pre_3, w, pre_2, stats_2, gain_2, shift_2, d_third, d_act, copies, gain_out, shift_out):
    total = sc[0]
    channels, width = pre_3.shape[1], pre_2.shape[1]
    sums = collect(copies_in)
    gain_grad, shift_grad = part(sums, 0, channels), part(sums, channels, channels)
    gain_out[...] = gain_grad
    shift_out[...] = shift_grad
    scale, base, slope = back_terms(
        gain_3[...], stats_3[0:1, :], stats_3[1:2, :], gain_grad, shift_grad, total
    )
    valid = place[:, 0:1]
    for c in chunks(channels, 2 * LANE):
        d_third[:, c] = (
            d_summed[:, c] * scale[:, c] + valid * (base[:, c] + pre_3[:, c] * slope[:, c])
        ).astype(BF16)
    d_z = dot_cols(d_third[...], w[...])
    normed = (pre_2[...] - stats_2[0:1, :]) * stats_2[1:2, :]
    d_here = silu_grad(normed * gain_2[...] + shift_2[...], d_z)
    d_act[...] = d_here
    emit(copies, 0, column_sum(d_here * normed))
    emit(copies, width, column_sum(d_here))


def second_back_kernel(frames, sc, copies_in, stats_2, gain_2, d_act_2, pre_2, place, w, pre_1, stats_1, gain_1, shift_1, d_second, d_act, copies, gain_out, shift_out, last, first, padded):
    total = sc[0]
    rows, width = pre_1.shape
    sums = collect(copies_in)
    gain_grad, shift_grad = part(sums, 0, width), part(sums, width, width)
    gain_out[...] = gain_grad
    shift_out[...] = shift_grad
    scale, base, slope = back_terms(
        gain_2[...], stats_2[0:1, :], stats_2[1:2, :], gain_grad, shift_grad, total
    )
    low = (d_act_2[...] * scale + place[:, 0:1] * (base + pre_2[...] * slope)).astype(BF16)
    d_second[...] = low
    fill_padded(padded, low.astype(F32))
    d_z = dot_cols(low, w[4])
    for tap in range(9):
        if tap == 4:
            continue
        down, right = 1 - tap // 3, 1 - tap % 3
        start = EDGE + down * SIDE + right
        window = padded[start : start + rows, :] * inside(place, down, right)
        d_z = d_z + dot_cols(window.astype(BF16), w[tap])
    normed = (pre_1[...] - stats_1[0:1, :]) * stats_1[1:2, :]
    d_here = silu_grad(normed * gain_1[...] + shift_1[...], d_z)
    d_act[...] = d_here
    last[...] = d_act[(frames - 1) * AREA : frames * AREA, :].astype(BF16)
    first[...] = d_act[0:AREA, :].astype(BF16)
    emit(copies, 0, column_sum(d_here * normed))
    emit(copies, width, column_sum(d_here))


def input_back_kernel(d_taps, w, d_summed, input_grad):
    width = w.shape[2]
    for c in chunks(d_summed.shape[1], 2 * LANE):
        value = d_summed[:, c]
        for tap in range(3):
            value = value + dot_cols(d_taps[:, tap * width : (tap + 1) * width], w[tap, c, :])
        input_grad[:, c] = value


def put(both, part, start, value):
    rows = value.shape[0]
    for k, c in enumerate(chunks(value.shape[1])):
        both[part & 1, part >> 1, start + k * rows : start + (k + 1) * rows, :] = value[:, c]


def pack(both, part, start, value):
    wide = value.shape[1]
    fold = LANE // wide
    step = LANE // fold
    for k in range(fold):
        both[part & 1, part >> 1, start : start + step, k * wide : (k + 1) * wide] = value[
            k * step : (k + 1) * step, :
        ]


def split_out(mine, start, both, low, send, keep, sems):
    rows = low.shape[2]
    low[0] = both[mine].astype(BF16)
    kept = pltpu.make_async_copy(low.at[0], keep.at[:, start : start + rows], sems.at[0])
    kept.start()
    low[1] = both[1 - mine].astype(BF16)
    sent = pltpu.make_async_copy(low.at[1], send.at[:, start : start + rows], sems.at[1])
    sent.start()
    kept.wait()
    sent.wait()


def attend_grads_kernel(parts, start, bits, d_logits, cot, w, attended, d_final, unit, kv, send, keep, d_unit_part, d_theta, both, low, sems):
    inner, channels = attended.shape[1], unit.shape[1]
    d_theta[...] = dot(d_logits[...], kv[:, 0:inner]).astype(BF16)
    for c in chunks(channels, 2 * LANE):
        d_unit_part[:, c] = cot[:, c].astype(F32) + dot_cols(d_theta[...], w[c, :])
    wide = channels // parts
    for p in range(parts):
        here = slice(p * wide, (p + 1) * wide)
        put(both, p, inner * wide // LANE, dot_rows(unit[:, here], d_theta[...]))
    for c in chunks(inner):
        grad = dot_rows(attended[:, c], d_final[...])
        for p in range(parts):
            pack(both, p, c.start * wide // LANE, grad[:, p * wide : (p + 1) * wide])
    split_out(bits[0], start, both, low, send, keep, sems)


def pooled_grads_kernel(parts, start, bits, send_in, keep_in, pooled, d_pooled, send, keep, both, low, sems):
    wide = pooled.shape[1] // parts
    for p in range(parts):
        put(both, p, 0, dot_rows(pooled[:, p * wide : (p + 1) * wide], d_pooled[...]))
    split_out(bits[0], start, both, low, send, keep, sems)


def expand_grads_kernel(parts, start, bits, z_2, d_third, send, keep, both, low, sems):
    wide = d_third.shape[1] // parts
    for c in chunks(z_2.shape[1]):
        grad = dot_rows(z_2[:, c], d_third[...])
        for p in range(parts):
            pack(both, p, c.start * wide // LANE, grad[:, p * wide : (p + 1) * wide])
    split_out(bits[0], start, both, low, send, keep, sems)


def time_grads_kernel(frames, parts, start, bits, sc, send_in, keep_in, windows, d_second, x, copies_in, stats_1, gain_1, d_act, pre_1, place, near, d_before, d_after, pre_before, pre_after, send, keep, d_taps, gain_out, shift_out, both, low, sems, whole, moved):
    total = sc[0]
    width = pre_1.shape[1]
    sums = collect(copies_in)
    gain_grad, shift_grad = part(sums, 0, width), part(sums, width, width)
    gain_out[...] = gain_grad
    shift_out[...] = shift_grad
    scale, base, slope = back_terms(
        gain_1[...], stats_1[0:1, :], stats_1[1:2, :], gain_grad, shift_grad, total
    )
    whole[...] = d_act[...] * scale + place[:, 0:1] * (base + pre_1[...] * slope)
    d_taps[:, width : 2 * width] = whole[...].astype(BF16)
    d_prev = d_before[...].astype(F32) * scale + near[:, 0:1] * (
        base + pre_before[...].astype(F32) * slope
    )
    d_next = d_after[...].astype(F32) * scale + near[:, 1:2] * (
        base + pre_after[...].astype(F32) * slope
    )
    for t in range(frames):
        here = slice(t * AREA, (t + 1) * AREA)
        ahead = d_next if t == frames - 1 else whole[(t + 1) * AREA : (t + 2) * AREA, :]
        moved[here, :] = ahead * sc[1 + frames + t]
    d_taps[:, 0:width] = moved[...].astype(BF16)
    for t in range(frames):
        here = slice(t * AREA, (t + 1) * AREA)
        behind = d_prev if t == 0 else whole[(t - 1) * AREA : t * AREA, :]
        moved[here, :] = behind * sc[1 + t]
    d_taps[:, 2 * width :] = moved[...].astype(BF16)
    step = width // parts
    for tap in range(9):
        grad = dot_rows(windows[:, tap * width : (tap + 1) * width], d_second[...])
        for p in range(parts):
            put(both, p, tap * step * width // LANE, grad[p * step : (p + 1) * step, :])
    wide = x.shape[1] // parts
    for p in range(parts):
        put(both, p, 9 * step * width // LANE, dot_rows(x[:, p * wide : (p + 1) * wide], d_taps[...]))
    split_out(bits[0], start, both, low, send, keep, sems)


def core_stage_kernel(cut, low_bit, high_bit, bits, keep_in, received, send_1, keep_1, send_2, keep_2):
    count = send_1.shape[0]
    rows = keep_in.shape[1]
    for send, keep, bit, here, low in (
        (send_1, keep_1, low_bit, slice(0, cut), True),
        (send_2, keep_2, high_bit, slice(cut, rows), False),
    ):
        mine = bits[bit]
        for i in range(count):
            at = 2 * i + mine if low else i + count * mine
            off = 2 * i + 1 - mine if low else i + count * (1 - mine)
            keep[i] = (keep_in[at, here, :].astype(F32) + received[at, here, :].astype(F32)).astype(BF16)
            send[i] = (keep_in[off, here, :].astype(F32) + received[off, here, :].astype(F32)).astype(BF16)


def plane_stage_kernel(low_bit, high_bit, bits, in_1, received_1, in_2, received_2, send_1, keep_1, send_2, keep_2):
    count = send_1.shape[0]
    for keep_in, received, send, keep, bit, low in (
        (in_1, received_1, send_1, keep_1, low_bit, True),
        (in_2, received_2, send_2, keep_2, high_bit, False),
    ):
        mine = bits[bit]
        for i in range(count):
            at = 2 * i + mine if low else i + count * mine
            off = 2 * i + 1 - mine if low else i + count * (1 - mine)
            keep[i] = (keep_in[at].astype(F32) + received[at].astype(F32)).astype(BF16)
            send[i] = (keep_in[off].astype(F32) + received[off].astype(F32)).astype(BF16)


def half_stage_kernel(bit, bits, keep_in, received, send, keep):
    mine = bits[bit]
    keep[0] = (keep_in[mine].astype(F32) + received[mine].astype(F32)).astype(BF16)
    send[0] = (keep_in[1 - mine].astype(F32) + received[1 - mine].astype(F32)).astype(BF16)


def unfold(part, start, out):
    rows = out.shape[0]
    for k, c in enumerate(chunks(out.shape[1])):
        out[:, c] = part[start + k * rows : start + (k + 1) * rows, :]


def attend_outs_kernel(bit, bits, mine, other, out_grad, query_grad, key_grad, value_grad, both):
    swap = bits[bit] == 1
    here, there = mine[0].astype(F32), other[0].astype(F32)
    cut = here.shape[0]
    both[0:cut, :] = jnp.where(swap, there, here)
    both[cut : 2 * cut, :] = jnp.where(swap, here, there)
    unfold(both, 0, out_grad)
    unfold(both, cut // 2, query_grad)
    unfold(both, cut, key_grad)
    unfold(both, cut + cut // 2, value_grad)


def bottleneck_outs_kernel(bit, bits, mine, other, expand_grad, space_grad, time_grad, both):
    swap = bits[bit] == 1
    here, there = mine[0].astype(F32), other[0].astype(F32)
    cut = here.shape[0]
    both[0:cut, :] = jnp.where(swap, there, here)
    both[cut : 2 * cut, :] = jnp.where(swap, here, there)
    unfold(both, 0, expand_grad)
    start = expand_grad.shape[0]
    for grad in (space_grad, time_grad):
        taps, deep, width = grad.shape
        for tap in range(taps):
            for c in chunks(width):
                grad[tap, :, c] = both[start : start + deep, :]
                start += deep


class Bundle:
    def __init__(self, bits, cut):
        self.bits, self.cut = bits, cut
        self.pos_count, self.grp_count = lax.axis_size("pos"), lax.axis_size("grp")
        self.pos_bits = self.pos_count.bit_length() - 1
        self.grp_bits = self.grp_count.bit_length() - 1
        self.send = self.keep = None

    def add(self, kernel, start, rows, *arrays, extra=(), scratch=(), scalars=(), flops=0):
        whole = (self.pos_count // 2, 2 * self.cut, LANE)
        half = (self.pos_count // 2, rows, LANE)
        held = () if self.send is None else (self.send, self.keep)
        anywhere = pl.BlockSpec(memory_space=pl.ANY)
        inside_vmem = pl.BlockSpec(memory_space=pltpu.VMEM)
        shapes = [jax.ShapeDtypeStruct(whole, BF16)] * 2
        shapes += [jax.ShapeDtypeStruct(shape, kind) for shape, kind in extra]
        moved = sum(a.size * a.dtype.itemsize for a in arrays) + 6 * int(np.prod(half))
        self.send, self.keep, *rest = pl.pallas_call(
            functools.partial(kernel, self.pos_count, start),
            out_shape=shapes,
            in_specs=[pl.BlockSpec(memory_space=pltpu.SMEM)] * (1 + len(scalars))
            + [anywhere] * len(held)
            + [inside_vmem] * len(arrays),
            out_specs=[anywhere, anywhere] + [inside_vmem] * len(extra),
            scratch_shapes=[
                pltpu.VMEM((2,) + half, F32), pltpu.VMEM((2,) + half, BF16),
                pltpu.SemaphoreType.DMA((2,)),
            ]
            + list(scratch),
            input_output_aliases={1 + len(scalars): 0, 2 + len(scalars): 1} if held else {},
            compiler_params=pltpu.CompilerParams(vmem_limit_bytes=VMEM_BYTES),
            cost_estimate=pl.CostEstimate(flops=flops, bytes_accessed=moved, transcendentals=0),
        )(self.bits, *scalars, *held, *arrays)
        return rest

    def begin(self):
        self.received = lax.ppermute(self.send, "pos", flip(self.pos_count, 1))

    def plane(self):
        count = self.pos_count // 4
        bits = (1, self.pos_bits - 1)
        outs = []
        for rows in (self.cut, self.cut):
            outs += [((count, rows, LANE), BF16)] * 2
        outs = call(
            functools.partial(core_stage_kernel, self.cut, *bits), outs, (self.bits,),
            self.keep, self.received,
        )
        self.parts = [list(outs[:2]), list(outs[2:])]
        self.pair = bits

    def turn(self):
        for k in range(2):
            pairs = flip(self.pos_count, 1 << self.pair[k])
            self.parts[k].append(lax.ppermute(self.parts[k][0], "pos", pairs))

    def hold(self, value):
        value, self.parts[0][0], self.parts[1][0] = tie(
            value, self.parts[0][0], self.parts[1][0]
        )
        return value

    def more(self, last=True):
        while self.parts[0][1].shape[0] > 1:
            count = self.parts[0][1].shape[0] // 2
            self.pair = (self.pair[0] + 1, self.pair[1] - 1)
            outs = [((count, self.cut, LANE), BF16)] * 4
            (_, keep_1, got_1), (_, keep_2, got_2) = self.parts
            outs = call(
                functools.partial(plane_stage_kernel, *self.pair), outs, (self.bits,),
                keep_1, got_1, keep_2, got_2,
            )
            self.parts = [list(outs[:2]), list(outs[2:])]
            if self.parts[0][1].shape[0] > 1 or last:
                self.turn()

    def after(self, others):
        for k, other in enumerate(others):
            self.parts[k][2], _ = tie(self.parts[k][2], other)

    def layer(self):
        (_, keep_1, got_1), (_, keep_2, got_2) = self.parts
        first = keep_1.astype(F32) + got_1.astype(F32)
        second = keep_2.astype(F32) + got_2.astype(F32)
        swap = self.bits[self.pos_bits] == 1
        keep = jnp.where(swap, second, first).astype(BF16)
        send = jnp.where(swap, first, second).astype(BF16)
        self.keep = keep
        self.got = lax.ppermute(send, "grp", flip(self.grp_count, 1))

    def exchange(self):
        keep, got = self.keep, self.got
        for bit in range(1, self.grp_bits - 1):
            shape = (2, keep.shape[1] // 2, LANE)
            half = (1,) + shape[1:]
            send, keep = call(
                functools.partial(half_stage_kernel, self.pos_bits + bit),
                [(half, BF16), (half, BF16)], (self.bits,), keep.reshape(shape), got.reshape(shape),
            )
            got = lax.ppermute(send, "grp", flip(self.grp_count, 1 << bit))
        self.low = (keep.astype(F32) + got.astype(F32)).astype(BF16)
        self.other = lax.ppermute(self.low, "grp", flip(self.grp_count, self.grp_count // 2))

    def finish(self):
        final = (self.low.astype(F32) + self.other.astype(F32)).astype(BF16)
        for bit in reversed(range(1, self.grp_bits - 1)):
            mine = self.bits[self.pos_bits + bit]
            other = lax.ppermute(final, "grp", flip(self.grp_count, 1 << bit))
            lower = jnp.where(mine == 0, final, other)
            upper = jnp.where(mine == 0, other, final)
            final = jnp.concatenate([lower, upper], axis=1)
        self.mine = final
        self.other = lax.ppermute(final, "grp", flip(self.grp_count, 1))

    def outs(self, kernel, shapes):
        return call(
            functools.partial(kernel, self.pos_bits), [(shape, F32) for shape in shapes],
            (self.bits,), self.mine, self.other, scratch=[pltpu.VMEM((2 * self.cut, LANE), F32)],
        )

    def shares(self):
        swap = self.bits[self.pos_bits] == 1
        first = jnp.where(swap, self.other, self.mine)[0].astype(F32)
        second = jnp.where(swap, self.mine, self.other)[0].astype(F32)
        return first, second


def local(
    inputs, segment_ids, pad_mask, time_weight, gain_first, shift_first, space_weight, gain_second,
    shift_second, expand_weight, gain_third, shift_third, query_weight, key_weight, value_weight,
    out_weight, gain_final, shift_final, cotangent,
):
    rows, channels = inputs.shape
    frames = rows // AREA
    narrow = time_weight.shape[2]
    inner = query_weight.shape[1]
    pos_count, grp_count = lax.axis_size("pos"), lax.axis_size("grp")
    group_frames = frames * grp_count
    layer, block = lax.axis_index("grp"), lax.axis_index("pos")
    up = [(i, i + 1) for i in range(grp_count - 1)]
    down = [(i + 1, i) for i in range(grp_count - 1)]
    copies = first_count()
    own_keys = frames * HALF * HALF
    size = -(-own_keys // 16) * 16
    row = lambda v: v.reshape(1, -1)
    deep, wide = channels // pos_count, narrow // pos_count
    bits = jnp.stack(
        [(block >> k) & 1 for k in range(pos_count.bit_length() - 1)]
        + [(layer >> k) & 1 for k in range(grp_count.bit_length() - 1)]
    ).astype(jnp.int32)
    gain_1, shift_1, gain_2, shift_2 = map(row, (gain_first, shift_first, gain_second, shift_second))
    gain_3, shift_3, gain_4 = map(row, (gain_third, shift_third, gain_final))

    seg_group = lax.dynamic_slice_in_dim(segment_ids, block * group_frames, group_frames)
    border = jnp.full((1,), -1, jnp.int32)
    seg_padded = jnp.concatenate([border, seg_group, border])
    seg_own = lax.dynamic_slice_in_dim(seg_padded, layer * frames + 1, frames)
    seg_before = lax.dynamic_slice_in_dim(seg_padded, layer * frames, frames)
    seg_after = lax.dynamic_slice_in_dim(seg_padded, layer * frames + 2, frames)
    total = jnp.sum(pad_mask.astype(F32))
    scalars = jnp.concatenate(
        [total[None], (seg_before == seg_own).astype(F32), (seg_after == seg_own).astype(F32)]
    )
    start = (block * grp_count + layer) * rows
    valid = lax.dynamic_slice_in_dim(pad_mask, start, rows).astype(F32)
    spot = np.arange(rows)
    place = jnp.stack(
        [
            valid,
            jnp.asarray(spot % SIDE, F32),
            jnp.asarray(spot % AREA // SIDE, F32),
            jnp.broadcast_to(seg_own[:, None], (frames, AREA)).reshape(rows).astype(F32),
        ],
        axis=1,
    )
    near_start = jnp.stack([jnp.maximum(start - AREA, 0), start + rows])
    near = jnp.stack(
        [lax.dynamic_slice_in_dim(pad_mask, near_start[k], AREA) for k in range(2)], axis=1
    ).astype(F32)
    owner = (spot // AREA) * HALF * HALF + (spot % AREA // SIDE // 2) * HALF + spot % SIDE // 2
    member = np.zeros((size, rows), np.float32)
    member[owner, spot] = 1.0
    pool = (jnp.asarray(member) * valid[None, :]).astype(BF16)
    half_spread = (jnp.asarray(member.T.copy()) * valid[:, None]).astype(BF16)
    spread = jnp.concatenate([half_spread, half_spread], axis=1)
    mask_group = lax.dynamic_slice_in_dim(
        pad_mask, block * group_frames * AREA, group_frames * AREA
    ).astype(F32)
    key_counts = jnp.sum(
        mask_group.reshape(grp_count, frames, HALF, 2, HALF, 2), axis=(3, 5)
    ).reshape(grp_count, own_keys)
    key_seg = jnp.broadcast_to(
        seg_group.reshape(grp_count, frames, 1), (grp_count, frames, HALF * HALF)
    ).reshape(grp_count, own_keys)
    key_seg = jnp.where(key_counts > 0.5, key_seg.astype(F32), -1.0)
    key_seg = jnp.pad(key_seg, ((0, 0), (0, size - own_keys)), constant_values=-1.0)
    order = layer ^ np.arange(grp_count)
    floor = np.full((grp_count, size), MASKED_SCORE, np.float32)
    floor[:, own_keys:] = PAD_SCORE
    key_row = jnp.stack([key_seg[order].reshape(-1), jnp.asarray(floor.reshape(-1))])
    counts = jnp.pad(
        lax.dynamic_index_in_dim(key_counts, layer, 0, False), (0, size - own_keys)
    )[:, None]

    narrow_f32 = ((rows, narrow), F32)
    wide_f32 = ((rows, channels), F32)
    wide_bf16 = ((rows, channels), BF16)
    frame_f32 = ((AREA, narrow), F32)
    frame_bf16 = ((AREA, narrow), BF16)

    small = (copies, 2, narrow)
    shift_sums = jnp.sum(cotangent.astype(F32), axis=0).reshape(1, 2, channels // 2)
    shift_sums = jnp.broadcast_to(shift_sums, (copies, 2, channels // 2))
    tap_0, tap_2, to_next, to_prev = call(
        border_kernel, [narrow_f32, narrow_f32, frame_f32, frame_f32], (),
        inputs, time_weight,
        flops=4 * rows * channels * narrow,
    )
    before = lax.ppermute(to_next, "grp", up)
    after = lax.ppermute(to_prev, "grp", down)
    tap_1 = dot(inputs, time_weight[1])
    pre_1, sums, last, first = call(
        functools.partial(first_kernel, frames),
        [narrow_f32, (small, F32), frame_bf16, frame_bf16],
        (scalars,), tap_0, tap_1, tap_2, place, before, after,
    )
    sums = trade(sums)
    pre_before = lax.ppermute(last, "grp", up)
    pre_after = lax.ppermute(first, "grp", down)
    pre_2, z_1, sums, stats_1 = call(
        second_kernel,
        [narrow_f32, ((rows, narrow), BF16), (small, F32), ((2, narrow), F32)],
        (scalars,), sums, pre_1, gain_1, shift_1, place,
        space_weight.reshape(9 * narrow, narrow),
        scratch=[
            pltpu.VMEM((rows + 2 * EDGE, narrow), F32), pltpu.VMEM((rows, 9 * narrow), BF16),
        ],
        flops=18 * rows * narrow * narrow,
    )
    sums = trade(sums)
    (windows,) = call(
        windows_kernel, [((rows, 9 * narrow), BF16)], (), z_1, place,
        scratch=[pltpu.VMEM((rows + 2 * EDGE, narrow), F32)],
    )
    sums, windows = tie(sums, windows)
    sums, pre_before, pre_after = tie(sums, pre_before, pre_after)
    z_2, pre_3, sums, stats_2 = call(
        third_kernel,
        [
            ((rows, narrow), BF16), wide_f32, ((copies, 2, (narrow + channels) // 2), F32),
            ((2, narrow), F32),
        ],
        (scalars,), sums, pre_2, gain_2, shift_2, place, expand_weight,
        flops=2 * rows * narrow * channels,
    )
    sums = trade(sums)
    lines = own_keys * 2 * inner // LANE
    packed_bf16 = ((lines, LANE), BF16)
    unit, pooled, kv_own, stats_3 = call(
        functools.partial(unit_kernel, own_keys),
        [wide_bf16, ((2 * size, channels), BF16), packed_bf16, ((2, channels), F32)],
        (scalars,), sums, expand_weight, gain_3, shift_3, pre_3, inputs, pool, counts,
        key_weight, value_weight,
        scratch=[pltpu.VMEM((lines, LANE), F32)],
        flops=2 * size * channels * (rows + 4 * inner),
    )
    shift_sums, _ = tie(shift_sums, kv_own)
    shift_sums = trade(shift_sums)
    kv = [kv_own] + [
        lax.ppermute(kv_own, "grp", flip(grp_count, step)) for step in range(1, grp_count)
    ]
    theta = dot(unit, query_weight).astype(BF16)
    kv_all, probs, attended, sums = call(
        functools.partial(attend_kernel, grp_count, own_keys),
        [
            ((grp_count * size, 2 * inner), BF16), ((rows, grp_count * size), F32), ((rows, inner), BF16),
            ((copies, 4, (inner + 2 * channels) // 4), F32),
        ],
        (scalars,), theta, place, key_row, out_weight, cotangent, *kv,
        scratch=[pltpu.VMEM((lines + 16, LANE), F32)],
        flops=2 * rows * inner * (2 * grp_count * size + channels),
    )
    sums = trade(sums)
    pre_4 = dot(attended, out_weight)

    d_final, d_logits, mean_4, inv_4, gain_final_grad, shift_final_grad, d_kv, *d_sent = call(
        functools.partial(attend_back_kernel, grp_count, own_keys),
        [
            wide_bf16, ((rows, grp_count * size), BF16),
        ]
        + [((1, channels), F32)] * 4
        + [((size, 2 * inner), F32)]
        + [packed_bf16] * (grp_count - 1),
        (scalars,), sums, shift_sums, gain_4, place, key_row, out_weight, pre_4,
        cotangent, kv_all, probs, theta,
        scratch=[pltpu.VMEM((lines, LANE), F32)],
        flops=2 * rows * inner * (3 * grp_count * size + channels),
    )
    d_received = [
        lax.ppermute(d_sent[step - 1], "grp", flip(grp_count, step)) for step in range(1, grp_count)
    ]
    output = (
        unit.astype(F32)
        + (pre_4 - mean_4) * inv_4 * gain_final
        + shift_final
    ).astype(BF16)
    half = deep * inner // LANE
    bundle_1 = Bundle(bits, 2 * half)
    d_unit_part, _ = bundle_1.add(
        attend_grads_kernel, 0, 2 * half,
        d_logits, cotangent, query_weight, attended, d_final, unit, kv_all,
        extra=[wide_f32, ((rows, inner), BF16)],
        flops=2 * rows * inner * (grp_count * size + 3 * channels),
    )
    d_pooled, d_summed, sums = call(
        functools.partial(summed_back_kernel, grp_count, own_keys),
        [((2 * size, 2 * inner), BF16), wide_f32, ((copies, 8, channels // 4), F32)],
        (scalars,), d_kv, counts, key_weight, value_weight, stats_3, gain_3,
        shift_3, spread, d_unit_part, pre_3, inputs, *d_received,
        scratch=[
            pltpu.VMEM((2 * size, channels), BF16), pltpu.VMEM((lines + 16, LANE), F32),
            pltpu.VMEM((size, 2 * inner), BF16),
        ],
        flops=4 * size * channels * (inner + rows),
    )
    sums = trade(sums)
    bundle_1.add(
        pooled_grads_kernel, 2 * half, 2 * half, pooled, d_pooled,
        flops=8 * size * channels * inner,
    )
    sums, bundle_1.send = tie(sums, bundle_1.send)
    bundle_1.begin()
    d_third, d_act_2, sums, gain_third_grad, shift_third_grad = call(
        third_back_kernel,
        [wide_bf16, narrow_f32, (small, F32), ((1, channels), F32), ((1, channels), F32)],
        (scalars,), sums, stats_3, gain_3, place, d_summed, pre_3, expand_weight,
        pre_2, stats_2, gain_2, shift_2,
        flops=2 * rows * narrow * channels,
    )
    sums, bundle_1.received = tie(sums, bundle_1.received)
    sums = trade(sums)
    tap_rows = wide * narrow // LANE
    expand_rows = narrow * deep // LANE
    time_start = expand_rows + 9 * tap_rows
    cut = -(-(time_start + 3 * deep * narrow // LANE) // 32) * 16
    bundle_2 = Bundle(bits, cut)
    bundle_2.add(
        expand_grads_kernel, 0, expand_rows, z_2, d_third,
        flops=2 * rows * narrow * channels,
    )
    bundle_1.plane()
    sums, _ = tie(sums, bundle_2.send)
    sums = bundle_1.hold(sums)
    bundle_1.turn()
    d_second, d_act_1, sums, gain_second_grad, shift_second_grad, last, first = call(
        functools.partial(second_back_kernel, frames),
        [
            ((rows, narrow), BF16), narrow_f32, (small, F32), ((1, narrow), F32), ((1, narrow), F32),
            frame_bf16, frame_bf16,
        ],
        (scalars,), sums, stats_2, gain_2, d_act_2, pre_2, place, space_weight, pre_1, stats_1,
        gain_1, shift_1,
        scratch=[pltpu.VMEM((rows + 2 * EDGE, narrow), F32)],
        flops=18 * rows * narrow * narrow,
    )
    sums = trade(sums)
    d_before = lax.ppermute(last, "grp", up)
    d_after = lax.ppermute(first, "grp", down)
    (_, _, got_1), (_, _, got_2) = bundle_1.parts
    sums, got_1, got_2 = tie(sums, got_1, got_2)
    bundle_1.parts[0][2], bundle_1.parts[1][2] = got_1, got_2
    bundle_1.more(last=False)
    sums = bundle_1.hold(sums)
    d_taps, gain_first_grad, shift_first_grad = bundle_2.add(
        functools.partial(time_grads_kernel, frames), expand_rows,
        9 * tap_rows + 3 * deep * narrow // LANE, windows, d_second, inputs, sums, stats_1, gain_1, d_act_1, pre_1, place, near, d_before, d_after,
        pre_before, pre_after,
        extra=[((rows, 3 * narrow), BF16), ((1, narrow), F32), ((1, narrow), F32)],
        scratch=[pltpu.VMEM((rows, narrow), F32), pltpu.VMEM((rows, narrow), F32)],
        scalars=(scalars,),
        flops=6 * rows * narrow * channels,
    )

    bundle_2.begin()
    bundle_1.turn()
    bundle_2.plane()
    bundle_2.turn()
    d_taps, _ = tie(d_taps, bundle_2.parts[0][1])
    (input_grad,) = call(
        input_back_kernel, [wide_f32], (), d_taps, time_weight, d_summed,
        flops=6 * rows * narrow * channels,
    )
    bundle_1.layer()
    bundle_2.after([input_grad])
    bundle_2.more(last=False)
    bundle_1.got = bundle_2.hold(bundle_1.got)
    bundle_2.turn()
    bundle_1.exchange()
    bundle_2.layer()
    bundle_2.got, bundle_1.other = tie(bundle_2.got, bundle_1.other)
    bundle_2.exchange()
    bundle_1.finish()
    bundle_2.other, bundle_1.other = tie(bundle_2.other, bundle_1.other)
    bundle_2.finish()
    if deep == LANE:
        out_grad, query_grad, key_grad, value_grad = bundle_1.outs(
            attend_outs_kernel, [(inner, deep)] + [(deep, inner)] * 3
        )
        expand_grad, space_grad, time_grad = bundle_2.outs(
            bottleneck_outs_kernel, [(narrow, deep), (9, wide, narrow), (3, deep, narrow)]
        )
    else:

        def columns(share, start, height, width):
            part = share[start : start + height * width // LANE]
            return part.reshape(width // LANE, height, LANE).transpose(1, 0, 2).reshape(height, width)

        def folded(share, start, height, width):
            part = share[start : start + height * width // LANE]
            part = part.reshape(height // LANE, width, LANE // width, width)
            return part.transpose(0, 2, 1, 3).reshape(height, width)

        first, second = bundle_1.shares()
        out_grad = folded(first, 0, inner, deep)
        query_grad = columns(first, half, deep, inner)
        key_grad = columns(second, 0, deep, inner)
        value_grad = columns(second, half, deep, inner)
        both = jnp.concatenate(bundle_2.shares(), axis=0)
        expand_grad = folded(both, 0, narrow, deep)
        space_grad = jnp.stack(
            [columns(both, expand_rows + tap * tap_rows, wide, narrow) for tap in range(9)]
        )
        time_all = columns(both, time_start, deep, 3 * narrow)
        time_grad = jnp.stack([time_all[:, k * narrow : (k + 1) * narrow] for k in range(3)])
    return (
        output, input_grad, time_grad, gain_first_grad[0], shift_first_grad[0], space_grad,
        gain_second_grad[0], shift_second_grad[0], expand_grad, gain_third_grad[0], shift_third_grad[0],
        query_grad, key_grad, value_grad, out_grad, gain_final_grad[0], shift_final_grad[0],
    )


def solution(mesh):
    split = P(("pos", "grp"), None)
    in_specs = (split,) + (P(),) * 17 + (split,)
    out_specs = (
        split, split, P(None, "pos", None), P(), P(), P(None, "pos", None), P(), P(),
        P(None, "pos"), P(), P(), P("pos", None), P("pos", None), P("pos", None),
        P(None, "pos"), P(), P(),
    )
    return jax.shard_map(local, mesh=mesh, in_specs=in_specs, out_specs=out_specs, check_vma=False)
```
